32 devices in a mesh: wide: 8 (over z, core), narrow: 4 (over y, x).
Axes of the slice: x: 2, y: 2, z: 4, core: 2. Of those that a mesh axis runs over, the one named last changes fastest.
Arguments:
- tokens: bfloat16 [2, 9216, 512], P(None, ('wide', 'narrow')), may hold values from -6 to 6
- image_lengths: int32 [2, 64], P(None, ('wide', 'narrow')), may hold values from 49 to 144, as said below
- expert_index: int32 [2, 9216, 2], P(None, ('wide', 'narrow')), may hold values from 0 to 15, all different within a row; in each aligned block of 288 rows (0 to 287, 288 to 575, ..., all dimensions but the last counted through in order) at most 38 rows name the same one
- grad_out: bfloat16 [2, 9216, 512], P(None, ('wide', 'narrow')), may hold values from -6 to 6
- ln1_gain: bfloat16 [512], replicated, may hold values from 0.5 to 1.5
- ln1_bias: bfloat16 [512], replicated, may hold values from -3 to 3
- w_qkv: bfloat16 [512, 1536], replicated, may hold values from -0.25 to 0.25
- bias_query: bfloat16 [512], replicated, may hold values from -3 to 3
- bias_value: bfloat16 [512], replicated, may hold values from -3 to 3
- w_out: bfloat16 [512, 512], replicated, may hold values from -0.75 to 0.75
- bias_out: bfloat16 [512], replicated, may hold values from -3 to 3
- ln2_gain: bfloat16 [512], replicated, may hold values from 0.5 to 1.5
- ln2_bias: bfloat16 [512], replicated, may hold values from -3 to 3
- w_router: bfloat16 [512, 16], replicated, may hold values from -0.1875 to 0.1875
- experts_in: bfloat16 [16, 512, 2048], P('wide', None, 'narrow'), may hold values from -0.25 to 0.25
- experts_in_bias: bfloat16 [16, 2048], P('wide', 'narrow'), may hold values from -3 to 3
- experts_out: bfloat16 [16, 2048, 512], P('wide', 'narrow'), may hold values from -4 to 4
- experts_out_bias: bfloat16 [16, 512], P('wide'), may hold values from -12 to 12
Outputs:
- mixed: bfloat16 [2, 9216, 512], P(None, ('wide', 'narrow'))
- grad_tokens: float32 [2, 9216, 512], P(None, ('wide', 'narrow'))
- grad_ln1_gain: float32 [512], replicated
- grad_ln1_bias: float32 [512], replicated
- grad_w_qkv: float32 [512, 1536], replicated
- grad_bias_query: float32 [512], replicated
- grad_bias_value: float32 [512], replicated
- grad_w_out: float32 [512, 512], replicated
- grad_bias_out: float32 [512], replicated
- grad_ln2_gain: float32 [512], replicated
- grad_ln2_bias: float32 [512], replicated
- grad_w_router: float32 [512, 16], replicated
- grad_experts_in: float32 [16, 512, 2048], P('wide', None, 'narrow')
- grad_experts_in_bias: float32 [16, 2048], P('wide', 'narrow')
- grad_experts_out: float32 [16, 2048, 512], P('wide', 'narrow')
- grad_experts_out_bias: float32 [16, 512], P('wide')
The draws below stay inside these ranges and needn't reach their ends.
Inputs may be any that keep to these rules, and one draw needn't show every extreme that they name: Image i of micro-batch m has its first image_lengths[m, i] patch slots filled; every value is 49 or 144, and both occur. `expert_index`: each patch names two different experts. Among the 288 patches of one device in a micro-batch (aligned blocks of rows), no expert is named more than 38 times, a bound that some block reaches.
All inputs are finite; a program needn't handle non-finite values.
Results may differ from the reference program's by a relative error of at most 0.015.
Values may be sent and summed in bfloat16 or wider, within the bound.
A program may use at most 320 MiB of HBM per device.

```python
import math
import jax
import jax.numpy as jnp
import numpy as np
from jax import lax

HEADS = 8
HEAD_DIM = 64
D = 512
FF = 2048
EXPERTS = 16
SEQ = 144
SHORT_LEN = 49
MICRO = 2
TOK_DEV = 288
IMAGES = 64
TOKENS = 9216
CAP = 38
N_WIDE = 8
N_NARROW = 4


def draw_image_lengths(key, part):
    key = jax.random.fold_in(key, 11)
    choose_full = jax.random.randint(key, (MICRO, IMAGES), 0, 4)
    lengths = jnp.where(choose_full == 0, SHORT_LEN, SEQ).astype(jnp.int32)
    lengths = lengths.at[0, 0].set(SHORT_LEN).at[0, 1].set(SEQ)
    return lengths


def block_levels(key, shape, pieces, smallest, high):
    level = 1.0
    for position, blocks in pieces:
        draws = jax.random.uniform(jax.random.fold_in(jax.random.fold_in(key, 6), position), (blocks,), jnp.float32, smallest / len(pieces), high / len(pieces))
        level = level * jnp.repeat(jnp.exp(draws), shape[position] // blocks).reshape((-1,) + (1,) * (len(shape) - 1 - position))
    return level


def assign_block(own_key, own, number, rows, amount, top, bound, slope):
    order = jax.random.permutation(own_key, amount)
    crowded, usual = load_shares(amount, rows * top, bound, slope, True), load_shares(amount, rows * top, bound, slope, False)
    places = jnp.arange(amount)

    def named(sizes, offset_by):
        used = int((sizes > 0).sum())
        fixed = max(1, used // 4)
        passed = fixed + (places - fixed + offset_by * (used - fixed)) % max(1, amount - fixed)
        return jnp.zeros((amount,), jnp.int32).at[order[jnp.where(places < fixed, places, passed)]].set(jnp.asarray(sizes, jnp.int32))

    sizes = jnp.where(number % 4 == 0, named(crowded, number // 4), named(usual, number - number // 4 - 1))
    mixed = jax.random.permutation(jax.random.fold_in(own, 3), amount)
    giver, taker = mixed[0:amount // 2 * 2:2], mixed[1:amount // 2 * 2:2]
    room = jnp.minimum(sizes[giver] - 1, bound - sizes[taker]) // 2
    room = jnp.where((giver == order[0]) | (taker == order[0]) | (sizes[taker] == 0), 0, jnp.maximum(room, 0))
    passed = jax.random.randint(jax.random.fold_in(own, 4), (amount // 2,), 0, 1 << 20) % (room + 1)
    sizes = sizes.at[giver].add(-passed).at[taker].add(passed)
    labels = jnp.searchsorted(jnp.cumsum(sizes), jnp.arange(rows * top), side="right").astype(jnp.int32)
    table = labels.reshape(top, rows).T
    table = table[jax.random.permutation(jax.random.fold_in(own, 1), rows)]
    offset_by = jax.random.randint(jax.random.fold_in(own, 2), (rows, 1), 0, top)
    return jnp.take_along_axis(table, (jnp.arange(top)[None, :] + offset_by) % top, axis=1)


def load_shares(amount, total, most, slope, full):
    portions = [(1 << 20) // math.isqrt(standing ** slope) + 1 for standing in range(1, amount + 1)]
    largest = most if full else min(most, max(-(-total // amount), total * portions[0] // sum(portions)))
    least = 1 if total - largest >= amount - 1 else 0
    holding, rest = [largest] + [least] * (amount - 1), total - largest - least * (amount - 1)
    while rest > 0:
        candidates = [i for i in range(1, amount) if holding[i] < largest] or [i for i in range(1, amount) if holding[i] < most]
        whole, remaining = sum([portions[i] for i in candidates]), rest
        for i in candidates:
            extra = min(most - holding[i], max(1, remaining * portions[i] // whole), rest)
            holding[i] = holding[i] + extra
            rest = rest - extra
    return np.array(holding)


def scatter_about(stream_key, extent, deviation, limit, cuts=(), kind=jnp.bfloat16):
    values = jax.random.normal(stream_key, extent, jnp.float32) * deviation
    if len(cuts) > 0:
        values = block_levels(stream_key, extent, cuts, -0.22, 0.18) * values
    return jnp.clip(values, min=-limit, max=limit).astype(kind)


def setup_inputs(seed: int = 0) -> dict:
    keys = jax.random.split(jax.random.key(seed), 19)
    tokens = scatter_about(keys[0], (MICRO, TOKENS, D), 1.0, 6.0, ((1, 32),))
    image_lengths = draw_image_lengths(jax.random.fold_in(keys[18], 71), 0)
    expert_index_keys = jax.random.split(jax.random.fold_in(keys[2], 1), MICRO * TOKENS // TOK_DEV)
    expert_index_turns = jax.random.permutation(jax.random.fold_in(keys[2], 3), MICRO * TOKENS // TOK_DEV)
    expert_index = jax.vmap(lambda own, number: assign_block(jax.random.fold_in(keys[2], 2), own, number, TOK_DEV, EXPERTS, 2, CAP, 2))(expert_index_keys, expert_index_turns).reshape((MICRO, TOKENS, 2))
    grad_out = scatter_about(keys[3], (MICRO, TOKENS, D), 1.0, 6.0, ((1, 32),))
    ln1_gain = jnp.clip(1.0 + 0.1 * jax.random.normal(keys[4], (D,), jnp.float32), 0.5, 1.5).astype(jnp.bfloat16)
    ln1_bias = scatter_about(keys[5], (D,), 0.5, 3.0)
    w_qkv = scatter_about(keys[6], (D, 3 * D), D ** -0.5, 0.25)
    bias_query = scatter_about(keys[7], (D,), 0.5, 3.0)
    bias_value = scatter_about(keys[8], (D,), 0.5, 3.0)
    w_out = scatter_about(keys[9], (D, D), (D // 8) ** -0.5, 0.75)
    bias_out = scatter_about(keys[10], (D,), 0.5, 3.0)
    ln2_gain = jnp.clip(1.0 + 0.1 * jax.random.normal(keys[11], (D,), jnp.float32), 0.5, 1.5).astype(jnp.bfloat16)
    ln2_bias = scatter_about(keys[12], (D,), 0.5, 3.0)
    w_router = scatter_about(keys[13], (D, EXPERTS), (2 * D) ** -0.5, 0.1875)
    experts_in = scatter_about(keys[14], (EXPERTS, D, FF), D ** -0.5, 0.25, ((0, 8), (2, 4)))
    experts_in_bias = scatter_about(keys[15], (EXPERTS, FF), 0.5, 3.0, ((0, 8), (1, 4)))
    experts_out = scatter_about(keys[16], (EXPERTS, FF, D), (max(FF // 1024, 1)) ** -0.5, 4.0, ((0, 8), (1, 4)))
    experts_out_bias = scatter_about(keys[17], (EXPERTS, D), 3.0, 12.0, ((0, 8),))
    return {"tokens": tokens, "image_lengths": image_lengths, "expert_index": expert_index, "grad_out": grad_out, "ln1_gain": ln1_gain, "ln1_bias": ln1_bias, "w_qkv": w_qkv, "bias_query": bias_query, "bias_value": bias_value, "w_out": w_out, "bias_out": bias_out, "ln2_gain": ln2_gain, "ln2_bias": ln2_bias, "w_router": w_router, "experts_in": experts_in, "experts_in_bias": experts_in_bias, "experts_out": experts_out, "experts_out_bias": experts_out_bias}


@jax.custom_vjp
def low(v):
    return lax.optimization_barrier(v.astype(jnp.bfloat16)).astype(jnp.float32)

@jax.custom_vjp
def low_back(v):
    return v

def low_keep(v):
    return (low(v), None)

def low_pass(kept, grad):
    return (grad,)

def back_keep(v):
    return (v, None)

def back_low(kept, grad):
    return (low(grad),)
low.defvjp(low_keep, low_pass)
low_back.defvjp(back_keep, back_low)
image_group = 16

def matmul(left, right):
    return jnp.dot(left, right, precision=lax.Precision.HIGHEST, preferred_element_type=jnp.float32)

def layer_norm(values, norm_gain, norm_shift):
    row_mean = lax.optimization_barrier(jnp.mean(values, axis=-1, keepdims=True))
    centred = values - row_mean
    spread = lax.optimization_barrier(jnp.mean(centred * centred, axis=-1, keepdims=True))
    return centred * lax.rsqrt(spread + 1e-06) * norm_gain + norm_shift

def gate_values(route_ids, normed, router_weight):
    router_logits = matmul(normed, router_weight)
    expert_probs = jax.nn.softmax(router_logits, axis=-1)
    chosen = route_ids[:, :, None] == jnp.arange(router_weight.shape[1], dtype=jnp.int32)[None, None, :]
    return lax.optimization_barrier(jnp.sum(jnp.where(chosen, expert_probs[:, None, :], 0.0), axis=-1))

def attend_group(group_args):
    queries, key_rows, value_rows, lengths = group_args
    images, seq_len = (queries.shape[0], queries.shape[1])
    head_shape = (images, seq_len, HEADS, HEAD_DIM)
    scores = jnp.einsum('gqhd,gkhd->ghqk', queries.reshape(head_shape), key_rows.reshape(head_shape), precision=lax.Precision.HIGHEST) * HEAD_DIM ** (-0.5)
    scores = low_back(scores)
    visible = jnp.arange(seq_len, dtype=jnp.int32)[None, None, None, :] < lengths[:, None, None, None]
    scores = jnp.where(visible, scores, -1e+30)
    top_score = lax.optimization_barrier(jnp.max(scores, axis=-1, keepdims=True))
    raised = jnp.exp(scores - top_score)
    probs = low(raised / lax.optimization_barrier(jnp.sum(raised, axis=-1, keepdims=True)))
    attended = jnp.einsum('ghqk,gkhd->gqhd', probs, value_rows.reshape(head_shape), precision=lax.Precision.HIGHEST)
    return attended.reshape(images, seq_len, HEADS * HEAD_DIM)

def expert_apply(expert_args):
    rows_in, weight_in, bias_in, weight_back, bias_back = expert_args
    pre_act = low_back(matmul(rows_in, weight_in) + bias_in)
    hidden = low(jax.nn.gelu(pre_act))
    return matmul(hidden, weight_back) + bias_back

def slot_positions(route_ids):
    devices = N_WIDE * N_NARROW
    paired = route_ids.reshape(devices, -1)
    one_hot = (paired[:, :, None] == jnp.arange(EXPERTS, dtype=jnp.int32)[None, None, :]).astype(jnp.int32)
    before = (jnp.cumsum(one_hot, axis=1) - one_hot).astype(jnp.int32)
    slot = lax.optimization_barrier(jnp.sum(before * one_hot, axis=2)).astype(jnp.int32)
    device_ids = jnp.arange(devices, dtype=jnp.int32)[:, None]
    flat = paired * (devices * CAP) + device_ids * CAP + slot
    return flat.reshape(-1).astype(jnp.int32)

def micro_block(inputs, lengths, route_ids, params):
    ln1_gain, ln1_bias, w_qkv, bias_query, bias_value, w_out, bias_out, ln2_gain, ln2_bias, w_router, experts_in, experts_in_bias, experts_out, experts_out_bias = params
    model_width = inputs.shape[1]
    normed = low(layer_norm(inputs, ln1_gain, ln1_bias))
    projected = matmul(normed, w_qkv)
    queries = low_back(low(projected[:, :model_width] + bias_query))
    key_rows = low_back(low(projected[:, model_width:2 * model_width]))
    value_rows = low_back(low(projected[:, 2 * model_width:] + bias_value))
    group_shape = (IMAGES // image_group, image_group, SEQ, model_width)
    attended = lax.map(jax.checkpoint(attend_group), (queries.reshape(group_shape), key_rows.reshape(group_shape), value_rows.reshape(group_shape), lengths.reshape(IMAGES // image_group, image_group)))
    attended = low_back(low(attended.reshape(-1, model_width)))
    branch = low_back(matmul(attended, w_out) + bias_out)
    residual = inputs + branch
    normed_two = layer_norm(residual, ln2_gain, ln2_bias)
    expert_in = low(normed_two)
    gates = gate_values(route_ids, expert_in, w_router)
    flat = slot_positions(route_ids)
    pair_rows = low_back(jnp.repeat(expert_in, 2, axis=0))
    buffer_rows = jnp.zeros((EXPERTS * N_WIDE * N_NARROW * CAP, model_width), jnp.float32).at[flat].set(pair_rows)
    buffer_rows = buffer_rows.reshape(EXPERTS, -1, model_width)
    expert_rows = lax.map(jax.checkpoint(expert_apply), (buffer_rows, experts_in, experts_in_bias, experts_out, experts_out_bias))
    picked = low_back(low(expert_rows.reshape(-1, model_width)[flat])).reshape(-1, 2, model_width)
    return residual + lax.optimization_barrier(jnp.sum(gates[:, :, None] * picked, axis=1))

def reference(tokens, image_lengths, expert_index, grad_out, ln1_gain, ln1_bias, w_qkv, bias_query, bias_value, w_out, bias_out, ln2_gain, ln2_bias, w_router, experts_in, experts_in_bias, experts_out, experts_out_bias):
    floats = [value.astype(jnp.float32) for value in (tokens, ln1_gain, ln1_bias, w_qkv, bias_query, bias_value, w_out, bias_out, ln2_gain, ln2_bias, w_router, experts_in, experts_in_bias, experts_out, experts_out_bias)]

    def forward(inputs, *params):
        outputs = []
        for micro_step in range(MICRO):
            outputs.append(jax.checkpoint(micro_block)(inputs[micro_step], image_lengths[micro_step], expert_index[micro_step], params))
        return jnp.stack(outputs, axis=0)
    result, pull_back = jax.vjp(forward, *floats)
    grads = pull_back(grad_out.astype(jnp.float32))
    return (result.astype(jnp.bfloat16), grads[0], grads[1], grads[2], grads[3], grads[4], grads[5], grads[6], grads[7], grads[8], grads[9], grads[10], grads[11], grads[12], grads[13], grads[14])
```

```python
import functools

import jax
import jax.numpy as jnp
from jax import lax
from jax.experimental import pallas as pl
from jax.experimental.pallas import tpu as pltpu
from jax.sharding import PartitionSpec as P

HEADS = 8
HEAD_DIM = 64
MESH = pl.DeviceIdType.MESH
BF = jnp.bfloat16
F32 = jnp.float32
VMEM_LIMIT = 60 * 2**20


def dot(a, b):
    return lax.dot_general(a, b, (((1,), (0,)), ((), ())), preferred_element_type=F32)


def dot_nt(a, b):
    return lax.dot_general(a, b, (((1,), (1,)), ((), ())), preferred_element_type=F32)


def dot_tn(a, b):
    return lax.dot_general(a, b, (((0,), (0,)), ((), ())), preferred_element_type=F32)


class Geometry:
    def __init__(self, n_wide, n_narrow, local_experts):
        self.planes = n_wide // 2
        self.places = n_narrow
        self.local_experts = local_experts
        self.plane_experts = 2 * local_experts
        self.group = n_narrow // self.plane_experts
        self.partners = self.planes * self.plane_experts

    def here(self):
        wide, place = lax.axis_index("wide"), lax.axis_index("narrow")
        return wide // 2, wide % 2, place

    def mine(self):
        z, _, n = self.here()
        return z * self.plane_experts + n // self.group

    def partner(self, p):
        _, k, n = self.here()
        place = (p % self.plane_experts) * self.group + n % self.group
        return ((p // self.plane_experts) * 2 + k, place)


def remote(src, dst, send_sem, recv_sem, device):
    return pltpu.make_async_remote_copy(
        src_ref=src,
        dst_ref=dst,
        send_sem=send_sem,
        recv_sem=recv_sem,
        device_id=device,
        device_id_type=MESH,
    )


def greet(devices):
    barrier = pltpu.get_barrier_semaphore()
    for device in devices:
        pl.semaphore_signal(barrier, inc=1, device_id=device, device_id_type=MESH)
    pl.semaphore_wait(barrier, len(devices))


def swap_blocks_start(geo, src, dst, send_sem, recv_sem, local_sem):
    mine = geo.mine()

    def send(i, _):
        p = lax.rem(mine + i, geo.partners)
        remote(src.at[p], dst.at[mine], send_sem.at[p], recv_sem.at[mine], geo.partner(p)).start()
        return 0

    lax.fori_loop(1, geo.partners, send, 0)
    pltpu.make_async_copy(src.at[mine], dst.at[mine], local_sem).start()


def swap_blocks_wait(geo, src, dst, send_sem, recv_sem, local_sem):
    mine = geo.mine()
    pltpu.make_async_copy(src.at[mine], dst.at[mine], local_sem).wait()

    def wait(i, _):
        p = lax.rem(mine + i, geo.partners)
        copy = remote(src.at[p], dst.at[p], send_sem.at[p], recv_sem.at[p], geo.partner(p))
        copy.wait()
        return 0

    lax.fori_loop(1, geo.partners, wait, 0)


def greet_partners(geo):
    mine = geo.mine()
    greet([geo.partner(lax.rem(mine + i, geo.partners)) for i in range(1, geo.partners)])


def swap_kernel(geo, count, *refs):
    srcs, dsts = refs[:count], refs[count : 2 * count]
    send_sem, recv_sem, local_sem = refs[2 * count :]
    greet_partners(geo)
    for i in range(count):
        swap_blocks_start(geo, srcs[i], dsts[i], send_sem.at[i], recv_sem.at[i], local_sem.at[i])
    for i in range(count):
        swap_blocks_wait(geo, srcs[i], dsts[i], send_sem.at[i], recv_sem.at[i], local_sem.at[i])


def swap(geo, collective_id, arrays):
    count = len(arrays)
    return pl.pallas_call(
        functools.partial(swap_kernel, geo, count),
        out_shape=[jax.ShapeDtypeStruct(a.shape, a.dtype) for a in arrays],
        in_specs=[pl.BlockSpec(memory_space=pltpu.VMEM)] * count,
        out_specs=[pl.BlockSpec(memory_space=pltpu.VMEM)] * count,
        scratch_shapes=[
            pltpu.SemaphoreType.DMA((count, geo.partners)),
            pltpu.SemaphoreType.DMA((count, geo.partners)),
            pltpu.SemaphoreType.DMA((count,)),
        ],
        compiler_params=pltpu.CompilerParams(
            collective_id=collective_id, has_side_effects=True, vmem_limit_bytes=VMEM_LIMIT
        ),
    )(*arrays)


def plane_devices(geo):
    z, k, n = geo.here()
    others = [(z * 2 + k, lax.rem(n + i, geo.places)) for i in range(1, geo.places)]
    return others + [(z * 2 + 1 - k, lax.rem(n + i, geo.places)) for i in range(geo.places)]


def weights_start(geo, own, full, tiles, all_tiles, sems):
    z, k, n = geo.here()
    send_sem, recv_sem, tile_send, tile_recv, local_sem, tile_local = sems
    for i in range(geo.local_experts):
        for g in range(geo.group):
            place = (geo.local_experts * k + i) * geo.group + g
            for core in range(2):
                device = (z * 2 + core, place)
                here = jnp.logical_and(k == core, place == n)

                @pl.when(here)
                def _():
                    pltpu.make_async_copy(own[core].at[i], full[core].at[n], local_sem).start()
                    pltpu.make_async_copy(tiles.at[i], all_tiles.at[n], tile_local).start()

                @pl.when(jnp.logical_not(here))
                def _():
                    remote(
                        own[core].at[i],
                        full[core].at[n],
                        send_sem.at[core, i, g],
                        recv_sem.at[n],
                        device,
                    ).start()
                    remote(
                        tiles.at[i],
                        all_tiles.at[n],
                        tile_send.at[core, i, g],
                        tile_recv.at[n],
                        device,
                    ).start()


def weights_relay(geo, own, full, tiles, all_tiles, sems, relay_sems):
    z, k, n = geo.here()
    send_sem, recv_sem, tile_send, tile_recv, local_sem, tile_local = sems
    relay_send, relay_recv = relay_sems
    owner_core = (n // geo.group) // geo.local_experts
    sibling = (z * 2 + 1 - k, n)
    for s in range(geo.places):
        here = jnp.logical_and(k == owner_core, n == s)
        for core in range(2):
            mine = k == core

            @pl.when(jnp.logical_and(mine, here))
            def _():
                pltpu.make_async_copy(own[core].at[0], full[core].at[s], local_sem).wait()
                pltpu.make_async_copy(tiles.at[0], all_tiles.at[s], tile_local).wait()

            @pl.when(jnp.logical_and(mine, jnp.logical_not(here)))
            def _():
                remote(
                    own[core].at[0], full[core].at[s], send_sem.at[core, 0, 0], recv_sem.at[s], sibling
                ).wait_recv()
                remote(
                    tiles.at[0], all_tiles.at[s], tile_send.at[core, 0, 0], tile_recv.at[s], sibling
                ).wait_recv()

            @pl.when(mine)
            def _():
                remote(
                    full[core].at[s], full[core].at[s], relay_send.at[s], relay_recv.at[s], sibling
                ).start()


def weights_finish(geo, own, full, tiles, all_tiles, sems, relay_sems):
    z, k, n = geo.here()
    send_sem, recv_sem, tile_send, tile_recv, local_sem, tile_local = sems
    relay_send, relay_recv = relay_sems
    sibling = (z * 2 + 1 - k, n)
    for s in range(geo.places):
        for core in range(2):

            @pl.when(k == core)
            def _():
                remote(
                    full[core].at[s], full[core].at[s], relay_send.at[s], relay_recv.at[s], sibling
                ).wait_send()
                other = full[1 - core].at[s]
                remote(other, other, relay_send.at[s], relay_recv.at[s], sibling).wait_recv()

    for i in range(geo.local_experts):
        for g in range(geo.group):
            place = (geo.local_experts * k + i) * geo.group + g
            for core in range(2):
                here = jnp.logical_and(k == core, place == n)

                @pl.when(jnp.logical_not(here))
                def _():
                    remote(
                        own[core].at[i],
                        full[core].at[0],
                        send_sem.at[core, i, g],
                        recv_sem.at[0],
                        sibling,
                    ).wait_send()
                    remote(
                        tiles.at[i],
                        all_tiles.at[0],
                        tile_send.at[core, i, g],
                        tile_recv.at[0],
                        sibling,
                    ).wait_send()


def weights_sems(geo):
    dma = pltpu.SemaphoreType.DMA
    sends = (2, geo.local_experts, geo.group)
    return [dma(sends), dma((geo.places,)), dma(sends), dma((geo.places,)), dma, dma]


def weights_kernel(geo, w1, w2, tiles, f1, f2, all_tiles, *sems):
    greet(plane_devices(geo))
    weights_start(geo, (w1, w2), (f1, f2), tiles, all_tiles, sems[:6])
    weights_relay(geo, (w1, w2), (f1, f2), tiles, all_tiles, sems[:6], sems[6:])
    weights_finish(geo, (w1, w2), (f1, f2), tiles, all_tiles, sems[:6], sems[6:])


def gather_weights(geo, collective_id, w1, w2, tiles):
    def whole(a):
        return jax.ShapeDtypeStruct((geo.places,) + a.shape[1:], a.dtype)

    return pl.pallas_call(
        functools.partial(weights_kernel, geo),
        out_shape=[whole(w1), whole(w2), whole(tiles)],
        in_specs=[pl.BlockSpec(memory_space=pltpu.VMEM)] * 3,
        out_specs=[pl.BlockSpec(memory_space=pltpu.VMEM)] * 3,
        scratch_shapes=weights_sems(geo) + [pltpu.SemaphoreType.DMA((geo.places,))] * 2,
        compiler_params=pltpu.CompilerParams(
            collective_id=collective_id, has_side_effects=True, vmem_limit_bytes=VMEM_LIMIT
        ),
    )(w1, w2, tiles)


def expert_grads_kernel(geo, d1, d2, tiles, o1, o2, ot, *scratch):
    half, got1, got2, sum1, sum2, gotb, sumb, in1, in2, inb, *sems = scratch
    (pair_send, pair_recv, own_send, own_recv, tile_send, tile_recv, local_sem, tile_local) = sems
    z, k, n = geo.here()
    sibling = (z * 2 + 1 - k, n)
    greet(plane_devices(geo))
    for core, away, got in ((0, d2, got1), (1, d1, got2)):

        @pl.when(k == core)
        def _(away=away, got=got):
            there = got2 if got is got1 else got1
            remote(away, there, pair_send.at[0], pair_recv.at[0], sibling).start()

    remote(tiles, gotb, pair_send.at[1], pair_recv.at[1], sibling).start()
    expert = n // geo.group
    owner_core = expert // geo.local_experts
    i_there = expert % geo.local_experts
    g_there = n % geo.group
    remote(tiles, gotb, pair_send.at[1], pair_recv.at[1], sibling).wait()
    sumb[...] = tiles[...] + gotb[...]
    for core, keep, away, got, summed, inbox in (
        (0, d1, d2, got1, sum1, in1),
        (1, d2, d1, got2, sum2, in2),
    ):

        @pl.when(k == core)
        def _(core=core, keep=keep, away=away, got=got, summed=summed, inbox=inbox):
            remote(away, away, pair_send.at[0], pair_recv.at[0], sibling).wait_send()
            remote(got, got, pair_send.at[0], pair_recv.at[0], sibling).wait_recv()

            for s in range(geo.places):
                summed[s] = (keep[s].astype(F32) + got[s].astype(F32)).astype(BF)
                here = jnp.logical_and(owner_core == core, n == s)
                owner = (z * 2 + owner_core, s)
                spot = inbox.at[i_there, g_there]

                @pl.when(here)
                def _():
                    pltpu.make_async_copy(summed.at[s], spot, local_sem).start()

                @pl.when(jnp.logical_not(here))
                def _():
                    remote(
                        summed.at[s], spot, own_send.at[s], own_recv.at[core, i_there, g_there], owner
                    ).start()

    for s in range(geo.places):
        here = jnp.logical_and(owner_core == 0, n == s)
        owner = (z * 2 + owner_core, s)
        spot = inb.at[i_there, g_there]

        @pl.when(jnp.logical_and(k == 0, here))
        def _():
            pltpu.make_async_copy(sumb.at[s], spot, tile_local).start()

        @pl.when(jnp.logical_and(k == 0, jnp.logical_not(here)))
        def _():
            remote(
                sumb.at[s], spot, tile_send.at[s], tile_recv.at[i_there, g_there], owner
            ).start()

    for i in range(geo.local_experts):
        for g in range(geo.group):
            source = (k * geo.local_experts + i) * geo.group + g
            for core, inbox in ((0, in1), (1, in2)):
                here = jnp.logical_and(k == core, source == n)
                spot = inbox.at[i, g]

                @pl.when(here)
                def _():
                    pltpu.make_async_copy(spot, spot, local_sem).wait()

                @pl.when(jnp.logical_not(here))
                def _():
                    remote(spot, spot, own_send.at[0], own_recv.at[core, i, g], sibling).wait_recv()

            here = jnp.logical_and(k == 0, source == n)
            spot = inb.at[i, g]

            @pl.when(here)
            def _():
                pltpu.make_async_copy(spot, spot, tile_local).wait()

            @pl.when(jnp.logical_not(here))
            def _():
                remote(spot, spot, tile_send.at[0], tile_recv.at[i, g], sibling).wait_recv()

    for out, inbox in ((o1, in1), (o2, in2), (ot, inb)):
        for i in range(geo.local_experts):
            total = inbox[i, 0].astype(F32)
            for g in range(1, geo.group):
                total = total + inbox[i, g].astype(F32)
            out[i] = total
    for core, summed in ((0, sum1), (1, sum2)):

        @pl.when(k == core)
        def _(core=core, summed=summed):
            for s in range(geo.places):
                here = jnp.logical_and(owner_core == core, n == s)

                @pl.when(jnp.logical_not(here))
                def _():
                    remote(
                        summed.at[s], summed.at[s], own_send.at[s], own_recv.at[0, 0, 0], sibling
                    ).wait_send()

    for s in range(geo.places):
        here = jnp.logical_and(owner_core == 0, n == s)

        @pl.when(jnp.logical_and(k == 0, jnp.logical_not(here)))
        def _():
            remote(sumb.at[s], sumb.at[s], tile_send.at[s], tile_recv.at[0, 0], sibling).wait_send()


def return_expert_grads(geo, collective_id, d1, d2, tiles):
    local, group, places = geo.local_experts, geo.group, geo.places
    dma = pltpu.SemaphoreType.DMA

    def owned(a):
        return jax.ShapeDtypeStruct((local,) + a.shape[1:], F32)

    def inbox(a):
        return pltpu.VMEM((local, group) + a.shape[1:], a.dtype)

    return pl.pallas_call(
        functools.partial(expert_grads_kernel, geo),
        out_shape=[owned(d1), owned(d2), owned(tiles)],
        in_specs=[pl.BlockSpec(memory_space=pltpu.VMEM)] * 3,
        out_specs=[pl.BlockSpec(memory_space=pltpu.VMEM)] * 3,
        scratch_shapes=[
            pltpu.VMEM((8, 128), F32),
            pltpu.VMEM(d1.shape, BF),
            pltpu.VMEM(d2.shape, BF),
            pltpu.VMEM(d1.shape, BF),
            pltpu.VMEM(d2.shape, BF),
            pltpu.VMEM(tiles.shape, F32),
            pltpu.VMEM(tiles.shape, F32),
            inbox(d1),
            inbox(d2),
            inbox(tiles),
            dma((2,)),
            dma((2,)),
            dma((places,)),
            dma((2, local, group)),
            dma((places,)),
            dma((local, group)),
            dma,
            dma,
        ],
        compiler_params=pltpu.CompilerParams(
            collective_id=collective_id, has_side_effects=True, vmem_limit_bytes=VMEM_LIMIT
        ),
    )(d1, d2, tiles)


def sum_kernel(geo, big, small, big_out, small_out, *scratch):
    (mine, got_pair, part, got_plane, piece, got_z, whole, s_mine, s_pair, s_plane, s_z, *sems) = scratch
    (pair_send, pair_recv, plane_send, plane_recv, z_send, z_recv) = sems[:6]
    (zg_send, zg_recv, pg_send, pg_recv, cg_send, cg_recv) = sems[6:12]
    (sp_send, sp_recv, sn_send, sn_recv, sz_send, sz_recv) = sems[12:]
    z, k, n = geo.here()
    places, planes = geo.places, geo.planes
    half = big.shape[0] // 2
    rows = half // places
    columns = big.shape[1] // planes
    sibling = (z * 2 + 1 - k, n)
    row_peers = [(z * 2 + k, lax.rem(n + i, places)) for i in range(1, places)]
    z_peers = [(lax.rem(z + i, planes) * 2 + k, n) for i in range(1, planes)]
    greet([sibling] + row_peers + z_peers)
    mine[...] = big[...].astype(BF)
    s_mine[...] = small[...]
    pair = remote(mine.at[pl.ds((1 - k) * half, half)], got_pair, pair_send, pair_recv, sibling)
    pair.start()
    small_pair = remote(s_mine, s_pair.at[1], sp_send, sp_recv, sibling)
    small_pair.start()
    pair.wait()
    part[...] = (
        mine[pl.ds(k * half, half)].astype(F32) + got_pair[...].astype(F32)
    ).astype(BF)
    copies = []
    for i in range(1, places):
        q = lax.rem(n + i, places)
        copy = remote(
            part.at[pl.ds(q * rows, rows)],
            got_plane.at[n],
            plane_send.at[q],
            plane_recv.at[n],
            (z * 2 + k, q),
        )
        copy.start()
        copies.append((q, copy))
    small_pair.wait()
    s_plane[n] = s_mine[...] + s_pair[1]
    small_copies = []
    for i in range(1, places):
        q = lax.rem(n + i, places)
        copy = remote(s_plane.at[n], s_plane.at[n], sn_send.at[q], sn_recv.at[n], (z * 2 + k, q))
        copy.start()
        small_copies.append((q, copy))
    got_plane[n] = part[pl.ds(n * rows, rows)]
    for q, copy in copies:
        remote(
            got_plane.at[q], got_plane.at[q], plane_send.at[q], plane_recv.at[q], sibling
        ).wait_recv()
    total = got_plane[0].astype(F32)
    for i in range(1, places):
        total = total + got_plane[i].astype(F32)
    for i in range(planes):
        piece[i] = total[:, i * columns : (i + 1) * columns].astype(BF)
    z_copies = []
    for i in range(1, planes):
        q = lax.rem(z + i, planes)
        copy = remote(piece.at[q], got_z.at[z], z_send.at[q], z_recv.at[z], (q * 2 + k, n))
        copy.start()
        z_copies.append((q, copy))
    for q, copy in small_copies:
        copy.wait_send()
        remote(s_plane.at[q], s_plane.at[q], sn_send.at[q], sn_recv.at[q], sibling).wait_recv()
    s_total = s_plane[0]
    for i in range(1, places):
        s_total = s_total + s_plane[i]
    s_z[z] = s_total
    small_z = []
    for i in range(1, planes):
        q = lax.rem(z + i, planes)
        copy = remote(s_z.at[z], s_z.at[z], sz_send.at[q], sz_recv.at[z], (q * 2 + k, n))
        copy.start()
        small_z.append((q, copy))
    got_z[z] = piece[z]
    for q, copy in z_copies:
        remote(got_z.at[q], got_z.at[q], z_send.at[q], z_recv.at[q], sibling).wait_recv()
    total = got_z[0].astype(F32)
    for i in range(1, planes):
        total = total + got_z[i].astype(F32)
    whole[k, n, z] = total.astype(BF)
    gathers = []
    for i in range(1, planes):
        q = lax.rem(z + i, planes)
        copy = remote(
            whole.at[k, n, z], whole.at[k, n, z], zg_send.at[q], zg_recv.at[z], (q * 2 + k, n)
        )
        copy.start()
        gathers.append((q, copy))
    for i in range(planes):
        p = lax.rem(z + i, planes)
        if i > 0:
            spot = whole.at[k, n, p]
            remote(spot, spot, zg_send.at[p], zg_recv.at[p], sibling).wait_recv()
        spot = whole.at[k, n, p]
        for j in range(1, places):
            q = lax.rem(n + j, places)
            remote(spot, spot, pg_send.at[q, p], pg_recv.at[n, p], (z * 2 + k, q)).start()
        remote(spot, spot, cg_send.at[n, p], cg_recv.at[n, p], sibling).start()
    for j in range(1, places):
        q = lax.rem(n + j, places)
        for i in range(planes):
            p = lax.rem(z + i, planes)
            spot = whole.at[k, q, p]
            remote(spot, spot, pg_send.at[q, p], pg_recv.at[q, p], sibling).wait_recv()
            remote(spot, spot, cg_send.at[q, p], cg_recv.at[q, p], sibling).start()
    for q in range(places):
        for p in range(planes):
            spot = whole.at[1 - k, q, p]
            remote(spot, spot, cg_send.at[q, p], cg_recv.at[q, p], sibling).wait_recv()
    for c in range(2):
        for q in range(places):
            for p in range(planes):
                big_out[
                    c * half + q * rows : c * half + (q + 1) * rows, p * columns : (p + 1) * columns
                ] = whole[c, q, p].astype(F32)
    for q, copy in small_z:
        copy.wait_send()
        remote(s_z.at[q], s_z.at[q], sz_send.at[q], sz_recv.at[q], sibling).wait_recv()
    s_total = s_z[0]
    for i in range(1, planes):
        s_total = s_total + s_z[i]
    small_out[...] = s_total
    for q, copy in copies + z_copies + gathers:
        copy.wait_send()
    for j in range(1, places):
        q = lax.rem(n + j, places)
        for i in range(planes):
            spot = whole.at[k, n, i]
            remote(spot, spot, pg_send.at[q, i], pg_recv.at[q, i], sibling).wait_send()
    for q in range(places):
        for p in range(planes):
            spot = whole.at[k, q, p]
            remote(spot, spot, cg_send.at[q, p], cg_recv.at[q, p], sibling).wait_send()


def sum_all(geo, collective_id, big, small):
    places, planes = geo.places, geo.planes
    half = big.shape[0] // 2
    rows, columns = half // places, big.shape[1] // planes
    dma = pltpu.SemaphoreType.DMA
    return pl.pallas_call(
        functools.partial(sum_kernel, geo),
        out_shape=[
            jax.ShapeDtypeStruct(big.shape, F32),
            jax.ShapeDtypeStruct(small.shape, F32),
        ],
        in_specs=[pl.BlockSpec(memory_space=pltpu.VMEM)] * 2,
        out_specs=[pl.BlockSpec(memory_space=pltpu.VMEM)] * 2,
        scratch_shapes=[
            pltpu.VMEM(big.shape, BF),
            pltpu.VMEM((half, big.shape[1]), BF),
            pltpu.VMEM((half, big.shape[1]), BF),
            pltpu.VMEM((places, rows, big.shape[1]), BF),
            pltpu.VMEM((planes, rows, columns), BF),
            pltpu.VMEM((planes, rows, columns), BF),
            pltpu.VMEM((2, places, planes, rows, columns), BF),
            pltpu.VMEM(small.shape, F32),
            pltpu.VMEM((2,) + small.shape, F32),
            pltpu.VMEM((places,) + small.shape, F32),
            pltpu.VMEM((planes,) + small.shape, F32),
            dma,
            dma,
            dma((places,)),
            dma((places,)),
            dma((planes,)),
            dma((planes,)),
            dma((planes,)),
            dma((planes,)),
            dma((places, planes)),
            dma((places, planes)),
            dma((places, planes)),
            dma((places, planes)),
            dma,
            dma,
            dma((places,)),
            dma((places,)),
            dma((planes,)),
            dma((planes,)),
        ],
        compiler_params=pltpu.CompilerParams(
            collective_id=collective_id, has_side_effects=True, vmem_limit_bytes=VMEM_LIMIT
        ),
    )(big, small)


def norm_parts(values):
    centred = values - jnp.mean(values, axis=-1, keepdims=True)
    scale = lax.rsqrt(jnp.mean(centred * centred, axis=-1, keepdims=True) + 1e-06)
    return centred * scale, scale


def norm_back(grad, unit, scale, gain):
    pulled = grad * gain
    inner = jnp.mean(pulled, axis=-1, keepdims=True)
    along = jnp.mean(pulled * unit, axis=-1, keepdims=True)
    return scale * (pulled - inner - unit * along)


def head_pair(rows, low):
    zero = jnp.zeros_like(rows)
    return jnp.concatenate([jnp.where(low, rows, zero), jnp.where(low, zero, rows)], axis=0)


def pair_probs(stacked, keys, length):
    scores = dot_nt(stacked, keys) * HEAD_DIM ** (-0.5)
    visible = lax.broadcasted_iota(jnp.int32, scores.shape, 1) < length
    scores = jnp.where(visible, scores, -1e30)
    raised = jnp.exp(scores - jnp.max(scores, axis=-1, keepdims=True))
    return raised / jnp.sum(raised, axis=-1, keepdims=True)


def attend_image(queries, keys, values, length):
    seq = queries.shape[0]
    low = lax.broadcasted_iota(jnp.int32, (seq, 128), 1) < HEAD_DIM
    parts = []
    for g in range(queries.shape[1] // 128):
        cols = slice(g * 128, (g + 1) * 128)
        probs = pair_probs(head_pair(queries[:, cols], low), keys[:, cols], length).astype(BF)
        out = dot(probs, values[:, cols])
        parts.append(jnp.where(low, out[:seq], out[seq:]).astype(BF))
    return jnp.concatenate(parts, axis=1)


def attend_image_back(queries, keys, values, length, grad):
    seq = queries.shape[0]
    low = lax.broadcasted_iota(jnp.int32, (seq, 128), 1) < HEAD_DIM
    scale = HEAD_DIM ** (-0.5)
    parts = ([], [], [])
    for g in range(queries.shape[1] // 128):
        cols = slice(g * 128, (g + 1) * 128)
        stacked = head_pair(queries[:, cols], low)
        stacked_grad = head_pair(grad[:, cols], low)
        probs = pair_probs(stacked, keys[:, cols], length)
        grad_probs = dot_nt(stacked_grad, values[:, cols])
        parts[2].append(dot_tn(probs.astype(BF), stacked_grad).astype(BF))
        centre = jnp.sum(probs * grad_probs, axis=-1, keepdims=True)
        grad_scores = (probs * (grad_probs - centre)).astype(BF)
        grad_q = dot(grad_scores, keys[:, cols])
        parts[0].append((jnp.where(low, grad_q[:seq], grad_q[seq:]) * scale).astype(BF))
        parts[1].append((dot_tn(grad_scores, stacked) * scale).astype(BF))
    return [jnp.concatenate(part, axis=1) for part in parts]


def slot_tables(choices, experts, capacity, block_rows, per_micro):
    rows = choices.shape[1]
    ids = lax.broadcasted_iota(jnp.int32, (experts, rows), 0)
    named = [ids == choices[k : k + 1, :] for k in range(2)]
    either = jnp.logical_or(named[0], named[1])
    first = lax.broadcasted_iota(jnp.int32, (rows, rows), 0)
    second = lax.broadcasted_iota(jnp.int32, (rows, rows), 1)
    earlier = jnp.logical_and(first < second, first // per_micro == second // per_micro)
    before = dot(either.astype(BF), earlier.astype(BF))
    micro = lax.broadcasted_iota(jnp.int32, (experts, rows), 1) // per_micro
    slot = before + (micro * capacity).astype(F32)
    spots = lax.broadcasted_iota(jnp.int32, (block_rows, rows), 0).astype(F32)
    tables = []
    for k in range(2):
        held = jnp.where(named[k], slot, -1.0)
        blocks = [(spots == held[e : e + 1, :]).astype(BF) for e in range(experts)]
        tables.append(jnp.concatenate(blocks, axis=0))
    return tables, [n.astype(F32) for n in named]


def split_two(values):
    high = values.astype(BF)
    return high, (values - high.astype(F32)).astype(BF)


def expert_rows(x, cot, gate, slices, bias_back):
    grad_out = (gate * cot.astype(F32)).astype(BF)
    root = 0.7978845608028654
    returned = grad_in = None
    hidden_parts, grad_parts = [], []
    for first, bias, second in slices:
        pre = dot(x, first) + bias
        square = pre * pre
        bend = jnp.tanh(root * pre * (1.0 + 0.044715 * square))
        hidden = (0.5 * pre * (1.0 + bend)).astype(BF)
        slope = 0.5 * (1.0 + bend) + 0.5 * pre * (1.0 - bend * bend) * root * (
            1.0 + 3 * 0.044715 * square
        )
        out = dot(hidden, second)
        returned = out if returned is None else returned + out
        grad_pre = (dot_nt(grad_out, second) * slope).astype(BF)
        back = dot_nt(grad_pre, first)
        grad_in = back if grad_in is None else grad_in + back
        hidden_parts.append(hidden)
        grad_parts.append(grad_pre)
    returned = (returned + bias_back).astype(BF)
    grad_gate = jnp.sum(cot.astype(F32) * returned.astype(F32), axis=-1, keepdims=True)
    return returned, grad_in.astype(BF), grad_gate, grad_out, hidden_parts, grad_parts


def on_device(
    geo,
    tokens,
    image_lengths,
    expert_index,
    grad_out,
    ln1_gain,
    ln1_bias,
    w_qkv,
    bias_query,
    bias_value,
    w_out,
    bias_out,
    ln2_gain,
    ln2_bias,
    w_router,
    experts_in,
    experts_in_bias,
    experts_out,
    experts_out_bias,
):
    micros, per_micro, width = tokens.shape
    rows = micros * per_micro
    images = image_lengths.shape[1]
    seq = per_micro // images
    experts = geo.partners
    capacity = (per_micro * 42 + 20 * experts - 1) // (20 * experts)
    block = -(-(micros * capacity + 2) // 16) * 16
    hidden = experts_in.shape[2]
    wide_row = lambda v: v.astype(F32)[None, :]
    gain1, shift1, gain2, shift2 = map(wide_row, (ln1_gain, ln1_bias, ln2_gain, ln2_bias))
    qkv_bias = jnp.concatenate(
        [bias_query.astype(F32), jnp.zeros((width,), F32), bias_value.astype(F32)]
    )[None, :]
    out_bias = wide_row(bias_out)

    tile = jnp.zeros((geo.local_experts, 8, width), F32)
    tile = tile.at[:, 0, :hidden].set(experts_in_bias.astype(F32))
    tile = tile.at[:, 1, :].set(experts_out_bias.astype(F32))
    first, second, tiles = gather_weights(geo, 0, experts_in, experts_out, tile)

    inputs = tokens.reshape(rows, width).astype(F32)
    cot = grad_out.reshape(rows, width)
    choices = expert_index.reshape(rows, 2).T
    (table0, table1), named = slot_tables(choices, experts, capacity, block, per_micro)
    table = table0 + table1
    unit1, scale1 = norm_parts(inputs)
    normed = (unit1 * gain1 + shift1).astype(BF)
    qkv = (dot(normed, w_qkv) + qkv_bias).astype(BF)
    queries, keys, values = (qkv[:, i * width : (i + 1) * width] for i in range(3))
    lengths = image_lengths.reshape(-1)
    attended = jnp.concatenate(
        [
            attend_image(
                queries[i * seq : (i + 1) * seq],
                keys[i * seq : (i + 1) * seq],
                values[i * seq : (i + 1) * seq],
                lengths[i],
            )
            for i in range(micros * images)
        ],
        axis=0,
    )
    residual = inputs + dot(attended, w_out) + out_bias
    unit2, scale2 = norm_parts(residual)
    expert_in = (unit2 * gain2 + shift2).astype(BF)
    probs = jax.nn.softmax(dot(expert_in, w_router), axis=-1)
    gates = [jnp.sum(probs * named[k].T, axis=-1, keepdims=True) for k in range(2)]

    x_blocks = dot(table, expert_in)
    cot_blocks = dot(table, cot).astype(BF).reshape(experts, block, width)
    slot_gate = jnp.sum(
        table.reshape(experts, block, rows).astype(F32) * probs.T[:, None, :], axis=-1
    )
    gate_high, gate_low = split_two(slot_gate)
    lanes = ((0, 0), (0, width - block))
    x_blocks = x_blocks.astype(BF).reshape(experts, block, width)
    x_blocks = x_blocks.at[:, micros * capacity].set(jnp.pad(gate_high, lanes))
    x_blocks = x_blocks.at[:, micros * capacity + 1].set(jnp.pad(gate_low, lanes))
    x_got, cot_got = swap(geo, 1, [x_blocks, cot_blocks])

    spot = micros * capacity
    gate = (x_got[:, spot, :block].astype(F32) + x_got[:, spot + 1, :block].astype(F32)).reshape(-1, 1)
    x_rows, cot_rows = x_got.reshape(-1, width), cot_got.reshape(-1, width)
    parts = [(first[s], tiles[s, 0:1, :hidden], second[s]) for s in range(geo.places)]
    returned, grad_in, grad_gate, grad_ret, hiddens, grad_pres = expert_rows(
        x_rows, cot_rows, gate, parts, tiles[0, 1:2, :]
    )
    d_first = jnp.stack([dot_tn(x_rows, g) for g in grad_pres])
    d_second = jnp.stack([dot_tn(h, grad_ret) for h in hiddens])
    d_tiles = jnp.zeros((geo.places, 8, width), F32)
    for s, g in enumerate(grad_pres):
        d_tiles = d_tiles.at[s, 0, :hidden].set(jnp.sum(g.astype(F32), axis=0))
    d_tiles = d_tiles.at[:, 1, :].set(jnp.sum(grad_ret.astype(F32), axis=0)[None, :])
    grad_gate = grad_gate.reshape(experts, block)
    gg_high, gg_low = split_two(grad_gate)
    grad_in = grad_in.reshape(experts, block, width)
    grad_in = grad_in.at[:, spot].set(jnp.pad(gg_high, lanes))
    grad_in = grad_in.at[:, spot + 1].set(jnp.pad(gg_low, lanes))
    grad_got, returned_got = swap(geo, 2, [grad_in, returned.reshape(experts, block, width)])
    d_in, d_out, d_bias = return_expert_grads(geo, 3, d_first.astype(BF), d_second.astype(BF), d_tiles)

    returned_rows = returned_got.reshape(-1, width)
    picked = [dot_tn(t, returned_rows) for t in (table0, table1)]
    mixed = (residual + gates[0] * picked[0] + gates[1] * picked[1]).astype(BF)
    grad_pairs = dot_tn(table, grad_got.reshape(-1, width))
    slot_grad = grad_got[:, spot, :block].astype(F32) + grad_got[:, spot + 1, :block].astype(F32)
    grad_choice = jnp.sum(
        table.reshape(experts, block, rows).astype(F32) * slot_grad[:, :, None], axis=1
    ).T
    grad_logits = probs * (grad_choice - jnp.sum(probs * grad_choice, axis=-1, keepdims=True))
    gl_high, gl_low = split_two(grad_logits)
    d_router = dot_tn(gl_high, expert_in) + dot_tn(gl_low, expert_in)
    grad_two = dot_nt(gl_high, w_router) + dot_nt(gl_low, w_router) + grad_pairs
    d_gain2 = jnp.sum(grad_two * unit2, axis=0, keepdims=True)
    d_shift2 = jnp.sum(grad_two, axis=0, keepdims=True)
    grad_residual = cot.astype(F32) + norm_back(grad_two, unit2, scale2, gain2)
    grad_branch = grad_residual.astype(BF)
    d_out_bias = jnp.sum(grad_branch.astype(F32), axis=0, keepdims=True)
    d_w_out = dot_tn(attended, grad_branch)
    grad_attended = dot_nt(grad_branch, w_out).astype(BF)
    grads = [
        jnp.concatenate(
            attend_image_back(
                queries[i * seq : (i + 1) * seq],
                keys[i * seq : (i + 1) * seq],
                values[i * seq : (i + 1) * seq],
                lengths[i],
                grad_attended[i * seq : (i + 1) * seq],
            ),
            axis=1,
        )
        for i in range(micros * images)
    ]
    grad_qkv = jnp.concatenate(grads, axis=0)
    d_qkv_bias = jnp.sum(grad_qkv.astype(F32), axis=0, keepdims=True)
    d_qkv = dot_tn(normed, grad_qkv)
    grad_normed = dot_nt(grad_qkv, w_qkv)
    d_gain1 = jnp.sum(grad_normed * unit1, axis=0, keepdims=True)
    d_shift1 = jnp.sum(grad_normed, axis=0, keepdims=True)
    grad_tokens = grad_residual + norm_back(grad_normed, unit1, scale1, gain1)
    small = jnp.concatenate(
        [
            d_gain1,
            d_shift1,
            d_qkv_bias[:, :width],
            d_qkv_bias[:, 2 * width :],
            d_out_bias,
            d_gain2,
            d_shift2,
            jnp.zeros_like(d_shift2),
            d_router,
        ],
        axis=0,
    )
    big, small = sum_all(geo, 4, jnp.concatenate([d_qkv, d_w_out], axis=1), small)
    return (
        mixed.reshape(tokens.shape),
        grad_tokens.reshape(tokens.shape),
        small[0],
        small[1],
        big[:, : 3 * width],
        small[2],
        small[3],
        big[:, 3 * width :],
        small[4],
        small[5],
        small[6],
        small[8:].T,
        d_in,
        d_bias[:, 0, :hidden],
        d_out,
        d_bias[:, 1, :],
    )


def solution(mesh):
    split = ("wide", "narrow")
    in_specs = (
        P(None, split, None),
        P(None, split),
        P(None, split, None),
        P(None, split, None),
        *([P()] * 10),
        P("wide", None, "narrow"),
        P("wide", "narrow"),
        P("wide", "narrow", None),
        P("wide", None),
    )
    out_specs = (
        P(None, split, None),
        P(None, split, None),
        *([P()] * 10),
        P("wide", None, "narrow"),
        P("wide", "narrow"),
        P("wide", "narrow", None),
        P("wide", None),
    )

    def step(*args):
        geo = Geometry(mesh.shape["wide"], mesh.shape["narrow"], args[14].shape[0])
        return on_device(geo, *args)

    return jax.shard_map(step, mesh=mesh, in_specs=in_specs, out_specs=out_specs, check_vma=False)
```

```python
import functools
from types import SimpleNamespace

import jax
import jax.numpy as jnp
from jax import lax
from jax.experimental import pallas as pl
from jax.experimental.pallas import tpu as pltpu
from jax.sharding import PartitionSpec as P

HEADS = 8
HEAD_DIM = 64
MESH = pl.DeviceIdType.MESH
BF = jnp.bfloat16
F32 = jnp.float32
VMEM_LIMIT = 60 * 2**20


def dot(a, b):
    return lax.dot_general(a, b, (((1,), (0,)), ((), ())), preferred_element_type=F32)


def dot_nt(a, b):
    return lax.dot_general(a, b, (((1,), (1,)), ((), ())), preferred_element_type=F32)


def dot_tn(a, b):
    return lax.dot_general(a, b, (((0,), (0,)), ((), ())), preferred_element_type=F32)


class Geometry:
    def __init__(self, n_wide, n_narrow, local_experts):
        self.planes = n_wide // 2
        self.places = n_narrow
        self.local_experts = local_experts
        self.plane_experts = 2 * local_experts
        self.group = n_narrow // self.plane_experts
        self.partners = self.planes * self.plane_experts

    def here(self):
        wide, place = lax.axis_index("wide"), lax.axis_index("narrow")
        return wide // 2, wide % 2, place

    def mine(self):
        z, _, n = self.here()
        return z * self.plane_experts + n // self.group

    def partner(self, p):
        _, k, n = self.here()
        place = (p % self.plane_experts) * self.group + n % self.group
        return ((p // self.plane_experts) * 2 + k, place)


def remote(src, dst, send_sem, recv_sem, device):
    return pltpu.make_async_remote_copy(
        src_ref=src,
        dst_ref=dst,
        send_sem=send_sem,
        recv_sem=recv_sem,
        device_id=device,
        device_id_type=MESH,
    )


def norm_parts(values):
    centred = values - jnp.mean(values, axis=-1, keepdims=True)
    scale = lax.rsqrt(jnp.mean(centred * centred, axis=-1, keepdims=True) + 1e-06)
    return centred * scale, scale


def norm_back(grad, unit, scale, gain):
    pulled = grad * gain
    inner = jnp.mean(pulled, axis=-1, keepdims=True)
    along = jnp.mean(pulled * unit, axis=-1, keepdims=True)
    return scale * (pulled - inner - unit * along)


def head_pair(rows, low):
    zero = jnp.zeros_like(rows)
    return jnp.concatenate([jnp.where(low, rows, zero), jnp.where(low, zero, rows)], axis=0)


def pair_probs(stacked, keys, length):
    scores = dot_nt(stacked, keys) * HEAD_DIM ** (-0.5)
    visible = lax.broadcasted_iota(jnp.int32, scores.shape, 1) < length
    scores = jnp.where(visible, scores, -1e30)
    raised = jnp.exp(scores - jnp.max(scores, axis=-1, keepdims=True))
    return raised / jnp.sum(raised, axis=-1, keepdims=True)


def attend_image(queries, keys, values, length):
    seq = queries.shape[0]
    low = lax.broadcasted_iota(jnp.int32, (seq, 128), 1) < HEAD_DIM
    parts = []
    for g in range(queries.shape[1] // 128):
        cols = slice(g * 128, (g + 1) * 128)
        probs = pair_probs(head_pair(queries[:, cols], low), keys[:, cols], length).astype(BF)
        out = dot(probs, values[:, cols])
        parts.append(jnp.where(low, out[:seq], out[seq:]).astype(BF))
    return jnp.concatenate(parts, axis=1)


def attend_image_back(queries, keys, values, length, grad):
    seq = queries.shape[0]
    low = lax.broadcasted_iota(jnp.int32, (seq, 128), 1) < HEAD_DIM
    scale = HEAD_DIM ** (-0.5)
    parts = ([], [], [])
    for g in range(queries.shape[1] // 128):
        cols = slice(g * 128, (g + 1) * 128)
        stacked = head_pair(queries[:, cols], low)
        stacked_grad = head_pair(grad[:, cols], low)
        probs = pair_probs(stacked, keys[:, cols], length)
        grad_probs = dot_nt(stacked_grad, values[:, cols])
        parts[2].append(dot_tn(probs.astype(BF), stacked_grad).astype(BF))
        centre = jnp.sum(probs * grad_probs, axis=-1, keepdims=True)
        grad_scores = (probs * (grad_probs - centre)).astype(BF)
        grad_q = dot(grad_scores, keys[:, cols])
        parts[0].append((jnp.where(low, grad_q[:seq], grad_q[seq:]) * scale).astype(BF))
        parts[1].append((dot_tn(grad_scores, stacked) * scale).astype(BF))
    return [jnp.concatenate(part, axis=1) for part in parts]


def split_two(values):
    high = values.astype(BF)
    return high, (values - high.astype(F32)).astype(BF)


def each(count, step, unroll=False):
    if unroll:
        for i in range(count):
            step(i)
    else:

        def body(i, _):
            step(i)
            return 0

        lax.fori_loop(0, count, body, 0)


class Swap:
    def __init__(self, geo, block, src, dst, sems):
        self.geo, self.block, self.src, self.dst = geo, block, src, dst
        self.send_sem, self.recv_sem, self.local_sem = sems

    def rows(self, ref, p):
        return ref.at[pl.ds(pl.multiple_of(p * self.block, 16), self.block)]

    def local(self):
        mine = self.geo.mine()
        return pltpu.make_async_copy(self.rows(self.src, mine), self.rows(self.dst, mine), self.local_sem)

    def send(self, p):
        mine = self.geo.mine()

        @pl.when(p == mine)
        def _():
            self.local().start()

        @pl.when(p != mine)
        def _():
            remote(
                self.rows(self.src, p),
                self.rows(self.dst, mine),
                self.send_sem.at[p],
                self.recv_sem.at[mine],
                self.geo.partner(p),
            ).start()

    def copy(self, p):
        return remote(
            self.rows(self.src, p),
            self.rows(self.dst, p),
            self.send_sem.at[p],
            self.recv_sem.at[p],
            self.geo.partner(p),
        )

    def wait_got(self, p):
        mine = self.geo.mine()

        @pl.when(p == mine)
        def _():
            self.local().wait()

        @pl.when(p != mine)
        def _():
            self.copy(p).wait_recv()

    def wait_sent(self):
        mine = self.geo.mine()
        each(self.geo.partners - 1, lambda i: self.copy(lax.rem(mine + 1 + i, self.geo.partners)).wait_send())


def swap_sems(geo):
    dma = pltpu.SemaphoreType.DMA
    return [dma((geo.partners,)), dma((geo.partners,)), dma]


class Weights:
    def __init__(self, geo, own, full, tiles, all_tiles, sems):
        self.geo, self.own, self.full, self.tiles, self.all_tiles = geo, own, full, tiles, all_tiles
        (
            self.send_sem,
            self.recv_sem,
            self.tile_send,
            self.tile_recv,
            self.relay_send,
            self.relay_recv,
            self.local_sem,
            self.tile_local,
        ) = sems

    @staticmethod
    def sems(geo):
        dma = pltpu.SemaphoreType.DMA
        sends, places = (2, geo.local_experts, geo.group), (geo.places,)
        return [dma(sends), dma(places), dma(sends), dma(places), dma(places), dma(places), dma, dma]

    def slot(self, core, s):
        part = self.own[core].shape[2 - core]
        spot = pl.ds(pl.multiple_of(s * part, 128), part)
        return self.full[0].at[:, spot] if core == 0 else self.full[1].at[spot]

    def targets(self):
        geo = self.geo
        z, k, n = geo.here()
        for i in range(geo.local_experts):
            for g in range(geo.group):
                place = (geo.local_experts * k + i) * geo.group + g
                for core in range(2):
                    yield i, g, core, jnp.logical_and(k == core, place == n), (z * 2 + core, place)

    def start(self):
        n = self.geo.here()[2]
        for i, g, core, here, device in self.targets():

            @pl.when(here)
            def _():
                pltpu.make_async_copy(self.own[core].at[i], self.slot(core, n), self.local_sem).start()
                pltpu.make_async_copy(self.tiles.at[i], self.all_tiles.at[n], self.tile_local).start()

            @pl.when(jnp.logical_not(here))
            def _():
                remote(
                    self.own[core].at[i],
                    self.slot(core, n),
                    self.send_sem.at[core, i, g],
                    self.recv_sem.at[n],
                    device,
                ).start()
                remote(
                    self.tiles.at[i],
                    self.all_tiles.at[n],
                    self.tile_send.at[core, i, g],
                    self.tile_recv.at[n],
                    device,
                ).start()

    def relay_copy(self, core, s):
        z, k, n = self.geo.here()
        spot = self.slot(core, s)
        return remote(spot, spot, self.relay_send.at[s], self.relay_recv.at[s], (z * 2 + 1 - k, n))

    def relay(self):
        geo = self.geo
        z, k, n = geo.here()
        owner_core = (n // geo.group) // geo.local_experts
        sibling = (z * 2 + 1 - k, n)
        for s in range(geo.places):
            here = jnp.logical_and(k == owner_core, n == s)

            @pl.when(here)
            def _():
                pltpu.make_async_copy(self.tiles.at[0], self.all_tiles.at[s], self.tile_local).wait()

            @pl.when(jnp.logical_not(here))
            def _():
                spot = self.all_tiles.at[s]
                remote(spot, spot, self.tile_send.at[0, 0, 0], self.tile_recv.at[s], sibling).wait_recv()

            for core in range(2):
                spot = self.slot(core, s)

                @pl.when(jnp.logical_and(k == core, here))
                def _():
                    pltpu.make_async_copy(self.own[core].at[0], spot, self.local_sem).wait()

                @pl.when(jnp.logical_and(k == core, jnp.logical_not(here)))
                def _():
                    remote(spot, spot, self.send_sem.at[0, 0, 0], self.recv_sem.at[s], sibling).wait_recv()

                @pl.when(k == core)
                def _():
                    self.relay_copy(core, s).start()

    def finish(self):
        k = self.geo.here()[1]
        for s in range(self.geo.places):
            for core in range(2):

                @pl.when(k == core)
                def _():
                    self.relay_copy(1 - core, s).wait_recv()

    def wait_sent(self):
        k = self.geo.here()[1]
        for s in range(self.geo.places):
            for core in range(2):

                @pl.when(k == core)
                def _():
                    self.relay_copy(core, s).wait_send()

        for i, g, core, here, device in self.targets():

            @pl.when(jnp.logical_not(here))
            def _():
                remote(
                    self.own[core].at[i],
                    self.slot(core, 0),
                    self.send_sem.at[core, i, g],
                    self.recv_sem.at[0],
                    device,
                ).wait_send()
                remote(
                    self.tiles.at[i],
                    self.all_tiles.at[0],
                    self.tile_send.at[core, i, g],
                    self.tile_recv.at[0],
                    device,
                ).wait_send()


class ExpertGrads:
    def __init__(self, geo, grads, got, tiles, got_tiles, inbox, inbox_tiles, sems):
        self.geo, self.grads, self.got, self.tiles = geo, grads, got, tiles
        self.got_tiles, self.inbox, self.inbox_tiles = got_tiles, inbox, inbox_tiles
        (
            self.pair_send,
            self.pair_recv,
            self.send_sem,
            self.recv_sem,
            self.tile_send,
            self.tile_recv,
            self.local_sem,
            self.tile_local,
        ) = sems
        self.half = grads.shape[2] // 2
        self.part = grads.shape[2] // geo.places

    @staticmethod
    def sems(geo):
        dma = pltpu.SemaphoreType.DMA
        owners = (geo.local_experts, geo.group)
        return [
            dma((3,)),
            dma((3,)),
            dma((2, geo.places)),
            dma((2,) + owners),
            dma((geo.places,)),
            dma(owners),
            dma((2,)),
            dma,
        ]

    def columns(self, layer, first, count):
        return self.grads.at[layer, :, pl.ds(pl.multiple_of(first, 128), count)]

    def pair(self, layer):
        z, k, n = self.geo.here()
        away = self.columns(layer, (1 - k) * self.half, self.half)
        sibling = (z * 2 + 1 - k, n)
        return remote(away, self.got.at[layer], self.pair_send.at[layer], self.pair_recv.at[layer], sibling)

    def pair_tiles(self):
        z, k, n = self.geo.here()
        return remote(self.tiles, self.got_tiles, self.pair_send.at[2], self.pair_recv.at[2], (z * 2 + 1 - k, n))

    def towards(self):
        n = self.geo.here()[2]
        expert = n // self.geo.group
        return expert // self.geo.local_experts, expert % self.geo.local_experts, n % self.geo.group

    def slices(self):
        geo = self.geo
        z, k, n = geo.here()
        owner_core = self.towards()[0]
        for j in range(geo.places // 2):
            s = k * (geo.places // 2) + j
            yield s, jnp.logical_and(owner_core == k, n == s), (z * 2 + owner_core, s)

    def forward(self):
        k = self.geo.here()[1]
        _, i, g = self.towards()
        for layer in range(2):
            self.pair(layer).wait()
            for j in range(self.geo.places // 2):
                here = pl.ds(j * self.part, self.part)
                there = pl.ds(pl.multiple_of(k * self.half + j * self.part, 128), self.part)
                total = self.grads[layer, :, there].astype(F32) + self.got[layer, :, here].astype(F32)
                self.grads[layer, :, there] = total.astype(BF)
            for s, here, owner in self.slices():
                src = self.columns(layer, s * self.part, self.part)
                dst = self.inbox.at[layer, i, g]

                @pl.when(here)
                def _():
                    pltpu.make_async_copy(src, dst, self.local_sem.at[layer]).start()

                @pl.when(jnp.logical_not(here))
                def _():
                    remote(
                        src, dst, self.send_sem.at[layer, s], self.recv_sem.at[layer, i, g], owner
                    ).start()

        self.pair_tiles().wait()
        self.tiles[...] = self.tiles[...] + self.got_tiles[...]
        for s, here, owner in self.slices():
            src, dst = self.tiles.at[s], self.inbox_tiles.at[i, g]

            @pl.when(here)
            def _():
                pltpu.make_async_copy(src, dst, self.tile_local).start()

            @pl.when(jnp.logical_not(here))
            def _():
                remote(src, dst, self.tile_send.at[s], self.tile_recv.at[i, g], owner).start()

    def wait_got(self):
        geo = self.geo
        z, k, n = geo.here()
        sibling = (z * 2 + 1 - k, n)
        keeper = n // (geo.places // 2)
        for i in range(geo.local_experts):
            for g in range(geo.group):
                source = (k * geo.local_experts + i) * geo.group + g
                here = jnp.logical_and(source == n, keeper == k)
                for layer in range(2):
                    spot = self.inbox.at[layer, i, g]

                    @pl.when(here)
                    def _():
                        pltpu.make_async_copy(spot, spot, self.local_sem.at[layer]).wait()

                    @pl.when(jnp.logical_not(here))
                    def _():
                        remote(
                            spot, spot, self.send_sem.at[0, 0], self.recv_sem.at[layer, i, g], sibling
                        ).wait_recv()

                spot = self.inbox_tiles.at[i, g]

                @pl.when(here)
                def _():
                    pltpu.make_async_copy(spot, spot, self.tile_local).wait()

                @pl.when(jnp.logical_not(here))
                def _():
                    remote(spot, spot, self.tile_send.at[0], self.tile_recv.at[i, g], sibling).wait_recv()

    def wait_sent(self):
        for s, here, owner in self.slices():

            @pl.when(jnp.logical_not(here))
            def _():
                for layer in range(2):
                    src = self.columns(layer, s * self.part, self.part)
                    remote(
                        src, src, self.send_sem.at[layer, s], self.recv_sem.at[0, 0, 0], owner
                    ).wait_send()
                src = self.tiles.at[s]
                remote(src, src, self.tile_send.at[s], self.tile_recv.at[0, 0], owner).wait_send()


class DenseSum:
    def __init__(self, geo, mine, got_pair, got_plane, piece, got_z, whole, small, s_pair, s_plane, s_z, sems):
        self.geo, self.mine, self.got_pair, self.got_plane = geo, mine, got_pair, got_plane
        self.piece, self.got_z, self.whole = piece, got_z, whole
        self.small, self.s_pair, self.s_plane, self.s_z = small, s_pair, s_plane, s_z
        self.sems = sems
        self.half = mine.shape[0] // 2
        self.rows = self.half // geo.places
        self.columns = mine.shape[1] // geo.planes

    @staticmethod
    def semaphores(geo):
        dma = pltpu.SemaphoreType.DMA
        places, planes, both = (geo.places,), (geo.planes,), (geo.places, geo.planes)
        shapes = dict(
            pair=(1,), plane=places, z=planes, zg=planes, pg=both, cg=both, sp=(1,), sn=places, sz=planes
        )
        return list(shapes), [dma(s) for s in shapes.values() for _ in range(2)]

    def sem(self, name):
        names, _ = self.semaphores(self.geo)
        i = names.index(name) * 2
        return self.sems[i], self.sems[i + 1]

    def where(self):
        z, k, n = self.geo.here()
        return z, k, n, (z * 2 + 1 - k, n)

    def half_rows(self, k):
        return self.mine.at[pl.ds(pl.multiple_of(k * self.half, 16), self.half)]

    def pair(self):
        z, k, n, sibling = self.where()
        send, recv = self.sem("pair")
        return remote(self.half_rows(1 - k), self.got_pair, send.at[0], recv.at[0], sibling)

    def place_rows(self, k, q):
        return pl.ds(pl.multiple_of(k * self.half + q * self.rows, 16), self.rows)

    def plane_copy(self, q):
        z, k, n, _ = self.where()
        send, recv = self.sem("plane")
        src = self.mine.at[self.place_rows(k, q)]
        return remote(src, self.got_plane.at[n], send.at[q], recv.at[n], (z * 2 + k, q))

    def plane_start(self):
        z, k, n, _ = self.where()
        geo = self.geo
        self.pair().wait()
        keep = self.half_rows(k)
        step = self.half // 4
        for i in range(4):
            there = pl.ds(pl.multiple_of(k * self.half + i * step, 16), step)
            total = self.mine[there].astype(F32) + self.got_pair[i * step : (i + 1) * step].astype(F32)
            self.mine[there] = total.astype(BF)
        for i in range(1, geo.places):
            self.plane_copy(lax.rem(n + i, geo.places)).start()
        self.got_plane[n] = self.mine[self.place_rows(k, n)]

    def z_copy(self, q):
        z, k, n, _ = self.where()
        send, recv = self.sem("z")
        return remote(self.piece.at[q], self.got_z.at[z], send.at[q], recv.at[z], (q * 2 + k, n))

    def z_start(self):
        z, k, n, sibling = self.where()
        geo = self.geo
        send, recv = self.sem("plane")
        for i in range(1, geo.places):
            q = lax.rem(n + i, geo.places)
            spot = self.got_plane.at[q]
            remote(spot, spot, send.at[q], recv.at[q], sibling).wait_recv()
        for p in range(geo.planes):
            cols = slice(p * self.columns, (p + 1) * self.columns)
            total = self.got_plane[0, :, cols].astype(F32)
            for i in range(1, geo.places):
                total = total + self.got_plane[i, :, cols].astype(F32)
            self.piece[p] = total.astype(BF)
        for i in range(1, geo.planes):
            self.z_copy(lax.rem(z + i, geo.planes)).start()
        self.got_z[z] = self.piece[z]

    def spot(self, k, q, p):
        cols = pl.ds(pl.multiple_of(p * self.columns, 128), self.columns)
        return self.whole.at[self.place_rows(k, q), cols]

    def gather_copy(self, name, k, q, p, index, device):
        send, recv = self.sem(name)
        spot = self.spot(k, q, p)
        return remote(spot, spot, send.at[index], recv.at[index], device)

    def zg_copy(self, q):
        z, k, n, _ = self.where()
        send, recv = self.sem("zg")
        spot = self.spot(k, n, z)
        return remote(spot, spot, send.at[q], recv.at[z], (q * 2 + k, n))

    def pg_copy(self, q, p):
        z, k, n, _ = self.where()
        send, recv = self.sem("pg")
        spot = self.spot(k, n, p)
        return remote(spot, spot, send.at[q, p], recv.at[n, p], (z * 2 + k, q))

    def cg_copy(self, q, p):
        z, k, n, sibling = self.where()
        send, recv = self.sem("cg")
        spot = self.spot(k, q, p)
        return remote(spot, spot, send.at[q, p], recv.at[q, p], sibling)

    def gather_start(self):
        z, k, n, sibling = self.where()
        geo = self.geo
        send, recv = self.sem("z")
        for i in range(1, geo.planes):
            q = lax.rem(z + i, geo.planes)
            spot = self.got_z.at[q]
            remote(spot, spot, send.at[q], recv.at[q], sibling).wait_recv()
        total = self.got_z[0].astype(F32)
        for i in range(1, geo.planes):
            total = total + self.got_z[i].astype(F32)
        cols = pl.ds(pl.multiple_of(z * self.columns, 128), self.columns)
        self.whole[self.place_rows(k, n), cols] = total.astype(BF)
        for i in range(1, geo.planes):
            self.zg_copy(lax.rem(z + i, geo.planes)).start()
        send, recv = self.sem("zg")
        for i in range(geo.planes):
            p = lax.rem(z + i, geo.planes)
            if i > 0:
                spot = self.spot(k, n, p)
                remote(spot, spot, send.at[p], recv.at[p], sibling).wait_recv()
            for j in range(1, geo.places):
                self.pg_copy(lax.rem(n + j, geo.places), p).start()
            self.cg_copy(n, p).start()

    def gather_finish(self):
        z, k, n, sibling = self.where()
        geo = self.geo
        send, recv = self.sem("pg")
        for j in range(1, geo.places):
            q = lax.rem(n + j, geo.places)
            for i in range(geo.planes):
                p = lax.rem(z + i, geo.planes)
                spot = self.spot(k, q, p)
                remote(spot, spot, send.at[q, p], recv.at[q, p], sibling).wait_recv()
                self.cg_copy(q, p).start()
        send, recv = self.sem("cg")
        for q in range(geo.places):
            for p in range(geo.planes):
                spot = self.spot(1 - k, q, p)
                remote(spot, spot, send.at[q, p], recv.at[q, p], sibling).wait_recv()

    def small_pair(self):
        send, recv = self.sem("sp")
        return remote(self.small, self.s_pair, send.at[0], recv.at[0], self.where()[3])

    def sn_copy(self, q):
        z, k, n, _ = self.where()
        send, recv = self.sem("sn")
        return remote(self.s_plane.at[n], self.s_plane.at[n], send.at[q], recv.at[n], (z * 2 + k, q))

    def sz_copy(self, q):
        z, k, n, _ = self.where()
        send, recv = self.sem("sz")
        return remote(self.s_z.at[z], self.s_z.at[z], send.at[q], recv.at[z], (q * 2 + k, n))

    def small_plane(self):
        z, k, n, _ = self.where()
        self.small_pair().wait()
        self.s_plane[n] = self.small[...] + self.s_pair[...]
        for i in range(1, self.geo.places):
            self.sn_copy(lax.rem(n + i, self.geo.places)).start()

    def small_z(self):
        z, k, n, sibling = self.where()
        geo = self.geo
        send, recv = self.sem("sn")
        for i in range(1, geo.places):
            q = lax.rem(n + i, geo.places)
            spot = self.s_plane.at[q]
            remote(spot, spot, send.at[q], recv.at[q], sibling).wait_recv()
        total = self.s_plane[0]
        for i in range(1, geo.places):
            total = total + self.s_plane[i]
        self.s_z[z] = total
        for i in range(1, geo.planes):
            self.sz_copy(lax.rem(z + i, geo.planes)).start()

    def small_finish(self, out):
        z, k, n, sibling = self.where()
        geo = self.geo
        send, recv = self.sem("sz")
        for i in range(1, geo.planes):
            q = lax.rem(z + i, geo.planes)
            spot = self.s_z.at[q]
            remote(spot, spot, send.at[q], recv.at[q], sibling).wait_recv()
        total = self.s_z[0]
        for i in range(1, geo.planes):
            total = total + self.s_z[i]
        out[...] = total

    def wait_sent(self):
        z, k, n, _ = self.where()
        geo = self.geo
        for i in range(1, geo.places):
            q = lax.rem(n + i, geo.places)
            self.plane_copy(q).wait_send()
            self.sn_copy(q).wait_send()
            for p in range(geo.planes):
                self.pg_copy(q, p).wait_send()
        for i in range(1, geo.planes):
            q = lax.rem(z + i, geo.planes)
            self.z_copy(q).wait_send()
            self.zg_copy(q).wait_send()
            self.sz_copy(q).wait_send()
        for q in range(geo.places):
            for p in range(geo.planes):
                self.cg_copy(q, p).wait_send()


def greet_start(devices):
    barrier = pltpu.get_barrier_semaphore()
    for device in devices:
        pl.semaphore_signal(barrier, inc=1, device_id=device, device_id_type=MESH)


def all_devices(geo):
    z, k, n = geo.here()
    found = [(z * 2 + k, lax.rem(n + i, geo.places)) for i in range(1, geo.places)]
    found += [(z * 2 + 1 - k, lax.rem(n + i, geo.places)) for i in range(geo.places)]
    for i in range(1, geo.planes):
        other = lax.rem(z + i, geo.planes)
        found += [geo.partner(other * geo.plane_experts + j) for j in range(geo.plane_experts)]
    return found


def lane_row(row, count):
    shape = (count, row.shape[1])
    diagonal = lax.broadcasted_iota(jnp.int32, shape, 0) == lax.broadcasted_iota(jnp.int32, shape, 1)
    return jnp.sum(jnp.where(diagonal, row, 0.0), axis=1, keepdims=True)


def row_of(column, lanes):
    shape = (column.shape[0], lanes)
    diagonal = lax.broadcasted_iota(jnp.int32, shape, 0) == lax.broadcasted_iota(jnp.int32, shape, 1)
    return jnp.sum(jnp.where(diagonal, column, 0.0), axis=0, keepdims=True)


def put_pair(tail, high, low):
    row = lax.broadcasted_iota(jnp.int32, tail.shape, 0)
    return jnp.where(row == 14, high, jnp.where(row == 15, low, tail))


def block_kernel(geo, sizes, names, *refs):
    r = SimpleNamespace(**dict(zip(names, refs, strict=True)))
    rows, per_micro, seq, capacity, block, width, hidden = sizes
    experts = geo.partners
    slots = experts * block
    images = rows // seq
    z, k, n = geo.here()
    quad = geo.plane_experts
    chunk = quad * block
    part = r.w1.shape[2]
    tile = 256

    r.mine = r.hidden.at[0:width, 0 : 4 * width]
    r.grad_qkv = r.grad_pre.at[0:rows, 0 : 3 * width]
    r.grad_branch = r.grad_pre.at[rows : 2 * rows, 0:width]
    r.grad_att = r.grad_pre.at[rows : 2 * rows, width : 2 * width]
    r.logits_high = r.grad_pre.at[0:rows, 4 * width - 256 : 4 * width - 128]
    r.logits_low = r.grad_pre.at[0:rows, 4 * width - 128 : 4 * width]
    lanes = -(-rows // 128) * 128
    r.table0 = r.grad_pre.at[:, 0:lanes]
    r.slot_grad = r.grad_pre.at[:, 3 * width : 3 * width + 256]

    def span(i, count, align=16):
        return pl.ds(pl.multiple_of(i * count, align), count)

    def sems(name):
        return [ref for key, ref in zip(names, refs, strict=True) if key.startswith(name)]

    greet_start(all_devices(geo))
    for i in range(geo.local_experts):
        r.tile[i] = jnp.zeros((8, width), F32)
        r.tile[i, 0:1, 0:part] = r.b1[i : i + 1, :].astype(F32)
        r.tile[i, 1:2, :] = r.b2[i : i + 1, :].astype(F32)
    weights = Weights(
        geo, (r.w1, r.w2), (r.first, r.second), r.tile, r.tiles, sems("weights_sem")
    )
    cot_swap = Swap(geo, block, r.send_a, r.cot_got, sems("cot_sem"))
    x_swap = Swap(geo, block, r.send_b, r.x_got, sems("x_sem"))
    grad_swap = Swap(geo, block, r.send_a, r.grad_got, sems("grad_sem"))
    ret_swap = Swap(geo, block, r.send_b, r.ret_got, sems("ret_sem"))

    choices = r.choices[...]
    ids = lax.broadcasted_iota(jnp.int32, (experts, rows), 0)
    named = [ids == choices[i : i + 1, :] for i in range(2)]
    either = jnp.logical_or(named[0], named[1])
    first_row = lax.broadcasted_iota(jnp.int32, (rows, rows), 0)
    second_row = lax.broadcasted_iota(jnp.int32, (rows, rows), 1)
    same = (first_row >= per_micro) == (second_row >= per_micro)
    earlier = jnp.logical_and(first_row < second_row, same)
    before = dot(either.astype(F32).astype(BF), earlier.astype(F32).astype(BF))
    late = lax.broadcasted_iota(jnp.int32, (experts, rows), 1) >= per_micro
    slot = before + jnp.where(late, float(capacity), 0.0)
    r.held[...] = jnp.full(r.held.shape, -1.0, F32)
    r.held[0, :, 0:rows] = jnp.where(either, slot, -1.0)
    r.held[1, :, 0:rows] = jnp.where(named[0], slot, -1.0)
    spots = lax.broadcasted_iota(jnp.int32, (block, lanes), 0).astype(F32)

    def fill(e):
        here = span(e, block)
        either, chosen = [
            jnp.where(spots == r.held[i, pl.ds(e, 1), :], 1.0, 0.0).astype(BF) for i in range(2)
        ]
        r.table[here, :] = either[:, 0:rows]
        r.table0[here, :] = chosen

    each(experts, fill)
    r.table[pl.ds(slots, 128), :] = jnp.zeros((128, rows), BF)

    pl.semaphore_wait(pltpu.get_barrier_semaphore(), len(all_devices(geo)))
    weights.start()

    def send_cot(i):
        plane = lax.rem(z + 1 + i, geo.planes)
        blocks = dot(r.table[span(plane, chunk), :], r.cot[...])
        r.send_a[span(plane, chunk), :] = blocks.astype(BF)
        for j in range(quad):
            cot_swap.send(plane * quad + j)

    each(geo.planes, send_cot)

    def norm_in(i):
        unit, _ = norm_parts(r.tokens[span(i, seq), :].astype(F32))
        normed = unit * r.gain1[...].astype(F32) + r.shift1[...].astype(F32)
        r.normed[span(i, seq), :] = normed.astype(BF)

    each(images, norm_in)
    for c in range(3 * width // tile):
        cols = slice(c * tile, (c + 1) * tile)
        out = dot(r.normed[...], r.w_qkv[:, cols])
        if c * tile < width:
            out = out + r.bias_q[:, cols].astype(F32)
        elif c * tile >= 2 * width:
            out = out + r.bias_v[:, c * tile - 2 * width : (c + 1) * tile - 2 * width].astype(F32)
        r.qkv[:, cols] = out.astype(BF)

    def attend(i):
        here = span(i, seq)
        length = r.lengths[i // (per_micro // seq), i % (per_micro // seq)]
        r.attended[here, :] = attend_image(
            r.qkv[here, 0:width],
            r.qkv[here, width : 2 * width],
            r.qkv[here, 2 * width : 3 * width],
            length,
        )

    each(images, attend)

    def branch(i):
        here = span(i, seq)
        residual = (
            r.tokens[here, :].astype(F32)
            + dot(r.attended[here, :], r.w_out[...])
            + r.bias_out[...].astype(F32)
        )
        r.residual[here, :] = residual
        unit, _ = norm_parts(residual)
        expert_in = (unit * r.gain2[...].astype(F32) + r.shift2[...].astype(F32)).astype(BF)
        r.expert_in[here, :] = expert_in
        logits = dot(expert_in, r.w_router[...])
        raised = jnp.exp(logits - jnp.max(logits, axis=-1, keepdims=True))
        probs = raised / jnp.sum(raised, axis=-1, keepdims=True)
        r.probs[here, 0:experts] = probs

    r.probs[...] = jnp.zeros(r.probs.shape, F32)
    each(images, branch)
    probs_t = jnp.transpose(r.probs[...])[0:experts, :]
    high, low = split_two(probs_t)
    r.probs_t[0:experts, :] = high
    r.probs_t[experts : 2 * experts, :] = low

    def send_x(i):
        plane = lax.rem(z + 1 + i, geo.planes)
        blocks = dot(r.table[span(plane, chunk), :], r.expert_in[...])
        for j in range(quad):
            e = plane * quad + j
            at = e * block
            values = blocks[j * block : (j + 1) * block]
            gates = dot_nt(r.probs_t[...], r.table[pl.ds(pl.multiple_of(at, 16), 128), :])
            line = lax.broadcasted_iota(jnp.int32, gates.shape, 0)
            high = jnp.sum(jnp.where(line == e, gates, 0.0), axis=0, keepdims=True)
            low = jnp.sum(jnp.where(line == experts + e, gates, 0.0), axis=0, keepdims=True)
            r.send_b[span(e, block), :] = values.astype(BF)
            tail = put_pair(values[block - 16 :, 0:128], high, low)
            r.send_b[pl.ds(pl.multiple_of(at + block - 16, 16), 16), 0:128] = tail.astype(BF)
            x_swap.send(e)

    each(geo.planes, send_x)

    r.table_t[...] = jnp.transpose(r.table[0:slots, :])
    r.table0_t[...] = jnp.transpose(r.table0[...])[0:rows, :]
    weights.relay()
    weights.finish()
    for s in range(geo.places):
        r.bias1[:, s * part : (s + 1) * part] = jnp.broadcast_to(r.tiles[s, 0:1, 0:part], (8, part))
    cot_swap.wait_sent()
    x_swap.wait_sent()

    root = 0.7978845608028654
    r.sum_pre[...] = jnp.zeros(r.sum_pre.shape, F32)
    r.sum_ret[...] = jnp.zeros(r.sum_ret.shape, F32)

    def expert_chunk(i):
        plane = lax.rem(z + i, geo.planes)
        here = span(plane, chunk)
        for j in range(quad):
            cot_swap.wait_got(plane * quad + j)
        for j in range(quad):
            x_swap.wait_got(plane * quad + j)
        for j in range(quad):
            at = (plane * quad + j) * block
            tail = r.x_got[pl.ds(pl.multiple_of(at + block - 16, 16), 16), 0:128].astype(F32)
            gate = lane_row(tail[14:15] + tail[15:16], block)
            there = span(plane * quad + j, block)
            r.grad_ret[there, :] = (gate * r.cot_got[there, :].astype(F32)).astype(BF)
        total_ret = jnp.sum(r.grad_ret[here, :].astype(F32), axis=0, keepdims=True)
        r.sum_ret[0:1, :] = r.sum_ret[0:1, :] + total_ret
        for c in range(hidden // tile):
            cols = slice(c * tile, (c + 1) * tile)
            pre = dot(r.x_got[here, :], r.first[:, cols]) + r.bias1[0:1, cols]
            square = pre * pre
            bend = jnp.tanh(root * pre * (1.0 + 0.044715 * square))
            half = 0.5 * (1.0 + bend)
            r.hidden[here, cols] = (pre * half).astype(BF)
            slope = half + 0.5 * pre * (1.0 - bend * bend) * (root + 3 * 0.044715 * root * square)
            back = dot_nt(r.grad_ret[here, :], r.second[cols, :])
            grad_pre = (back * slope).astype(BF)
            r.grad_pre[here, cols] = grad_pre
            total = jnp.sum(grad_pre.astype(F32), axis=0, keepdims=True)
            r.sum_pre[0:1, cols] = r.sum_pre[0:1, cols] + total
        returned = dot(r.hidden[here, :], r.second[...]) + r.tiles[0, 1:2, :]
        r.send_b[here, :] = returned.astype(BF)
        grad_in = dot_nt(r.grad_pre[here, :], r.first[...])
        for j in range(quad):
            e = plane * quad + j
            there = span(e, block)
            product = r.cot_got[there, :].astype(F32) * r.send_b[there, :].astype(F32)
            high, low = split_two(row_of(jnp.sum(product, axis=-1, keepdims=True), 128))
            values = grad_in[j * block : (j + 1) * block]
            r.send_a[there, :] = values.astype(BF)
            tail = put_pair(values[block - 16 :, 0:128], high.astype(F32), low.astype(F32))
            at = pl.ds(pl.multiple_of(e * block + block - 16, 16), 16)
            r.send_a[at, 0:128] = tail.astype(BF)
            grad_swap.send(e)

    each(geo.planes, expert_chunk)
    each(experts, lambda i: ret_swap.send(lax.rem(geo.mine() + 1 + i, experts)))

    grads = ExpertGrads(
        geo,
        r.d_experts,
        r.d_got,
        r.d_tiles,
        r.d_got_tiles,
        r.inbox,
        r.inbox_tiles,
        sems("expert_sem"),
    )
    quarter = hidden // 4

    def weight_grads(side):
        for layer, left, right in ((0, r.x_got, r.grad_pre), (1, r.grad_ret, r.hidden)):
            for c in range(2):
                cols = pl.ds(pl.multiple_of(side * (hidden // 2) + c * quarter, 128), quarter)
                r.d_experts[layer, :, cols] = dot_tn(left[...], right[:, cols]).astype(BF)

    weight_grads(1 - k)
    grads.pair(0).start()
    grads.pair(1).start()
    r.d_tiles[...] = jnp.zeros(r.d_tiles.shape, F32)
    for s in range(geo.places):
        r.d_tiles[s, 0:1, 0:part] = r.sum_pre[0:1, s * part : (s + 1) * part]
        r.d_tiles[s, 1:2, :] = r.sum_ret[0:1, :]
    grads.pair_tiles().start()
    weight_grads(k)
    grads.forward()

    dense = DenseSum(
        geo,
        r.mine,
        r.got_pair,
        r.got_plane,
        r.piece,
        r.got_z,
        r.whole,
        r.small,
        r.s_pair,
        r.s_plane,
        r.s_z,
        sems("dense_sem"),
    )

    def slot_grads(e):
        grad_swap.wait_got(e)
        at = pl.ds(pl.multiple_of(e * block + block - 16, 16), 16)
        tail = r.grad_got[at, 0:128].astype(F32)
        column = lane_row(tail[14:15] + tail[15:16], block)
        lane = lax.broadcasted_iota(jnp.int32, (block, 128), 1)
        high, low = split_two(jnp.where(lane == e, column, 0.0))
        r.slot_grad[span(e, block), 0:128] = high
        r.slot_grad[span(e, block), 128:256] = low

    each(experts, slot_grads)
    for c in range(width // tile):
        cols = slice(c * tile, (c + 1) * tile)
        r.grad_two[:, cols] = dot(r.table_t[...], r.grad_got[:, cols])
    both = dot(r.table_t[...], r.slot_grad[...])
    r.grad_choice[...] = both[:, 0:128] + both[:, 128:256]
    r.small[...] = jnp.zeros(r.small.shape, F32)

    def add_small(row, value):
        r.small[row : row + 1, :] = r.small[row : row + 1, :] + jnp.sum(value, axis=0, keepdims=True)

    def norm_two_back(i):
        here = span(i, seq)
        probs = r.probs[here, :]
        choice = r.grad_choice[here, :]
        logits = probs * (choice - jnp.sum(probs * choice, axis=-1, keepdims=True))
        high, low = split_two(logits)
        r.logits_high[here, :] = high
        r.logits_low[here, :] = low
        weight = r.w_router[...]
        grad = r.grad_two[here, :]
        grad = grad + dot_nt(high[:, 0:experts], weight) + dot_nt(low[:, 0:experts], weight)
        unit, scale = norm_parts(r.residual[here, :])
        add_small(5, grad * unit)
        add_small(6, grad)
        grad = r.cot[here, :].astype(F32) + norm_back(grad, unit, scale, r.gain2[...].astype(F32))
        r.grad_two[here, :] = grad
        low_grad = grad.astype(BF)
        r.grad_branch[here, :] = low_grad
        add_small(4, low_grad.astype(F32))

    each(images, norm_two_back)
    for c in range(width // tile):
        cols = slice(c * tile, (c + 1) * tile)
        r.grad_att[:, cols] = dot_nt(r.grad_branch[...], r.w_out[cols, :]).astype(BF)
        out = dot_tn(r.attended[...], r.grad_branch[:, cols])
        r.mine[:, 3 * width + c * tile : 3 * width + (c + 1) * tile] = out.astype(BF)
    router = dot_tn(r.logits_high[...], r.expert_in[...]) + dot_tn(
        r.logits_low[...], r.expert_in[...]
    )
    r.small[8 : 8 + experts, :] = router[0:experts, :]

    def attend_back(i):
        here = span(i, seq)
        length = r.lengths[i // (per_micro // seq), i % (per_micro // seq)]
        parts = attend_image_back(
            r.qkv[here, 0:width],
            r.qkv[here, width : 2 * width],
            r.qkv[here, 2 * width : 3 * width],
            length,
            r.grad_att[here, :],
        )
        for c, value in enumerate(parts):
            r.grad_qkv[here, c * width : (c + 1) * width] = value
        add_small(2, parts[0].astype(F32))
        add_small(3, parts[2].astype(F32))

    each(images, attend_back)
    for c in range(3 * width // tile):
        cols = slice(c * tile, (c + 1) * tile)
        r.mine[:, cols] = dot_tn(r.normed[...], r.grad_qkv[:, cols]).astype(BF)
    dense.pair().start()

    def norm_one_back(i):
        here = span(i, seq)
        grad = dot_nt(r.grad_qkv[here, :], r.w_qkv[...])
        unit, scale = norm_parts(r.tokens[here, :].astype(F32))
        add_small(0, grad * unit)
        add_small(1, grad)
        r.grad_two[here, :] = r.grad_two[here, :] + norm_back(
            grad, unit, scale, r.gain1[...].astype(F32)
        )

    each(images, norm_one_back)
    dense.small_pair().start()
    tokens_copy = pltpu.make_async_copy(r.grad_two, r.grad_tokens, r.out_sem.at[1])
    tokens_copy.start()
    dense.plane_start()
    dense.small_plane()

    each(experts, ret_swap.wait_got)

    def mix(i):
        here = span(i, seq)
        total = dot(r.table_t[here, :], r.ret_got[...])
        chosen = dot(r.table0_t[here, :], r.ret_got[...])
        probs = r.probs[here, :]
        lane = lax.broadcasted_iota(jnp.int32, probs.shape, 1)
        gates = [
            jnp.sum(jnp.where(lane == r.ids[here, j : j + 1], probs, 0.0), axis=-1, keepdims=True)
            for j in range(2)
        ]
        mixed = r.residual[here, :] + gates[0] * chosen + gates[1] * (total - chosen)
        r.expert_in[here, :] = mixed.astype(BF)

    each(images, mix)
    mixed_copy = pltpu.make_async_copy(r.expert_in, r.mixed, r.out_sem.at[0])
    mixed_copy.start()
    dense.small_z()
    dense.z_start()
    grads.wait_got()
    layers_copy = pltpu.make_async_copy(r.inbox, r.d_layers, r.out_sem.at[2])
    bias_copy = pltpu.make_async_copy(r.inbox_tiles, r.d_bias, r.out_sem.at[3])
    layers_copy.start()
    bias_copy.start()
    dense.gather_start()
    dense.small_finish(r.small_out)
    dense.gather_finish()
    big_copy = pltpu.make_async_copy(r.whole, r.big_out, r.out_sem.at[4])
    big_copy.start()
    grad_swap.wait_sent()
    ret_swap.wait_sent()
    weights.wait_sent()
    grads.wait_sent()
    dense.wait_sent()
    for copy in (mixed_copy, tokens_copy, layers_copy, bias_copy, big_copy):
        copy.wait()


def on_device(
    geo,
    tokens,
    image_lengths,
    expert_index,
    grad_out,
    ln1_gain,
    ln1_bias,
    w_qkv,
    bias_query,
    bias_value,
    w_out,
    bias_out,
    ln2_gain,
    ln2_bias,
    w_router,
    experts_in,
    experts_in_bias,
    experts_out,
    experts_out_bias,
):
    micros, per_micro, width = tokens.shape
    rows = micros * per_micro
    seq = per_micro // image_lengths.shape[1]
    experts = geo.partners
    capacity = (per_micro * 42 + 20 * experts - 1) // (20 * experts)
    block = -(-(micros * capacity + 2) // 16) * 16
    slots = experts * block
    part = experts_in.shape[2]
    hidden = part * geo.places
    places, planes, local, group = geo.places, geo.planes, geo.local_experts, geo.group
    flat_ids = expert_index.reshape(rows, 2)
    row = lambda v: v[None, :]
    inputs = dict(
        tokens=tokens.reshape(rows, width),
        cot=grad_out.reshape(rows, width),
        choices=flat_ids.T,
        ids=flat_ids,
        lengths=image_lengths,
        gain1=row(ln1_gain),
        shift1=row(ln1_bias),
        w_qkv=w_qkv,
        bias_q=row(bias_query),
        bias_v=row(bias_value),
        w_out=w_out,
        bias_out=row(bias_out),
        gain2=row(ln2_gain),
        shift2=row(ln2_bias),
        w_router=w_router,
        w1=experts_in,
        b1=experts_in_bias,
        w2=experts_out,
        b2=experts_out_bias,
    )
    vmem, smem = pl.BlockSpec(memory_space=pltpu.VMEM), pl.BlockSpec(memory_space=pltpu.SMEM)
    anywhere = pl.BlockSpec(memory_space=pl.ANY)
    in_specs = {name: vmem for name in inputs}
    in_specs.update(lengths=smem, w1=anywhere, w2=anywhere)
    small_rows = 8 + experts
    outputs = dict(
        mixed=((rows, width), BF, anywhere),
        grad_tokens=((rows, width), F32, anywhere),
        big_out=((width, 4 * width), BF, anywhere),
        small_out=((small_rows, width), F32, vmem),
        d_layers=((2, local, group, width, part), BF, anywhere),
        d_bias=((local, group, 8, width), F32, anywhere),
    )
    half = width // 2
    scratch = dict(
        tile=((local, 8, width), F32),
        tiles=((places, 8, width), F32),
        first=((width, hidden), BF),
        second=((hidden, width), BF),
        bias1=((8, hidden), F32),
        held=((2, experts, -(-rows // 128) * 128), F32),
        table=((slots + 128, rows), BF),
        table_t=((rows, slots), BF),
        table0_t=((rows, slots), BF),
        send_a=((slots, width), BF),
        send_b=((slots, width), BF),
        cot_got=((slots, width), BF),
        x_got=((slots, width), BF),
        grad_got=((slots, width), BF),
        ret_got=((slots, width), BF),
        normed=((rows, width), BF),
        qkv=((rows, 3 * width), BF),
        attended=((rows, width), BF),
        residual=((rows, width), F32),
        expert_in=((rows, width), BF),
        probs=((rows, 128), F32),
        probs_t=((2 * experts, rows), BF),
        grad_ret=((slots, width), BF),
        hidden=((slots, hidden), BF),
        grad_pre=((slots, hidden), BF),
        sum_pre=((8, hidden), F32),
        sum_ret=((8, width), F32),
        d_experts=((2, width, hidden), BF),
        d_got=((2, width, hidden // 2), BF),
        d_tiles=((places, 8, width), F32),
        d_got_tiles=((places, 8, width), F32),
        inbox=((2, local, group, width, part), BF),
        inbox_tiles=((local, group, 8, width), F32),
        grad_two=((rows, width), F32),
        grad_choice=((rows, 128), F32),
        got_pair=((half, 4 * width), BF),
        got_plane=((places, half // places, 4 * width), BF),
        piece=((planes, half // places, 4 * width // planes), BF),
        got_z=((planes, half // places, 4 * width // planes), BF),
        whole=((width, 4 * width), BF),
        small=((small_rows, width), F32),
        s_pair=((small_rows, width), F32),
        s_plane=((places, small_rows, width), F32),
        s_z=((planes, small_rows, width), F32),
    )
    sem_sets = dict(
        weights_sem=Weights.sems(geo),
        cot_sem=swap_sems(geo),
        x_sem=swap_sems(geo),
        grad_sem=swap_sems(geo),
        ret_sem=swap_sems(geo),
        expert_sem=ExpertGrads.sems(geo),
        dense_sem=DenseSum.semaphores(geo)[1],
    )
    sem_names = [name + str(i) for name, found in sem_sets.items() for i in range(len(found))]
    sem_shapes = [s for found in sem_sets.values() for s in found]
    names = [*inputs, *outputs, *scratch, *sem_names, "out_sem"]
    sizes = (rows, per_micro, seq, capacity, block, width, hidden)
    results = pl.pallas_call(
        functools.partial(block_kernel, geo, sizes, names),
        out_shape=[jax.ShapeDtypeStruct(shape, dtype) for shape, dtype, _ in outputs.values()],
        in_specs=list(in_specs.values()),
        out_specs=[spec for _, _, spec in outputs.values()],
        scratch_shapes=[pltpu.VMEM(shape, dtype) for shape, dtype in scratch.values()]
        + sem_shapes
        + [pltpu.SemaphoreType.DMA((5,))],
        compiler_params=pltpu.CompilerParams(
            collective_id=0, has_side_effects=True, vmem_limit_bytes=VMEM_LIMIT
        ),
    )(*inputs.values())
    out = dict(zip(outputs, results, strict=True))
    big, small = out["big_out"], out["small_out"]
    layers = jnp.sum(out["d_layers"].astype(F32), axis=2)
    d_bias = jnp.sum(out["d_bias"], axis=1)
    return (
        out["mixed"].reshape(tokens.shape),
        out["grad_tokens"].reshape(tokens.shape),
        small[0],
        small[1],
        big[:, : 3 * width].astype(F32),
        small[2],
        small[3],
        big[:, 3 * width :].astype(F32),
        small[4],
        small[5],
        small[6],
        small[8:].T,
        layers[0],
        d_bias[:, 0, :part],
        jnp.swapaxes(layers[1], 1, 2),
        d_bias[:, 1, :],
    )


def solution(mesh):
    split = ("wide", "narrow")
    in_specs = (
        P(None, split, None),
        P(None, split),
        P(None, split, None),
        P(None, split, None),
        *([P()] * 10),
        P("wide", None, "narrow"),
        P("wide", "narrow"),
        P("wide", "narrow", None),
        P("wide", None),
    )
    out_specs = (
        P(None, split, None),
        P(None, split, None),
        *([P()] * 10),
        P("wide", None, "narrow"),
        P("wide", "narrow"),
        P("wide", "narrow", None),
        P("wide", None),
    )

    def step(*args):
        geo = Geometry(mesh.shape["wide"], mesh.shape["narrow"], args[14].shape[0])
        return on_device(geo, *args)

    return jax.shard_map(step, mesh=mesh, in_specs=in_specs, out_specs=out_specs, check_vma=False)
```

```python
import functools
from types import SimpleNamespace

import jax
import jax.numpy as jnp
from jax import lax
from jax.experimental import pallas as pl
from jax.experimental.pallas import tpu as pltpu
from jax.sharding import PartitionSpec as P

HEADS = 8
HEAD_DIM = 64
MESH = pl.DeviceIdType.MESH
BF = jnp.bfloat16
F32 = jnp.float32
VMEM_LIMIT = 62 * 2**20


def dot(a, b):
    return lax.dot_general(a, b, (((1,), (0,)), ((), ())), preferred_element_type=F32)


def dot_nt(a, b):
    return lax.dot_general(a, b, (((1,), (1,)), ((), ())), preferred_element_type=F32)


def dot_tn(a, b):
    return lax.dot_general(a, b, (((0,), (0,)), ((), ())), preferred_element_type=F32)


class Geometry:
    def __init__(self, n_wide, n_narrow, local_experts):
        self.planes = n_wide // 2
        self.places = n_narrow
        self.local_experts = local_experts
        self.plane_experts = 2 * local_experts
        self.group = n_narrow // self.plane_experts
        self.partners = self.planes * self.plane_experts

    def here(self):
        wide, place = lax.axis_index("wide"), lax.axis_index("narrow")
        return wide // 2, wide % 2, place

    def mine(self):
        z, _, n = self.here()
        return z * self.plane_experts + n // self.group

    def partner(self, p):
        _, k, n = self.here()
        place = (p % self.plane_experts) * self.group + n % self.group
        return ((p // self.plane_experts) * 2 + k, place)


def remote(src, dst, send_sem, recv_sem, device):
    return pltpu.make_async_remote_copy(
        src_ref=src,
        dst_ref=dst,
        send_sem=send_sem,
        recv_sem=recv_sem,
        device_id=device,
        device_id_type=MESH,
    )


def norm_parts(values):
    centred = values - jnp.mean(values, axis=-1, keepdims=True)
    scale = lax.rsqrt(jnp.mean(centred * centred, axis=-1, keepdims=True) + 1e-06)
    return centred * scale, scale


def norm_back(grad, unit, scale, gain):
    pulled = grad * gain
    inner = jnp.mean(pulled, axis=-1, keepdims=True)
    along = jnp.mean(pulled * unit, axis=-1, keepdims=True)
    return scale * (pulled - inner - unit * along)


def head_pair(rows, low):
    zero = jnp.zeros_like(rows)
    return jnp.concatenate([jnp.where(low, rows, zero), jnp.where(low, zero, rows)], axis=0)


def pair_probs(stacked, keys, length):
    scores = dot_nt(stacked, keys) * HEAD_DIM ** (-0.5)
    visible = lax.broadcasted_iota(jnp.int32, scores.shape, 1) < length
    scores = jnp.where(visible, scores, -1e30)
    raised = jnp.exp(scores - jnp.max(scores, axis=-1, keepdims=True))
    return raised / jnp.sum(raised, axis=-1, keepdims=True)


def attend_image(queries, keys, values, length):
    seq = queries.shape[0]
    low = lax.broadcasted_iota(jnp.int32, (seq, 128), 1) < HEAD_DIM
    parts = []
    for g in range(queries.shape[1] // 128):
        cols = slice(g * 128, (g + 1) * 128)
        probs = pair_probs(head_pair(queries[:, cols], low), keys[:, cols], length).astype(BF)
        out = dot(probs, values[:, cols])
        parts.append(jnp.where(low, out[:seq], out[seq:]).astype(BF))
    return jnp.concatenate(parts, axis=1)


def attend_image_back(queries, keys, values, length, grad):
    seq = queries.shape[0]
    low = lax.broadcasted_iota(jnp.int32, (seq, 128), 1) < HEAD_DIM
    scale = HEAD_DIM ** (-0.5)
    parts = ([], [], [])
    for g in range(queries.shape[1] // 128):
        cols = slice(g * 128, (g + 1) * 128)
        stacked = head_pair(queries[:, cols], low)
        stacked_grad = head_pair(grad[:, cols], low)
        probs = pair_probs(stacked, keys[:, cols], length)
        grad_probs = dot_nt(stacked_grad, values[:, cols])
        parts[2].append(dot_tn(probs.astype(BF), stacked_grad).astype(BF))
        centre = jnp.sum(probs * grad_probs, axis=-1, keepdims=True)
        grad_scores = (probs * (grad_probs - centre)).astype(BF)
        grad_q = dot(grad_scores, keys[:, cols])
        parts[0].append((jnp.where(low, grad_q[:seq], grad_q[seq:]) * scale).astype(BF))
        parts[1].append((dot_tn(grad_scores, stacked) * scale).astype(BF))
    return [jnp.concatenate(part, axis=1) for part in parts]


def split_two(values):
    high = values.astype(BF)
    return high, (values - high.astype(F32)).astype(BF)


def each(count, step, unroll=False):
    if unroll:
        for i in range(count):
            step(i)
    else:

        def body(i, _):
            step(i)
            return 0

        lax.fori_loop(0, count, body, 0)


class Swap:
    def __init__(self, geo, block, src, dst, sems, first=0, count=None, base=0):
        self.geo, self.block, self.src, self.dst = geo, block, src, dst
        self.first, self.count, self.base = first, count or block, base
        self.send_sem, self.recv_sem, self.local_sem = sems

    def given(self, p):
        return self.src.at[pl.ds(pl.multiple_of(p * self.block + self.first, 16), self.count)]

    def kept(self, p):
        return self.dst.at[pl.ds(pl.multiple_of(self.base + p * self.count, 16), self.count)]

    def local(self):
        mine = self.geo.mine()
        return pltpu.make_async_copy(self.given(mine), self.kept(mine), self.local_sem)

    def send(self, p):
        mine = self.geo.mine()

        @pl.when(p == mine)
        def _():
            self.local().start()

        @pl.when(p != mine)
        def _():
            remote(
                self.given(p),
                self.kept(mine),
                self.send_sem.at[p],
                self.recv_sem.at[mine],
                self.geo.partner(p),
            ).start()

    def copy(self, p):
        return remote(
            self.given(p),
            self.kept(p),
            self.send_sem.at[p],
            self.recv_sem.at[p],
            self.geo.partner(p),
        )

    def wait_got(self, p):
        mine = self.geo.mine()

        @pl.when(p == mine)
        def _():
            self.local().wait()

        @pl.when(p != mine)
        def _():
            self.copy(p).wait_recv()

    def wait_sent(self):
        mine = self.geo.mine()
        each(self.geo.partners - 1, lambda i: self.copy(lax.rem(mine + 1 + i, self.geo.partners)).wait_send())


def swap_sems(geo):
    dma = pltpu.SemaphoreType.DMA
    return [dma((geo.partners,)), dma((geo.partners,)), dma]


class Weights:
    def __init__(self, geo, own, full, tiles, all_tiles, sems):
        self.geo, self.own, self.full, self.tiles, self.all_tiles = geo, own, full, tiles, all_tiles
        (
            self.send_sem,
            self.recv_sem,
            self.tile_send,
            self.tile_recv,
            self.relay_send,
            self.relay_recv,
            self.local_sem,
            self.tile_local,
        ) = sems

    @staticmethod
    def sems(geo):
        dma = pltpu.SemaphoreType.DMA
        sends, places = (2, geo.local_experts, geo.group), (geo.places,)
        return [dma(sends), dma(places), dma(sends), dma(places), dma(places), dma(places), dma, dma]

    def slot(self, core, s):
        part = self.own[core].shape[2 - core]
        spot = pl.ds(pl.multiple_of(s * part, 128), part)
        return self.full[0].at[:, spot] if core == 0 else self.full[1].at[spot]

    def targets(self):
        geo = self.geo
        z, k, n = geo.here()
        for i in range(geo.local_experts):
            for g in range(geo.group):
                place = (geo.local_experts * k + i) * geo.group + g
                for core in range(2):
                    yield i, g, core, jnp.logical_and(k == core, place == n), (z * 2 + core, place)

    def start(self):
        n = self.geo.here()[2]
        for i, g, core, here, device in self.targets():

            @pl.when(here)
            def _():
                pltpu.make_async_copy(self.own[core].at[i], self.slot(core, n), self.local_sem).start()
                pltpu.make_async_copy(self.tiles.at[i], self.all_tiles.at[n], self.tile_local).start()

            @pl.when(jnp.logical_not(here))
            def _():
                remote(
                    self.own[core].at[i],
                    self.slot(core, n),
                    self.send_sem.at[core, i, g],
                    self.recv_sem.at[n],
                    device,
                ).start()
                remote(
                    self.tiles.at[i],
                    self.all_tiles.at[n],
                    self.tile_send.at[core, i, g],
                    self.tile_recv.at[n],
                    device,
                ).start()

    def relay_copy(self, core, s):
        z, k, n = self.geo.here()
        spot = self.slot(core, s)
        return remote(spot, spot, self.relay_send.at[s], self.relay_recv.at[s], (z * 2 + 1 - k, n))

    def relay(self):
        geo = self.geo
        z, k, n = geo.here()
        owner_core = (n // geo.group) // geo.local_experts
        sibling = (z * 2 + 1 - k, n)
        for s in range(geo.places):
            here = jnp.logical_and(k == owner_core, n == s)

            @pl.when(here)
            def _():
                pltpu.make_async_copy(self.tiles.at[0], self.all_tiles.at[s], self.tile_local).wait()

            @pl.when(jnp.logical_not(here))
            def _():
                spot = self.all_tiles.at[s]
                remote(spot, spot, self.tile_send.at[0, 0, 0], self.tile_recv.at[s], sibling).wait_recv()

            for core in range(2):
                spot = self.slot(core, s)

                @pl.when(jnp.logical_and(k == core, here))
                def _():
                    pltpu.make_async_copy(self.own[core].at[0], spot, self.local_sem).wait()

                @pl.when(jnp.logical_and(k == core, jnp.logical_not(here)))
                def _():
                    remote(spot, spot, self.send_sem.at[0, 0, 0], self.recv_sem.at[s], sibling).wait_recv()

                @pl.when(k == core)
                def _():
                    self.relay_copy(core, s).start()

    def finish(self):
        k = self.geo.here()[1]
        for s in range(self.geo.places):
            for core in range(2):

                @pl.when(k == core)
                def _():
                    self.relay_copy(1 - core, s).wait_recv()

    def wait_sent(self):
        k = self.geo.here()[1]
        for s in range(self.geo.places):
            for core in range(2):

                @pl.when(k == core)
                def _():
                    self.relay_copy(core, s).wait_send()

        for i, g, core, here, device in self.targets():

            @pl.when(jnp.logical_not(here))
            def _():
                remote(
                    self.own[core].at[i],
                    self.slot(core, 0),
                    self.send_sem.at[core, i, g],
                    self.recv_sem.at[0],
                    device,
                ).wait_send()
                remote(
                    self.tiles.at[i],
                    self.all_tiles.at[0],
                    self.tile_send.at[core, i, g],
                    self.tile_recv.at[0],
                    device,
                ).wait_send()


class ExpertGrads:
    def __init__(self, geo, grads, got, tiles, got_tiles, inbox, inbox_tiles, sems):
        self.geo, self.grads, self.got, self.tiles = geo, grads, got, tiles
        self.got_tiles, self.inbox, self.inbox_tiles = got_tiles, inbox, inbox_tiles
        (
            self.pair_send,
            self.pair_recv,
            self.send_sem,
            self.recv_sem,
            self.tile_send,
            self.tile_recv,
            self.local_sem,
            self.tile_local,
        ) = sems
        self.half = grads.shape[2] // 2
        self.part = grads.shape[2] // geo.places

    @staticmethod
    def sems(geo):
        dma = pltpu.SemaphoreType.DMA
        owners = (geo.local_experts, geo.group)
        return [
            dma((3,)),
            dma((3,)),
            dma((2, geo.places)),
            dma((2,) + owners),
            dma((geo.places,)),
            dma(owners),
            dma((2,)),
            dma,
        ]

    def columns(self, layer, first, count):
        return self.grads.at[layer, :, pl.ds(pl.multiple_of(first, 128), count)]

    def pair(self, layer):
        z, k, n = self.geo.here()
        away = self.columns(layer, (1 - k) * self.half, self.half)
        sibling = (z * 2 + 1 - k, n)
        return remote(away, self.got.at[layer], self.pair_send.at[layer], self.pair_recv.at[layer], sibling)

    def pair_tiles(self):
        z, k, n = self.geo.here()
        return remote(self.tiles, self.got_tiles, self.pair_send.at[2], self.pair_recv.at[2], (z * 2 + 1 - k, n))

    def towards(self):
        n = self.geo.here()[2]
        expert = n // self.geo.group
        return expert // self.geo.local_experts, expert % self.geo.local_experts, n % self.geo.group

    def slices(self):
        geo = self.geo
        z, k, n = geo.here()
        owner_core = self.towards()[0]
        for j in range(geo.places // 2):
            s = k * (geo.places // 2) + j
            yield s, jnp.logical_and(owner_core == k, n == s), (z * 2 + owner_core, s)

    def forward(self):
        k = self.geo.here()[1]
        _, i, g = self.towards()
        for layer in range(2):
            self.pair(layer).wait()
            for j in range(self.geo.places // 2):
                here = pl.ds(j * self.part, self.part)
                there = pl.ds(pl.multiple_of(k * self.half + j * self.part, 128), self.part)
                total = self.grads[layer, :, there].astype(F32) + self.got[layer, :, here].astype(F32)
                self.grads[layer, :, there] = total.astype(BF)
            for s, here, owner in self.slices():
                src = self.columns(layer, s * self.part, self.part)
                dst = self.inbox.at[layer, i, g]

                @pl.when(here)
                def _():
                    pltpu.make_async_copy(src, dst, self.local_sem.at[layer]).start()

                @pl.when(jnp.logical_not(here))
                def _():
                    remote(
                        src, dst, self.send_sem.at[layer, s], self.recv_sem.at[layer, i, g], owner
                    ).start()

        self.pair_tiles().wait()
        self.tiles[...] = self.tiles[...] + self.got_tiles[...]
        for s, here, owner in self.slices():
            src, dst = self.tiles.at[s], self.inbox_tiles.at[i, g]

            @pl.when(here)
            def _():
                pltpu.make_async_copy(src, dst, self.tile_local).start()

            @pl.when(jnp.logical_not(here))
            def _():
                remote(src, dst, self.tile_send.at[s], self.tile_recv.at[i, g], owner).start()

    def wait_got(self):
        geo = self.geo
        z, k, n = geo.here()
        sibling = (z * 2 + 1 - k, n)
        keeper = n // (geo.places // 2)
        for i in range(geo.local_experts):
            for g in range(geo.group):
                source = (k * geo.local_experts + i) * geo.group + g
                here = jnp.logical_and(source == n, keeper == k)
                for layer in range(2):
                    spot = self.inbox.at[layer, i, g]

                    @pl.when(here)
                    def _():
                        pltpu.make_async_copy(spot, spot, self.local_sem.at[layer]).wait()

                    @pl.when(jnp.logical_not(here))
                    def _():
                        remote(
                            spot, spot, self.send_sem.at[0, 0], self.recv_sem.at[layer, i, g], sibling
                        ).wait_recv()

                spot = self.inbox_tiles.at[i, g]

                @pl.when(here)
                def _():
                    pltpu.make_async_copy(spot, spot, self.tile_local).wait()

                @pl.when(jnp.logical_not(here))
                def _():
                    remote(spot, spot, self.tile_send.at[0], self.tile_recv.at[i, g], sibling).wait_recv()

    def wait_sent(self):
        for s, here, owner in self.slices():

            @pl.when(jnp.logical_not(here))
            def _():
                for layer in range(2):
                    src = self.columns(layer, s * self.part, self.part)
                    remote(
                        src, src, self.send_sem.at[layer, s], self.recv_sem.at[0, 0, 0], owner
                    ).wait_send()
                src = self.tiles.at[s]
                remote(src, src, self.tile_send.at[s], self.tile_recv.at[0, 0], owner).wait_send()


class DenseSum:
    def __init__(
        self,
        geo,
        mine,
        got_pair,
        got_plane,
        piece,
        got_z,
        wide_z,
        wide_sum,
        wide_plane,
        whole,
        small,
        s_pair,
        s_plane,
        s_z,
        sems,
        wide_chunk,
    ):
        self.geo, self.mine, self.got_pair, self.got_plane = geo, mine, got_pair, got_plane
        self.piece, self.got_z, self.whole = piece, got_z, whole
        self.wide_z, self.wide_sum, self.wide_plane = wide_z, wide_sum, wide_plane
        self.wide_chunk = wide_chunk
        self.small, self.s_pair, self.s_plane, self.s_z = small, s_pair, s_plane, s_z
        self.sems = sems
        self.half = mine.shape[0] // 2
        self.rows = self.half // geo.places
        self.columns = self.chunk_columns(geo)
        self.part = self.columns // geo.planes

    @staticmethod
    def chunk_columns(geo):
        return 128 * geo.planes

    @staticmethod
    def semaphores(geo, chunks):
        dma = pltpu.SemaphoreType.DMA
        places, planes, both = (chunks, geo.places), (chunks, geo.planes), (chunks, geo.places)
        shapes = dict(
            pair=(chunks,),
            plane=places,
            z=planes,
            zg=planes,
            pg=both,
            cg=both,
            sp=(1,),
            sn=(geo.places,),
            sz=(geo.planes,),
        )
        return list(shapes), [dma(s) for s in shapes.values() for _ in range(2)]

    def sem(self, name):
        names, _ = self.semaphores(self.geo, 1)
        i = names.index(name) * 2
        return self.sems[i], self.sems[i + 1]

    def where(self):
        z, k, n = self.geo.here()
        return z, k, n, (z * 2 + 1 - k, n)

    def others(self, here, count):
        return [lax.rem(here + i, count) for i in range(1, count)]

    def cols(self, c):
        return pl.ds(c * self.columns, self.columns)

    def place_rows(self, k, q):
        return pl.ds(pl.multiple_of(k * self.half + q * self.rows, 16), self.rows)

    def pair(self, c):
        z, k, n, sibling = self.where()
        send, recv = self.sem("pair")
        away = pl.ds(pl.multiple_of((1 - k) * self.half, 16), self.half)
        return remote(
            self.mine.at[away, self.cols(c)], self.got_pair.at[c], send.at[c], recv.at[c], sibling
        )

    def plane_copy(self, c, q):
        z, k, n, _ = self.where()
        send, recv = self.sem("plane")
        src = self.mine.at[self.place_rows(k, q), self.cols(c)]
        return remote(src, self.got_plane.at[c, n], send.at[c, q], recv.at[c, n], (z * 2 + k, q))

    def plane_start(self, c):
        z, k, n, _ = self.where()
        self.pair(c).wait()
        keep = pl.ds(pl.multiple_of(k * self.half, 16), self.half)
        total = self.mine[keep, self.cols(c)].astype(F32) + self.got_pair[c].astype(F32)
        self.mine[keep, self.cols(c)] = total.astype(BF)
        for q in self.others(n, self.geo.places):
            self.plane_copy(c, q).start()
        self.got_plane[c, n] = self.mine[self.place_rows(k, n), self.cols(c)]

    def z_copy(self, c, q):
        z, k, n, _ = self.where()
        send, recv = self.sem("z")
        return remote(
            self.piece.at[c, q], self.got_z.at[c, z], send.at[c, q], recv.at[c, z], (q * 2 + k, n)
        )

    def z_start(self, c):
        z, k, n, sibling = self.where()
        send, recv = self.sem("plane")
        for q in self.others(n, self.geo.places):
            spot = self.got_plane.at[c, q]
            remote(spot, spot, send.at[c, q], recv.at[c, q], sibling).wait_recv()
        total = self.got_plane[c, 0].astype(F32)
        for i in range(1, self.geo.places):
            total = total + self.got_plane[c, i].astype(F32)
        for p in range(self.geo.planes):
            self.piece[c, p] = total[:, p * self.part : (p + 1) * self.part].astype(BF)
        for q in self.others(z, self.geo.planes):
            self.z_copy(c, q).start()
        self.got_z[c, z] = self.piece[c, z]

    def spot(self, c, p):
        k, n = self.geo.here()[1:]
        first = pl.multiple_of(c * self.columns + p * self.part, 128)
        return self.whole.at[self.place_rows(k, n), pl.ds(first, self.part)]

    def zg_copy(self, c, q):
        z, k, n, _ = self.where()
        send, recv = self.sem("zg")
        spot = self.spot(c, z)
        return remote(spot, spot, send.at[c, q], recv.at[c, z], (q * 2 + k, n))

    def gather_z(self, c):
        z, k, n, sibling = self.where()
        send, recv = self.sem("z")
        for q in self.others(z, self.geo.planes):
            spot = self.got_z.at[c, q]
            remote(spot, spot, send.at[c, q], recv.at[c, q], sibling).wait_recv()
        total = self.got_z[c, 0].astype(F32)
        for i in range(1, self.geo.planes):
            total = total + self.got_z[c, i].astype(F32)
        first = pl.multiple_of(c * self.columns + z * self.part, 128)
        self.whole[self.place_rows(k, n), pl.ds(first, self.part)] = total.astype(BF)
        for q in self.others(z, self.geo.planes):
            self.zg_copy(c, q).start()

    def row_spot(self, c, k, q):
        return self.whole.at[self.place_rows(k, q), self.cols(c)]

    def pg_copy(self, c, q):
        z, k, n, _ = self.where()
        send, recv = self.sem("pg")
        spot = self.row_spot(c, k, n)
        return remote(spot, spot, send.at[c, q], recv.at[c, n], (z * 2 + k, q))

    def cg_copy(self, c, q):
        z, k, n, sibling = self.where()
        send, recv = self.sem("cg")
        spot = self.row_spot(c, k, q)
        return remote(spot, spot, send.at[c, q], recv.at[c, q], sibling)

    def gather_plane(self, c):
        z, k, n, sibling = self.where()
        send, recv = self.sem("zg")
        for q in self.others(z, self.geo.planes):
            spot = self.spot(c, q)
            remote(spot, spot, send.at[c, q], recv.at[c, q], sibling).wait_recv()
        for q in self.others(n, self.geo.places):
            self.pg_copy(c, q).start()
        self.cg_copy(c, n).start()

    def gather_pair(self, c):
        z, k, n, sibling = self.where()
        send, recv = self.sem("pg")
        for q in self.others(n, self.geo.places):
            spot = self.row_spot(c, k, q)
            remote(spot, spot, send.at[c, q], recv.at[c, q], sibling).wait_recv()
            self.cg_copy(c, q).start()

    def gather_end(self, c):
        z, k, n, sibling = self.where()
        send, recv = self.sem("cg")
        for q in range(self.geo.places):
            spot = self.row_spot(c, 1 - k, q)
            remote(spot, spot, send.at[c, q], recv.at[c, q], sibling).wait_recv()


    def half_part(self, p, c):
        k = self.geo.here()[1]
        first = pl.multiple_of(c * self.columns + p * self.part, 128)
        return pl.ds(pl.multiple_of(k * self.half, 16), self.half), pl.ds(first, self.part)

    def wide_z_copy(self, c, q):
        z, k, n, _ = self.where()
        send, recv = self.sem("z")
        src = self.mine.at[self.half_part(q, c)]
        return remote(src, self.wide_z.at[z], send.at[c, q], recv.at[c, z], (q * 2 + k, n))

    def wide_z_start(self, c):
        z, k, n, _ = self.where()
        self.pair(c).wait()
        keep = pl.ds(pl.multiple_of(k * self.half, 16), self.half)
        total = self.mine[keep, self.cols(c)].astype(F32) + self.got_pair[c].astype(F32)
        self.mine[keep, self.cols(c)] = total.astype(BF)
        for q in self.others(z, self.geo.planes):
            self.wide_z_copy(c, q).start()

    def wide_plane_copy(self, c, q):
        z, k, n, _ = self.where()
        send, recv = self.sem("plane")
        src = self.wide_sum.at[pl.ds(pl.multiple_of(q * self.rows, 16), self.rows)]
        return remote(src, self.wide_plane.at[n], send.at[c, q], recv.at[c, n], (z * 2 + k, q))

    def wide_plane_start(self, c):
        z, k, n, sibling = self.where()
        send, recv = self.sem("z")
        total = self.mine[self.half_part(z, c)].astype(F32)
        for q in self.others(z, self.geo.planes):
            spot = self.wide_z.at[q]
            remote(spot, spot, send.at[c, q], recv.at[c, q], sibling).wait_recv()
            total = total + self.wide_z[q].astype(F32)
        self.wide_sum[...] = total.astype(BF)
        for q in self.others(n, self.geo.places):
            self.wide_plane_copy(c, q).start()

    def wide_gather_plane(self, c):
        z, k, n, sibling = self.where()
        send, recv = self.sem("plane")
        here = pl.ds(pl.multiple_of(n * self.rows, 16), self.rows)
        total = self.wide_sum[here].astype(F32)
        for q in self.others(n, self.geo.places):
            spot = self.wide_plane.at[q]
            remote(spot, spot, send.at[c, q], recv.at[c, q], sibling).wait_recv()
            total = total + self.wide_plane[q].astype(F32)
        first = pl.multiple_of(c * self.columns + z * self.part, 128)
        self.whole[self.place_rows(k, n), pl.ds(first, self.part)] = total.astype(BF)
        for q in self.others(n, self.geo.places):
            self.wide_pg_copy(c, q).start()

    def wide_spot(self, c, q):
        z, k, n, _ = self.where()
        first = pl.multiple_of(c * self.columns + z * self.part, 128)
        return self.whole.at[self.place_rows(k, q), pl.ds(first, self.part)]

    def wide_pg_copy(self, c, q):
        z, k, n, _ = self.where()
        send, recv = self.sem("pg")
        spot = self.wide_spot(c, n)
        return remote(spot, spot, send.at[c, q], recv.at[c, n], (z * 2 + k, q))

    def wide_zg_copy(self, c, q):
        z, k, n, _ = self.where()
        send, recv = self.sem("zg")
        spot = self.whole.at[self.half_part(z, c)]
        return remote(spot, spot, send.at[c, q], recv.at[c, z], (q * 2 + k, n))

    def wide_gather_z(self, c):
        z, k, n, sibling = self.where()
        send, recv = self.sem("pg")
        for q in self.others(n, self.geo.places):
            spot = self.wide_spot(c, q)
            remote(spot, spot, send.at[c, q], recv.at[c, q], sibling).wait_recv()
        for q in self.others(z, self.geo.planes):
            self.wide_zg_copy(c, q).start()

    def wide_pair_copy(self, c):
        z, k, n, sibling = self.where()
        send, recv = self.sem("cg")
        half = pl.ds(pl.multiple_of(k * self.half, 16), self.half)
        spot = self.whole.at[half, self.cols(c)]
        return remote(spot, spot, send.at[c, 0], recv.at[c, 0], sibling)

    def wide_gather_pair(self, c):
        z, k, n, sibling = self.where()
        send, recv = self.sem("zg")
        for q in self.others(z, self.geo.planes):
            spot = self.whole.at[self.half_part(q, c)]
            remote(spot, spot, send.at[c, q], recv.at[c, q], sibling).wait_recv()
        self.wide_pair_copy(c).start()

    def wide_gather_end(self, c):
        z, k, n, sibling = self.where()
        send, recv = self.sem("cg")
        half = pl.ds(pl.multiple_of((1 - k) * self.half, 16), self.half)
        spot = self.whole.at[half, self.cols(c)]
        remote(spot, spot, send.at[c, 0], recv.at[c, 0], sibling).wait_recv()

    def stages(self, c):
        if c == self.wide_chunk:
            return (
                self.wide_z_start,
                self.wide_plane_start,
                self.wide_gather_plane,
                self.wide_gather_z,
                self.wide_gather_pair,
                self.wide_gather_end,
            )
        return (
            self.plane_start,
            self.z_start,
            self.gather_z,
            self.gather_plane,
            self.gather_pair,
            self.gather_end,
        )

    def small_pair(self):
        send, recv = self.sem("sp")
        return remote(self.small, self.s_pair, send.at[0], recv.at[0], self.where()[3])

    def sn_copy(self, q):
        z, k, n, _ = self.where()
        send, recv = self.sem("sn")
        return remote(self.s_plane.at[n], self.s_plane.at[n], send.at[q], recv.at[n], (z * 2 + k, q))

    def sz_copy(self, q):
        z, k, n, _ = self.where()
        send, recv = self.sem("sz")
        return remote(self.s_z.at[z], self.s_z.at[z], send.at[q], recv.at[z], (q * 2 + k, n))

    def small_plane(self):
        z, k, n, _ = self.where()
        self.small_pair().wait()
        self.s_plane[n] = self.small[...] + self.s_pair[...]
        for i in range(1, self.geo.places):
            self.sn_copy(lax.rem(n + i, self.geo.places)).start()

    def small_z(self):
        z, k, n, sibling = self.where()
        geo = self.geo
        send, recv = self.sem("sn")
        for i in range(1, geo.places):
            q = lax.rem(n + i, geo.places)
            spot = self.s_plane.at[q]
            remote(spot, spot, send.at[q], recv.at[q], sibling).wait_recv()
        total = self.s_plane[0]
        for i in range(1, geo.places):
            total = total + self.s_plane[i]
        self.s_z[z] = total
        for i in range(1, geo.planes):
            self.sz_copy(lax.rem(z + i, geo.planes)).start()

    def small_finish(self, out):
        z, k, n, sibling = self.where()
        geo = self.geo
        send, recv = self.sem("sz")
        for i in range(1, geo.planes):
            q = lax.rem(z + i, geo.planes)
            spot = self.s_z.at[q]
            remote(spot, spot, send.at[q], recv.at[q], sibling).wait_recv()
        total = self.s_z[0]
        for i in range(1, geo.planes):
            total = total + self.s_z[i]
        out[...] = total

    def wait_sent(self, chunks):
        z, k, n, _ = self.where()
        for q in self.others(n, self.geo.places):
            self.sn_copy(q).wait_send()
        for q in self.others(z, self.geo.planes):
            self.sz_copy(q).wait_send()
        for c in range(chunks):
            if c == self.wide_chunk:
                for q in self.others(n, self.geo.places):
                    self.wide_plane_copy(c, q).wait_send()
                    self.wide_pg_copy(c, q).wait_send()
                for q in self.others(z, self.geo.planes):
                    self.wide_z_copy(c, q).wait_send()
                    self.wide_zg_copy(c, q).wait_send()
                self.wide_pair_copy(c).wait_send()
                continue
            for q in self.others(n, self.geo.places):
                self.plane_copy(c, q).wait_send()
                self.pg_copy(c, q).wait_send()
            for q in self.others(z, self.geo.planes):
                self.z_copy(c, q).wait_send()
                self.zg_copy(c, q).wait_send()
            for q in range(self.geo.places):
                self.cg_copy(c, q).wait_send()


def greet_start(devices):
    barrier = pltpu.get_barrier_semaphore()
    for device in devices:
        pl.semaphore_signal(barrier, inc=1, device_id=device, device_id_type=MESH)


def all_devices(geo):
    z, k, n = geo.here()
    found = [(z * 2 + k, lax.rem(n + i, geo.places)) for i in range(1, geo.places)]
    found += [(z * 2 + 1 - k, lax.rem(n + i, geo.places)) for i in range(geo.places)]
    for i in range(1, geo.planes):
        other = lax.rem(z + i, geo.planes)
        found += [geo.partner(other * geo.plane_experts + j) for j in range(geo.plane_experts)]
    return found


def vector(ref, cols=slice(None)):
    return ref[...].astype(F32)[None, :][:, cols]


def lane_row(row, count):
    shape = (count, row.shape[1])
    diagonal = lax.broadcasted_iota(jnp.int32, shape, 0) == lax.broadcasted_iota(jnp.int32, shape, 1)
    return jnp.sum(jnp.where(diagonal, row, 0.0), axis=1, keepdims=True)


def row_of(column, lanes):
    shape = (column.shape[0], lanes)
    diagonal = lax.broadcasted_iota(jnp.int32, shape, 0) == lax.broadcasted_iota(jnp.int32, shape, 1)
    return jnp.sum(jnp.where(diagonal, column, 0.0), axis=0, keepdims=True)


def put_pair(rows, line, high, low):
    row = lax.broadcasted_iota(jnp.int32, rows.shape, 0)
    return jnp.where(row == line, high, jnp.where(row == line + 1, low, rows))


def block_kernel(geo, sizes, names, *refs):
    r = SimpleNamespace(**dict(zip(names, refs, strict=True)))
    rows, per_micro, seq, capacity, block, width, hidden = sizes
    experts = geo.partners
    slots = experts * block
    images = rows // seq
    z, k, n = geo.here()
    quad = geo.plane_experts
    chunk = quad * block
    part = r.w1.shape[2]
    tile = 256

    r.mine = r.hidden.at[0:width, 0 : 4 * width]
    r.grad_qkv = r.grad_pre.at[0:rows, 0 : 3 * width]
    r.grad_branch = r.grad_pre.at[rows : 2 * rows, 0:width]
    r.grad_att = r.grad_pre.at[rows : 2 * rows, width : 2 * width]
    r.logits_high = r.grad_pre.at[0:rows, 4 * width - 256 : 4 * width - 128]
    r.logits_low = r.grad_pre.at[0:rows, 4 * width - 128 : 4 * width]
    lanes = -(-rows // 128) * 128
    r.late_table = r.grad_pre.at[:, 0:lanes]
    r.late_table0 = r.grad_pre.at[:, lanes : 2 * lanes]
    head = -(-(capacity + 2) // 16) * 16
    rest = block - head
    heads = experts * head
    gate_group, gate_line = capacity // 16 * 16, capacity % 16
    r.slot_grad = r.grad_pre.at[:, 3 * width : 3 * width + 256]

    def span(i, count, align=16):
        return pl.ds(pl.multiple_of(i * count, align), count)

    def sems(name):
        return [ref for key, ref in zip(names, refs, strict=True) if key.startswith(name)]

    greet_start(all_devices(geo))
    arrive = [
        pltpu.make_async_copy(src, dst, r.in_sem.at[i])
        for i, (src, dst) in enumerate(
            (
                (r.given_cot, r.cot),
                (r.given_tokens, r.tokens),
                (r.given_w_qkv, r.w_qkv),
                (r.given_w_out, r.w_out),
            )
        )
    ]
    for copy in arrive:
        copy.start()
    weights = Weights(
        geo, (r.w1, r.w2), (r.first, r.second), r.tile, r.tiles, sems("weights_sem")
    )
    cot_swap = Swap(geo, block, r.send_a, r.cot_got, sems("cot_sem"))
    x_swap = Swap(geo, block, r.send_b, r.x_got, sems("x_sem"))
    grad_swap, late_grad_swap = (
        Swap(geo, block, r.send_a, r.grad_got, sems("head_grad_sem"), 0, head, 0),
        Swap(geo, block, r.send_a, r.grad_got, sems("rest_grad_sem"), head, rest, heads),
    )
    ret_swap, late_ret_swap = (
        Swap(geo, block, r.send_b, r.ret_got, sems("head_ret_sem"), 0, head, 0),
        Swap(geo, block, r.send_b, r.ret_got, sems("rest_ret_sem"), head, rest, heads),
    )

    r.ids[...] = jnp.zeros(r.ids.shape, F32)
    for m in range(rows // per_micro):
        r.ids[0:2, m * per_micro : (m + 1) * per_micro] = r.choices[m].astype(F32)
    lines = lax.broadcasted_iota(jnp.int32, (experts, rows), 0).astype(F32)
    named = [lines == r.ids[i : i + 1, 0:rows] for i in range(2)]
    either = jnp.logical_or(named[0], named[1])
    first_row = lax.broadcasted_iota(jnp.int32, (rows, rows), 0)
    second_row = lax.broadcasted_iota(jnp.int32, (rows, rows), 1)
    same = (first_row >= per_micro) == (second_row >= per_micro)
    earlier = jnp.logical_and(first_row < second_row, same)
    before = dot(either.astype(F32).astype(BF), earlier.astype(F32).astype(BF))
    late = lax.broadcasted_iota(jnp.int32, (experts, rows), 1) >= per_micro
    slot = before + jnp.where(late, float(capacity + 2), 0.0)
    r.held[...] = jnp.full(r.held.shape, -1.0, F32)
    r.held[0, :, 0:rows] = jnp.where(either, slot, -1.0)
    r.held[1, :, 0:rows] = jnp.where(named[0], slot, -1.0)
    spots = lax.broadcasted_iota(jnp.int32, (block, lanes), 0).astype(F32)

    def fill(e):
        either = jnp.where(spots == r.held[0, pl.ds(e, 1), :], 1.0, 0.0).astype(BF)
        r.table[span(e, block), :] = either[:, 0:rows]

    def late_fill(e):
        for i, table in enumerate((r.late_table, r.late_table0)):
            found = jnp.where(spots == r.held[i, pl.ds(e, 1), :], 1.0, 0.0).astype(BF)
            table[span(e, head), :] = found[0:head]
            table[pl.ds(pl.multiple_of(heads + e * rest, 16), rest), :] = found[head:]

    def send_cot(i):
        plane = lax.rem(z + 1 + i, geo.planes)
        for j in range(quad):
            fill(plane * quad + j)

        @pl.when(i == 0)
        def _():
            arrive[0].wait()
            pl.semaphore_wait(pltpu.get_barrier_semaphore(), len(all_devices(geo)))

        blocks = dot(r.table[span(plane, chunk), :], r.cot[...])
        r.send_a[span(plane, chunk), :] = blocks.astype(BF)
        for j in range(quad):
            cot_swap.send(plane * quad + j)

    each(geo.planes, send_cot)
    r.table[pl.ds(slots, 128), :] = jnp.zeros((128, rows), BF)
    for i in range(geo.local_experts):
        r.tile[i] = jnp.zeros((8, width), F32)
        r.tile[i, 0:1, 0:part] = r.b1[i : i + 1, :].astype(F32)
        r.tile[i, 1:2, :] = r.b2[i : i + 1, :].astype(F32)
    weights.start()

    def norm_in(i):
        unit, _ = norm_parts(r.tokens[span(i, seq), :].astype(F32))
        normed = unit * vector(r.gain1) + vector(r.shift1)
        r.normed[span(i, seq), :] = normed.astype(BF)

    arrive[1].wait()
    each(images, norm_in)
    arrive[2].wait()
    for c in range(3 * width // tile):
        cols = slice(c * tile, (c + 1) * tile)
        out = dot(r.normed[...], r.w_qkv[:, cols])
        if c * tile < width:
            out = out + vector(r.bias_q, cols)
        elif c * tile >= 2 * width:
            out = out + vector(r.bias_v, slice(c * tile - 2 * width, (c + 1) * tile - 2 * width))
        r.qkv[:, cols] = out.astype(BF)

    def attend(i):
        here = span(i, seq)
        length = r.lengths[i // (per_micro // seq), i % (per_micro // seq)]
        r.attended[here, :] = attend_image(
            r.qkv[here, 0:width],
            r.qkv[here, width : 2 * width],
            r.qkv[here, 2 * width : 3 * width],
            length,
        )

    each(images, attend)

    def branch(i):
        here = span(i, seq)
        residual = (
            r.tokens[here, :].astype(F32)
            + dot(r.attended[here, :], r.w_out[...])
            + vector(r.bias_out)
        )
        r.residual[here, :] = residual
        unit, _ = norm_parts(residual)
        expert_in = (unit * vector(r.gain2) + vector(r.shift2)).astype(BF)
        r.expert_in[here, :] = expert_in
        logits = dot_nt(expert_in, r.w_router[...])
        raised = jnp.exp(logits - jnp.max(logits, axis=-1, keepdims=True))
        probs = raised / jnp.sum(raised, axis=-1, keepdims=True)
        r.probs[here, 0:experts] = probs

    r.probs[...] = jnp.zeros(r.probs.shape, F32)
    arrive[3].wait()
    each(images, branch)
    probs_t = jnp.transpose(r.probs[...])[0:experts, :]
    high, low = split_two(probs_t)
    r.probs_t[0:experts, :] = high
    r.probs_t[experts : 2 * experts, :] = low

    def send_x(i):
        plane = lax.rem(z + 1 + i, geo.planes)
        blocks = dot(r.table[span(plane, chunk), :], r.expert_in[...])
        for j in range(quad):
            e = plane * quad + j
            at = e * block
            values = blocks[j * block : (j + 1) * block]
            gates = dot_nt(r.probs_t[...], r.table[pl.ds(pl.multiple_of(at, 16), 128), :])
            line = lax.broadcasted_iota(jnp.int32, gates.shape, 0)
            high = jnp.sum(jnp.where(line == e, gates, 0.0), axis=0, keepdims=True)
            low = jnp.sum(jnp.where(line == experts + e, gates, 0.0), axis=0, keepdims=True)
            r.send_b[span(e, block), :] = values.astype(BF)
            group = put_pair(values[gate_group : gate_group + 16, 0:128], gate_line, high, low)
            r.send_b[pl.ds(pl.multiple_of(at + gate_group, 16), 16), 0:128] = group.astype(BF)
            x_swap.send(e)

    each(geo.planes, send_x)

    r.ids_t[...] = jnp.transpose(r.ids[...])
    each(experts, late_fill)
    r.table_t[...] = jnp.transpose(r.late_table[...])[0:rows, :]
    r.table0_t[...] = jnp.transpose(r.late_table0[...])[0:rows, :]
    weights.relay()
    weights.finish()
    for s in range(geo.places):
        r.bias1[:, s * part : (s + 1) * part] = jnp.broadcast_to(r.tiles[s, 0:1, 0:part], (8, part))
    cot_swap.wait_sent()
    x_swap.wait_sent()

    root = 0.7978845608028654
    r.sum_pre[...] = jnp.zeros(r.sum_pre.shape, F32)
    r.sum_ret[...] = jnp.zeros(r.sum_ret.shape, F32)

    def expert_chunk(i):
        plane = lax.rem(z + i, geo.planes)
        here = span(plane, chunk)
        for j in range(quad):
            cot_swap.wait_got(plane * quad + j)
        for j in range(quad):
            x_swap.wait_got(plane * quad + j)
        for j in range(quad):
            at = (plane * quad + j) * block
            group = r.x_got[pl.ds(pl.multiple_of(at + gate_group, 16), 16), 0:128].astype(F32)
            gate = lane_row(group[gate_line : gate_line + 1] + group[gate_line + 1 : gate_line + 2], block)
            there = span(plane * quad + j, block)
            r.grad_ret[there, :] = (gate * r.cot_got[there, :].astype(F32)).astype(BF)
        total_ret = jnp.sum(r.grad_ret[here, :].astype(F32), axis=0, keepdims=True)
        r.sum_ret[0:1, :] = r.sum_ret[0:1, :] + total_ret
        for c in range(hidden // tile):
            cols = slice(c * tile, (c + 1) * tile)
            pre = dot(r.x_got[here, :], r.first[:, cols]) + r.bias1[0:1, cols]
            square = pre * pre
            bend = jnp.tanh(root * pre * (1.0 + 0.044715 * square))
            half = 0.5 * (1.0 + bend)
            r.hidden[here, cols] = (pre * half).astype(BF)
            slope = half + 0.5 * pre * (1.0 - bend * bend) * (root + 3 * 0.044715 * root * square)
            back = dot_nt(r.grad_ret[here, :], r.second[cols, :])
            grad_pre = (back * slope).astype(BF)
            r.grad_pre[here, cols] = grad_pre
            total = jnp.sum(grad_pre.astype(F32), axis=0, keepdims=True)
            r.sum_pre[0:1, cols] = r.sum_pre[0:1, cols] + total
        returned = dot(r.hidden[here, :], r.second[...]) + r.tiles[0, 1:2, :]
        r.send_b[here, :] = returned.astype(BF)
        grad_in = dot_nt(r.grad_pre[here, :], r.first[...])
        for j in range(quad):
            e = plane * quad + j
            there = span(e, block)
            product = r.cot_got[there, :].astype(F32) * r.send_b[there, :].astype(F32)
            high, low = split_two(row_of(jnp.sum(product, axis=-1, keepdims=True), 128))
            values = grad_in[j * block : (j + 1) * block]
            r.send_a[there, :] = values.astype(BF)
            group = values[gate_group : gate_group + 16, 0:128]
            group = put_pair(group, gate_line, high.astype(F32), low.astype(F32))
            at = pl.ds(pl.multiple_of(e * block + gate_group, 16), 16)
            r.send_a[at, 0:128] = group.astype(BF)
            grad_swap.send(e)

    each(geo.planes, expert_chunk)
    for swap in (late_grad_swap, ret_swap, late_ret_swap):
        each(experts, lambda i: swap.send(lax.rem(geo.mine() + 1 + i, experts)))

    grads = ExpertGrads(
        geo,
        r.d_experts,
        r.d_got,
        r.d_tiles,
        r.d_got_tiles,
        r.inbox,
        r.inbox_tiles,
        sems("expert_sem"),
    )
    quarter = hidden // 4

    def weight_grads(side):
        for layer, left, right in ((0, r.x_got, r.grad_pre), (1, r.grad_ret, r.hidden)):
            for c in range(2):
                cols = pl.ds(pl.multiple_of(side * (hidden // 2) + c * quarter, 128), quarter)
                r.d_experts[layer, :, cols] = dot_tn(left[...], right[:, cols]).astype(BF)

    weight_grads(1 - k)
    grads.pair(0).start()
    grads.pair(1).start()
    r.d_tiles[...] = jnp.zeros(r.d_tiles.shape, F32)
    for s in range(geo.places):
        r.d_tiles[s, 0:1, 0:part] = r.sum_pre[0:1, s * part : (s + 1) * part]
        r.d_tiles[s, 1:2, :] = r.sum_ret[0:1, :]
    grads.pair_tiles().start()
    weight_grads(k)
    grads.forward()

    dense = DenseSum(
        geo,
        r.mine,
        r.got_pair,
        r.got_plane,
        r.piece,
        r.got_z,
        r.wide_z,
        r.wide_sum,
        r.wide_plane,
        r.whole,
        r.small,
        r.s_pair,
        r.s_plane,
        r.s_z,
        sems("dense_sem"),
        4 * width // (128 * geo.planes) - (2 if 128 * geo.planes == width else 1),
    )

    def slot_grads(e):
        grad_swap.wait_got(e)
        at = pl.ds(pl.multiple_of(e * head + gate_group, 16), 16)
        group = r.grad_got[at, 0:128].astype(F32)
        column = lane_row(group[gate_line : gate_line + 1] + group[gate_line + 1 : gate_line + 2], block)
        lane = lax.broadcasted_iota(jnp.int32, (block, 128), 1)
        late = pl.ds(pl.multiple_of(heads + e * rest, 16), rest)
        for i, value in enumerate(split_two(jnp.where(lane == e, column, 0.0))):
            cols = slice(i * 128, (i + 1) * 128)
            r.slot_grad[span(e, head), cols] = value[0:head]
            r.slot_grad[late, cols] = value[head:]

    def combine(m):
        here = slice(m * per_micro, (m + 1) * per_micro)
        there = slice(0, heads if m == 0 else slots)
        for c in range(width // tile):
            cols = slice(c * tile, (c + 1) * tile)
            r.grad_two[here, cols] = dot(r.table_t[here, there], r.grad_got[there, cols])
        both = dot(r.table_t[here, there], r.slot_grad[there, :])
        r.grad_choice[here, :] = both[:, 0:128] + both[:, 128:256]

    r.small[...] = jnp.zeros(r.small.shape, F32)

    def add_small(row, value):
        r.small[row : row + 1, :] = r.small[row : row + 1, :] + jnp.sum(value, axis=0, keepdims=True)

    def norm_two_back(i):
        here = span(i, seq)
        probs = r.probs[here, :]
        choice = r.grad_choice[here, :]
        logits = probs * (choice - jnp.sum(probs * choice, axis=-1, keepdims=True))
        high, low = split_two(logits)
        r.logits_high[here, :] = high
        r.logits_low[here, :] = low
        weight = r.w_router[...]
        grad = r.grad_two[here, :]
        grad = grad + dot(high[:, 0:experts], weight) + dot(low[:, 0:experts], weight)
        unit, scale = norm_parts(r.residual[here, :])
        add_small(5, grad * unit)
        add_small(6, grad)
        grad = r.cot[here, :].astype(F32) + norm_back(grad, unit, scale, vector(r.gain2))
        r.grad_two[here, :] = grad
        low_grad = grad.astype(BF)
        r.grad_branch[here, :] = low_grad
        add_small(4, low_grad.astype(F32))

    columns = dense.columns
    chunks = 4 * width // columns
    stages = dense.stages(chunks - 1)

    def dense_grad(first):
        cols = pl.ds(first, tile)
        if first < 3 * width:
            out = dot_tn(r.normed[...], r.grad_qkv[:, cols])
        else:
            out = dot_tn(r.attended[...], r.grad_branch[:, pl.ds(first - 3 * width, tile)])
        r.mine[:, cols] = out.astype(BF)

    early = columns == width

    def attend_grad(m):
        here = slice(m * per_micro, (m + 1) * per_micro)
        for c in range(width // tile):
            cols = slice(c * tile, (c + 1) * tile)
            r.grad_att[here, cols] = dot_nt(r.grad_branch[here, :], r.w_out[cols, :]).astype(BF)

    def attend_back(i):
        here = span(i, seq)
        length = r.lengths[i // (per_micro // seq), i % (per_micro // seq)]
        parts = attend_image_back(
            r.qkv[here, 0:width],
            r.qkv[here, width : 2 * width],
            r.qkv[here, 2 * width : 3 * width],
            length,
            r.grad_att[here, :],
        )
        for c, value in enumerate(parts):
            r.grad_qkv[here, c * width : (c + 1) * width] = value
        add_small(2, parts[0].astype(F32))
        add_small(3, parts[2].astype(F32))

    def norm_one_back(i):
        here = span(i, seq)
        grad = dot_nt(r.grad_qkv[here, :], r.w_qkv[...])
        unit, scale = norm_parts(r.tokens[here, :].astype(F32))
        add_small(0, grad * unit)
        add_small(1, grad)
        r.grad_two[here, :] = r.grad_two[here, :] + norm_back(
            grad, unit, scale, vector(r.gain1)
        )

    def mix(i):
        here = span(i, seq)
        total = dot(r.table_t[here, :], r.ret_got[...])
        chosen = dot(r.table0_t[here, :], r.ret_got[...])
        probs = r.probs[here, :]
        lane = lax.broadcasted_iota(jnp.int32, probs.shape, 1).astype(F32)
        gates = [
            jnp.sum(jnp.where(lane == r.ids_t[here, j : j + 1], probs, 0.0), axis=-1, keepdims=True)
            for j in range(2)
        ]
        mixed = r.residual[here, :] + gates[0] * chosen + gates[1] * (total - chosen)
        r.expert_in[here, :] = mixed.astype(BF)

    def some(step, m):
        count = images * per_micro // rows
        each(count, lambda i: step(m * count + i))

    micros = rows // per_micro
    each(experts, slot_grads)
    for m in range(micros):
        if m == 1:
            each(experts, late_grad_swap.wait_got)
        combine(m)
        some(norm_two_back, m)
        if m == micros - 1 and early:
            for first in range(3 * width, 4 * width, tile):
                dense_grad(first)
            dense.pair(chunks - 1).start()
        attend_grad(m)
        if m == micros - 1 and early:
            stages[0](chunks - 1)
        some(attend_back, m)
        if m < micros - 1:
            some(norm_one_back, m)
    router = dot_tn(r.logits_high[...], r.expert_in[...]) + dot_tn(r.logits_low[...], r.expert_in[...])
    r.small[8 : 8 + experts, :] = router[0:experts, :]
    late = chunks - 1 if early else chunks
    done = 1 if early else 0
    tokens_copy = pltpu.make_async_copy(r.grad_two, r.grad_tokens, r.out_sem.at[1])
    mixed_copy = pltpu.make_async_copy(r.expert_in, r.mixed, r.out_sem.at[0])
    layers_copy = pltpu.make_async_copy(r.inbox, r.d_layers, r.out_sem.at[2])
    bias_copy = pltpu.make_async_copy(r.inbox_tiles, r.d_bias, r.out_sem.at[3])

    def tokens_done():
        tokens_copy.start()
        dense.small_pair().start()

    def owner_done():
        grads.wait_got()
        layers_copy.start()
        bias_copy.start()

    beside = [functools.partial(norm_one_back, i) for i in range((micros - 1) * images // micros, images)]
    beside += [tokens_done, dense.small_plane, dense.small_z]
    beside += [lambda: each(experts, ret_swap.wait_got), lambda: each(experts, late_ret_swap.wait_got)]
    beside += [functools.partial(mix, i) for i in range(images)]
    beside += [mixed_copy.start, lambda: dense.small_finish(r.small_out), owner_done]
    for c in range(late):
        for first in range(c * columns, (c + 1) * columns, tile):
            dense_grad(first)
        dense.pair(c).start()
    for stage in range(len(stages)):
        for c in range(late):
            dense.stages(c)[stage](c)
        if early and done + stage < len(stages):
            stages[done + stage](chunks - 1)
        for step in beside[:4]:
            step()
        beside = beside[4:]
    for step in beside:
        step()
    big_copy = pltpu.make_async_copy(r.whole, r.big_out, r.out_sem.at[4])
    big_copy.start()
    for swap in (grad_swap, late_grad_swap, ret_swap, late_ret_swap):
        swap.wait_sent()
    weights.wait_sent()
    grads.wait_sent()
    dense.wait_sent(chunks)
    for copy in (mixed_copy, tokens_copy, layers_copy, bias_copy, big_copy):
        copy.wait()


def finish_kernel(names, *refs):
    r = SimpleNamespace(**dict(zip(names, refs, strict=True)))
    width, part = r.w_out.shape[0], r.w1.shape[2]
    local, group = r.g_d_layers.shape[1:3]
    come_big = pltpu.make_async_copy(r.g_big_out, r.v_big, r.sem.at[0])
    come_layers = pltpu.make_async_copy(r.g_d_layers, r.v_layers, r.sem.at[1])
    come_tokens = pltpu.make_async_copy(r.g_grad_tokens, r.v_tokens, r.sem.at[2])
    come_mixed = pltpu.make_async_copy(r.g_mixed, r.v_mixed, r.sem.at[3])
    copies = []
    for copy in (come_big, come_layers, come_tokens, come_mixed):
        copy.start()
    vectors = dict(gain1=0, shift1=1, bias_q=2, bias_v=3, bias_out=4, gain2=5, shift2=6)
    for name, line in vectors.items():
        getattr(r, name)[...] = r.g_small_out[line]
    r.router[...] = r.g_small_out[8:, :]
    tiles = r.g_d_bias[:, 0]
    for g in range(1, group):
        tiles = tiles + r.g_d_bias[:, g]
    r.b1[...] = tiles[:, 0, 0:part]
    r.b2[...] = tiles[:, 1, :]

    def leave(src, dst, sem):
        copy = pltpu.make_async_copy(src, dst, sem)
        copy.start()
        copies.append(copy)

    come_big.wait()
    for i, (out, first) in enumerate(((r.w_qkv, 0), (r.w_out, 3 * width))):
        cols = slice(first, first + out.shape[1])
        r.o_big[:, cols] = r.v_big[:, cols].astype(F32)
        leave(r.o_big.at[:, cols], out, r.sem.at[4 + i])
    come_tokens.wait()
    leave(r.v_tokens, r.grad_tokens, r.sem.at[2])
    come_mixed.wait()
    leave(r.v_mixed, r.mixed, r.sem.at[3])
    come_layers.wait()
    for i in range(local):
        for layer in range(2):
            total = r.v_layers[layer, i, 0].astype(F32)
            for g in range(1, group):
                total = total + r.v_layers[layer, i, g].astype(F32)
            if layer == 0:
                r.o_first[i] = total
                leave(r.o_first.at[i], r.w1.at[i], r.sem.at[6 + 2 * i])
            else:
                r.o_second[i] = jnp.transpose(total)
                leave(r.o_second.at[i], r.w2.at[i], r.sem.at[7 + 2 * i])
    for copy in copies:
        copy.wait()


def on_device(
    geo,
    tokens,
    image_lengths,
    expert_index,
    grad_out,
    ln1_gain,
    ln1_bias,
    w_qkv,
    bias_query,
    bias_value,
    w_out,
    bias_out,
    ln2_gain,
    ln2_bias,
    w_router,
    experts_in,
    experts_in_bias,
    experts_out,
    experts_out_bias,
):
    micros, per_micro, width = tokens.shape
    rows = micros * per_micro
    seq = per_micro // image_lengths.shape[1]
    experts = geo.partners
    capacity = (per_micro * 42 + 20 * experts - 1) // (20 * experts)
    block = -(-(micros * capacity + 2) // 16) * 16
    slots = experts * block
    part = experts_in.shape[2]
    hidden = part * geo.places
    places, planes, local, group = geo.places, geo.planes, geo.local_experts, geo.group
    inputs = dict(
        given_tokens=tokens.reshape(rows, width),
        given_cot=grad_out.reshape(rows, width),
        choices=jnp.swapaxes(expert_index, 1, 2),
        lengths=image_lengths,
        gain1=ln1_gain,
        shift1=ln1_bias,
        given_w_qkv=w_qkv,
        bias_q=bias_query,
        bias_v=bias_value,
        given_w_out=w_out,
        bias_out=bias_out,
        gain2=ln2_gain,
        shift2=ln2_bias,
        w_router=w_router.T,
        w1=experts_in,
        b1=experts_in_bias,
        w2=experts_out,
        b2=experts_out_bias,
    )
    vmem, smem = pl.BlockSpec(memory_space=pltpu.VMEM), pl.BlockSpec(memory_space=pltpu.SMEM)
    anywhere = pl.BlockSpec(memory_space=pl.ANY)
    in_specs = {name: vmem for name in inputs}
    in_specs.update(lengths=smem, w1=anywhere, w2=anywhere)
    in_specs.update({name: anywhere for name in inputs if name.startswith("given")})
    small_rows = 8 + experts
    outputs = dict(
        mixed=((rows, width), BF, anywhere),
        grad_tokens=((rows, width), F32, anywhere),
        big_out=((width, 4 * width), BF, anywhere),
        small_out=((small_rows, width), F32, vmem),
        d_layers=((2, local, group, width, part), BF, anywhere),
        d_bias=((local, group, 8, width), F32, anywhere),
    )
    half = width // 2
    columns = DenseSum.chunk_columns(geo)
    chunks = 4 * width // columns
    scratch = dict(
        tokens=((rows, width), BF),
        cot=((rows, width), BF),
        w_qkv=((width, 3 * width), BF),
        w_out=((width, width), BF),
        tile=((local, 8, width), F32),
        tiles=((places, 8, width), F32),
        first=((width, hidden), BF),
        second=((hidden, width), BF),
        bias1=((8, hidden), F32),
        ids=((8, -(-rows // 128) * 128), F32),
        ids_t=((-(-rows // 128) * 128, 8), F32),
        held=((2, experts, -(-rows // 128) * 128), F32),
        table=((slots + 128, rows), BF),
        table_t=((rows, slots), BF),
        table0_t=((rows, slots), BF),
        send_a=((slots, width), BF),
        send_b=((slots, width), BF),
        cot_got=((slots, width), BF),
        x_got=((slots, width), BF),
        grad_got=((slots, width), BF),
        ret_got=((slots, width), BF),
        normed=((rows, width), BF),
        qkv=((rows, 3 * width), BF),
        attended=((rows, width), BF),
        residual=((rows, width), F32),
        expert_in=((rows, width), BF),
        probs=((rows, 128), F32),
        probs_t=((2 * experts, rows), BF),
        grad_ret=((slots, width), BF),
        hidden=((slots, hidden), BF),
        grad_pre=((slots, hidden), BF),
        sum_pre=((8, hidden), F32),
        sum_ret=((8, width), F32),
        d_experts=((2, width, hidden), BF),
        d_got=((2, width, hidden // 2), BF),
        d_tiles=((places, 8, width), F32),
        d_got_tiles=((places, 8, width), F32),
        inbox=((2, local, group, width, part), BF),
        inbox_tiles=((local, group, 8, width), F32),
        grad_two=((rows, width), F32),
        grad_choice=((rows, 128), F32),
        got_pair=((chunks, half, columns), BF),
        got_plane=((chunks, places, half // places, columns), BF),
        piece=((chunks, planes, half // places, 128), BF),
        got_z=((chunks, planes, half // places, 128), BF),
        wide_z=((planes, half, 128), BF),
        wide_sum=((half, 128), BF),
        wide_plane=((places, half // places, 128), BF),
        whole=((width, 4 * width), BF),
        small=((small_rows, width), F32),
        s_pair=((small_rows, width), F32),
        s_plane=((places, small_rows, width), F32),
        s_z=((planes, small_rows, width), F32),
    )
    sem_sets = dict(
        weights_sem=Weights.sems(geo),
        cot_sem=swap_sems(geo),
        x_sem=swap_sems(geo),
        head_grad_sem=swap_sems(geo),
        rest_grad_sem=swap_sems(geo),
        head_ret_sem=swap_sems(geo),
        rest_ret_sem=swap_sems(geo),
        expert_sem=ExpertGrads.sems(geo),
        dense_sem=DenseSum.semaphores(geo, chunks)[1],
    )
    sem_names = [name + str(i) for name, found in sem_sets.items() for i in range(len(found))]
    sem_shapes = [s for found in sem_sets.values() for s in found]
    names = [*inputs, *outputs, *scratch, *sem_names, "out_sem", "in_sem"]
    sizes = (rows, per_micro, seq, capacity, block, width, hidden)
    results = pl.pallas_call(
        functools.partial(block_kernel, geo, sizes, names),
        out_shape=[jax.ShapeDtypeStruct(shape, dtype) for shape, dtype, _ in outputs.values()],
        in_specs=list(in_specs.values()),
        out_specs=[spec for _, _, spec in outputs.values()],
        scratch_shapes=[pltpu.VMEM(shape, dtype) for shape, dtype in scratch.values()]
        + sem_shapes
        + [pltpu.SemaphoreType.DMA((5,)), pltpu.SemaphoreType.DMA((4,))],
        compiler_params=pltpu.CompilerParams(
            collective_id=0, has_side_effects=True, vmem_limit_bytes=VMEM_LIMIT
        ),
    )(*inputs.values())
    out = dict(zip(outputs, results, strict=True))
    shapes = dict(
        mixed=((rows, width), BF, anywhere),
        grad_tokens=((rows, width), F32, anywhere),
        gain1=((width,), F32, vmem),
        shift1=((width,), F32, vmem),
        w_qkv=((width, 3 * width), F32, anywhere),
        bias_q=((width,), F32, vmem),
        bias_v=((width,), F32, vmem),
        w_out=((width, width), F32, anywhere),
        bias_out=((width,), F32, vmem),
        gain2=((width,), F32, vmem),
        shift2=((width,), F32, vmem),
        router=((experts, width), F32, vmem),
        w1=((local, width, part), F32, anywhere),
        b1=((local, part), F32, vmem),
        w2=((local, part, width), F32, anywhere),
        b2=((local, width), F32, vmem),
    )
    room = dict(
        v_big=((width, 4 * width), BF),
        v_layers=((2, local, group, width, part), BF),
        v_tokens=((rows, width), F32),
        v_mixed=((rows, width), BF),
        o_big=((width, 4 * width), F32),
        o_first=((local, width, part), F32),
        o_second=((local, part, width), F32),
    )
    given = ["g_" + name for name in outputs]
    made = pl.pallas_call(
        functools.partial(finish_kernel, [*given, *shapes, *room, "sem"]),
        out_shape=[jax.ShapeDtypeStruct(shape, dtype) for shape, dtype, _ in shapes.values()],
        in_specs=[vmem if name == "d_bias" else spec for name, (_, _, spec) in outputs.items()],
        out_specs=[spec for _, _, spec in shapes.values()],
        scratch_shapes=[pltpu.VMEM(shape, dtype) for shape, dtype in room.values()]
        + [pltpu.SemaphoreType.DMA((6 + 2 * local,))],
        compiler_params=pltpu.CompilerParams(vmem_limit_bytes=VMEM_LIMIT),
    )(*results)
    made = dict(zip(shapes, made, strict=True))
    made.update(
        mixed=made["mixed"].reshape(tokens.shape),
        grad_tokens=made["grad_tokens"].reshape(tokens.shape),
        router=made["router"].T,
    )
    return tuple(made.values())


def solution(mesh):
    split = ("wide", "narrow")
    in_specs = (
        P(None, split, None),
        P(None, split),
        P(None, split, None),
        P(None, split, None),
        *([P()] * 10),
        P("wide", None, "narrow"),
        P("wide", "narrow"),
        P("wide", "narrow", None),
        P("wide", None),
    )
    out_specs = (
        P(None, split, None),
        P(None, split, None),
        *([P()] * 10),
        P("wide", None, "narrow"),
        P("wide", "narrow"),
        P("wide", "narrow", None),
        P("wide", None),
    )

    def step(*args):
        geo = Geometry(mesh.shape["wide"], mesh.shape["narrow"], args[14].shape[0])
        return on_device(geo, *args)

    return jax.shard_map(step, mesh=mesh, in_specs=in_specs, out_specs=out_specs, check_vma=False)
```

```python
import functools
from types import SimpleNamespace

import jax
import jax.numpy as jnp
from jax import lax
from jax.experimental import pallas as pl
from jax.experimental.pallas import tpu as pltpu
from jax.sharding import PartitionSpec as P

HEADS = 8
HEAD_DIM = 64
MESH = pl.DeviceIdType.MESH
BF = jnp.bfloat16
F32 = jnp.float32
VMEM_LIMIT = 62 * 2**20


def dot(a, b):
    return lax.dot_general(a, b, (((1,), (0,)), ((), ())), preferred_element_type=F32)


def dot_nt(a, b):
    return lax.dot_general(a, b, (((1,), (1,)), ((), ())), preferred_element_type=F32)


def dot_tn(a, b):
    return lax.dot_general(a, b, (((0,), (0,)), ((), ())), preferred_element_type=F32)


class Geometry:
    def __init__(self, n_wide, n_narrow, local_experts):
        self.planes = n_wide // 2
        self.places = n_narrow
        self.local_experts = local_experts
        self.plane_experts = 2 * local_experts
        self.group = n_narrow // self.plane_experts
        self.partners = self.planes * self.plane_experts

    def here(self):
        wide, place = lax.axis_index("wide"), lax.axis_index("narrow")
        return wide // 2, wide % 2, place

    def mine(self):
        z, _, n = self.here()
        return z * self.plane_experts + n // self.group

    def partner(self, p):
        _, k, n = self.here()
        place = (p % self.plane_experts) * self.group + n % self.group
        return ((p // self.plane_experts) * 2 + k, place)


def remote(src, dst, send_sem, recv_sem, device):
    return pltpu.make_async_remote_copy(
        src_ref=src,
        dst_ref=dst,
        send_sem=send_sem,
        recv_sem=recv_sem,
        device_id=device,
        device_id_type=MESH,
    )


def norm_parts(values):
    centred = values - jnp.mean(values, axis=-1, keepdims=True)
    scale = lax.rsqrt(jnp.mean(centred * centred, axis=-1, keepdims=True) + 1e-06)
    return centred * scale, scale


def norm_back(grad, unit, scale, gain):
    pulled = grad * gain
    inner = jnp.mean(pulled, axis=-1, keepdims=True)
    along = jnp.mean(pulled * unit, axis=-1, keepdims=True)
    return scale * (pulled - inner - unit * along)


def head_pair(rows, low):
    zero = jnp.zeros_like(rows)
    return jnp.concatenate([jnp.where(low, rows, zero), jnp.where(low, zero, rows)], axis=0)


def pair_probs(stacked, keys, length):
    scores = dot_nt(keys, stacked) * HEAD_DIM ** (-0.5)
    visible = lax.broadcasted_iota(jnp.int32, scores.shape, 0) < length
    scores = jnp.where(visible, scores, -1e30)
    raised = jnp.exp(scores - jnp.max(scores, axis=0, keepdims=True))
    return raised * (1.0 / jnp.sum(raised, axis=0, keepdims=True))


def attend_image(queries, keys, values, length):
    seq = queries.shape[0]
    low = lax.broadcasted_iota(jnp.int32, (seq, 128), 1) < HEAD_DIM
    parts = []
    for g in range(queries.shape[1] // 128):
        cols = slice(g * 128, (g + 1) * 128)
        probs = pair_probs(head_pair(queries[:, cols], low), keys[:, cols], length).astype(BF)
        out = dot_tn(probs, values[:, cols])
        parts.append(jnp.where(low, out[:seq], out[seq:]).astype(BF))
    return jnp.concatenate(parts, axis=1)


def attend_image_back(queries, keys, values, length, grad):
    seq = queries.shape[0]
    low = lax.broadcasted_iota(jnp.int32, (seq, 128), 1) < HEAD_DIM
    scale = HEAD_DIM ** (-0.5)
    parts = ([], [], [])
    for g in range(queries.shape[1] // 128):
        cols = slice(g * 128, (g + 1) * 128)
        stacked = head_pair(queries[:, cols], low)
        stacked_grad = head_pair(grad[:, cols], low)
        probs = pair_probs(stacked, keys[:, cols], length)
        grad_probs = dot_nt(values[:, cols], stacked_grad)
        parts[2].append(dot(probs.astype(BF), stacked_grad).astype(BF))
        centre = jnp.sum(probs * grad_probs, axis=0, keepdims=True)
        grad_scores = (probs * (grad_probs - centre)).astype(BF)
        grad_q = dot_tn(grad_scores, keys[:, cols])
        parts[0].append((jnp.where(low, grad_q[:seq], grad_q[seq:]) * scale).astype(BF))
        parts[1].append((dot(grad_scores, stacked) * scale).astype(BF))
    return [jnp.concatenate(part, axis=1) for part in parts]


def split_two(values):
    high = values.astype(BF)
    return high, (values - high.astype(F32)).astype(BF)


def each(count, step, unroll=False):
    if unroll:
        for i in range(count):
            step(i)
    else:

        def body(i, _):
            step(i)
            return 0

        lax.fori_loop(0, count, body, 0)


class Swap:
    def __init__(self, geo, block, src, dst, sems, first=0, count=None, base=0, stride=None):
        self.geo, self.block, self.src, self.dst = geo, block, src, dst
        self.first, self.count, self.base = first, count or block, base
        self.stride = stride or block
        self.send_sem, self.recv_sem, self.local_sem = sems
        self.apart = self.recv_sem.shape[0] > 1

    def given(self, p):
        return self.src.at[pl.ds(pl.multiple_of(p * self.block + self.first, 16), self.count)]

    def kept(self, p):
        return self.dst.at[pl.ds(pl.multiple_of(self.base + p * self.stride, 16), self.count)]

    def local(self):
        mine = self.geo.mine()
        return pltpu.make_async_copy(self.given(mine), self.kept(mine), self.local_sem)

    def send(self, p):
        mine = self.geo.mine()

        @pl.when(p == mine)
        def _():
            self.local().start()

        @pl.when(p != mine)
        def _():
            sem = self.recv_sem.at[self.geo.here()[0] if self.apart else 0]
            remote(self.given(p), self.kept(mine), self.send_sem.at[0], sem, self.geo.partner(p)).start()

    def send_all(self):
        mine, partners = self.geo.mine(), self.geo.partners
        each(partners, lambda i: self.send(lax.rem(mine + 1 + i, partners)))

    def blocks(self, count, sem):
        spot = self.dst.at[pl.ds(0, count * self.count)]
        return remote(spot, spot, self.send_sem.at[0], self.recv_sem.at[sem], self.geo.partner(0))

    def wait_plane(self, plane):
        z, quad = self.geo.here()[0], self.geo.plane_experts

        @pl.when(plane == z)
        def _():
            self.local().wait()
            self.blocks(quad - 1, plane).wait_recv()

        @pl.when(plane != z)
        def _():
            self.blocks(quad, plane).wait_recv()

    def wait_all(self):
        self.local().wait()
        self.blocks(self.geo.partners - 1, 0).wait_recv()

    def wait_sent(self):
        self.blocks(self.geo.partners - 1, 0).wait_send()


def swap_sems(groups):
    dma = pltpu.SemaphoreType.DMA
    return [dma((1,)), dma((groups,)), dma]


class Weights:
    def __init__(self, geo, own, full, tiles, all_tiles, sems):
        self.geo, self.own, self.full, self.tiles, self.all_tiles = geo, own, full, tiles, all_tiles
        (
            self.send_sem,
            self.recv_sem,
            self.tile_send,
            self.tile_recv,
            self.relay_send,
            self.relay_recv,
            self.local_sem,
            self.tile_local,
        ) = sems

    @staticmethod
    def sems(geo):
        dma = pltpu.SemaphoreType.DMA
        sends, places = (2, geo.local_experts, geo.group), (geo.places,)
        return [dma(sends), dma(places), dma(sends), dma(places), dma(places), dma(places), dma, dma]

    def slot(self, core, s):
        part = self.own[core].shape[2 - core]
        spot = pl.ds(pl.multiple_of(s * part, 128), part)
        return self.full[0].at[:, spot] if core == 0 else self.full[1].at[spot]

    def targets(self):
        geo = self.geo
        z, k, n = geo.here()
        for i in range(geo.local_experts):
            for g in range(geo.group):
                place = (geo.local_experts * k + i) * geo.group + g
                for core in range(2):
                    yield i, g, core, jnp.logical_and(k == core, place == n), (z * 2 + core, place)

    def start(self):
        n = self.geo.here()[2]
        for i, g, core, here, device in self.targets():

            @pl.when(here)
            def _():
                pltpu.make_async_copy(self.own[core].at[i], self.slot(core, n), self.local_sem).start()
                pltpu.make_async_copy(self.tiles.at[i], self.all_tiles.at[n], self.tile_local).start()

            @pl.when(jnp.logical_not(here))
            def _():
                remote(
                    self.own[core].at[i],
                    self.slot(core, n),
                    self.send_sem.at[core, i, g],
                    self.recv_sem.at[n],
                    device,
                ).start()
                remote(
                    self.tiles.at[i],
                    self.all_tiles.at[n],
                    self.tile_send.at[core, i, g],
                    self.tile_recv.at[n],
                    device,
                ).start()

    def relay_copy(self, core, s):
        z, k, n = self.geo.here()
        spot = self.slot(core, s)
        return remote(spot, spot, self.relay_send.at[s], self.relay_recv.at[s], (z * 2 + 1 - k, n))

    def relay(self):
        geo = self.geo
        z, k, n = geo.here()
        owner_core = (n // geo.group) // geo.local_experts
        sibling = (z * 2 + 1 - k, n)
        for s in range(geo.places):
            here = jnp.logical_and(k == owner_core, n == s)

            @pl.when(here)
            def _():
                pltpu.make_async_copy(self.tiles.at[0], self.all_tiles.at[s], self.tile_local).wait()

            @pl.when(jnp.logical_not(here))
            def _():
                spot = self.all_tiles.at[s]
                remote(spot, spot, self.tile_send.at[0, 0, 0], self.tile_recv.at[s], sibling).wait_recv()

            for core in range(2):
                spot = self.slot(core, s)

                @pl.when(jnp.logical_and(k == core, here))
                def _():
                    pltpu.make_async_copy(self.own[core].at[0], spot, self.local_sem).wait()

                @pl.when(jnp.logical_and(k == core, jnp.logical_not(here)))
                def _():
                    remote(spot, spot, self.send_sem.at[0, 0, 0], self.recv_sem.at[s], sibling).wait_recv()

                @pl.when(k == core)
                def _():
                    self.relay_copy(core, s).start()

    def finish(self):
        k = self.geo.here()[1]
        for s in range(self.geo.places):
            for core in range(2):

                @pl.when(k == core)
                def _():
                    self.relay_copy(1 - core, s).wait_recv()

    def wait_sent(self):
        k = self.geo.here()[1]
        for s in range(self.geo.places):
            for core in range(2):

                @pl.when(k == core)
                def _():
                    self.relay_copy(core, s).wait_send()

        for i, g, core, here, device in self.targets():

            @pl.when(jnp.logical_not(here))
            def _():
                remote(
                    self.own[core].at[i],
                    self.slot(core, 0),
                    self.send_sem.at[core, i, g],
                    self.recv_sem.at[0],
                    device,
                ).wait_send()
                remote(
                    self.tiles.at[i],
                    self.all_tiles.at[0],
                    self.tile_send.at[core, i, g],
                    self.tile_recv.at[0],
                    device,
                ).wait_send()


class ExpertGrads:
    def __init__(self, geo, grads, got, tiles, got_tiles, inbox, inbox_tiles, sems):
        self.geo, self.grads, self.got, self.tiles = geo, grads, got, tiles
        self.got_tiles, self.inbox, self.inbox_tiles = got_tiles, inbox, inbox_tiles
        (
            self.pair_send,
            self.pair_recv,
            self.send_sem,
            self.recv_sem,
            self.tile_send,
            self.tile_recv,
            self.local_sem,
            self.tile_local,
        ) = sems
        self.half = grads.shape[2] // 2
        self.part = grads.shape[2] // geo.places

    @staticmethod
    def sems(geo):
        dma = pltpu.SemaphoreType.DMA
        owners = (geo.local_experts, geo.group)
        return [
            dma((3,)),
            dma((3,)),
            dma((2, geo.places)),
            dma((2,) + owners),
            dma((geo.places,)),
            dma(owners),
            dma((2,)),
            dma,
        ]

    def columns(self, layer, first, count):
        return self.grads.at[layer, :, pl.ds(pl.multiple_of(first, 128), count)]

    def pair(self, layer):
        z, k, n = self.geo.here()
        away = self.columns(layer, (1 - k) * self.half, self.half)
        sibling = (z * 2 + 1 - k, n)
        return remote(away, self.got.at[layer], self.pair_send.at[layer], self.pair_recv.at[layer], sibling)

    def pair_tiles(self):
        z, k, n = self.geo.here()
        return remote(self.tiles, self.got_tiles, self.pair_send.at[2], self.pair_recv.at[2], (z * 2 + 1 - k, n))

    def towards(self):
        n = self.geo.here()[2]
        expert = n // self.geo.group
        return expert // self.geo.local_experts, expert % self.geo.local_experts, n % self.geo.group

    def slices(self):
        geo = self.geo
        z, k, n = geo.here()
        owner_core = self.towards()[0]
        for j in range(geo.places // 2):
            s = k * (geo.places // 2) + j
            yield s, jnp.logical_and(owner_core == k, n == s), (z * 2 + owner_core, s)

    def forward(self):
        k = self.geo.here()[1]
        _, i, g = self.towards()
        for layer in range(2):
            self.pair(layer).wait()
            for j in range(self.geo.places // 2):
                here = pl.ds(j * self.part, self.part)
                there = pl.ds(pl.multiple_of(k * self.half + j * self.part, 128), self.part)
                total = self.grads[layer, :, there].astype(F32) + self.got[layer, :, here].astype(F32)
                self.grads[layer, :, there] = total.astype(BF)
            for s, here, owner in self.slices():
                src = self.columns(layer, s * self.part, self.part)
                dst = self.inbox.at[layer, i, g]

                @pl.when(here)
                def _():
                    pltpu.make_async_copy(src, dst, self.local_sem.at[layer]).start()

                @pl.when(jnp.logical_not(here))
                def _():
                    remote(
                        src, dst, self.send_sem.at[layer, s], self.recv_sem.at[layer, i, g], owner
                    ).start()

        self.pair_tiles().wait()
        self.tiles[...] = self.tiles[...] + self.got_tiles[...]
        for s, here, owner in self.slices():
            src, dst = self.tiles.at[s], self.inbox_tiles.at[i, g]

            @pl.when(here)
            def _():
                pltpu.make_async_copy(src, dst, self.tile_local).start()

            @pl.when(jnp.logical_not(here))
            def _():
                remote(src, dst, self.tile_send.at[s], self.tile_recv.at[i, g], owner).start()

    def wait_got(self):
        geo = self.geo
        z, k, n = geo.here()
        sibling = (z * 2 + 1 - k, n)
        keeper = n // (geo.places // 2)
        for i in range(geo.local_experts):
            for g in range(geo.group):
                source = (k * geo.local_experts + i) * geo.group + g
                here = jnp.logical_and(source == n, keeper == k)
                for layer in range(2):
                    spot = self.inbox.at[layer, i, g]

                    @pl.when(here)
                    def _():
                        pltpu.make_async_copy(spot, spot, self.local_sem.at[layer]).wait()

                    @pl.when(jnp.logical_not(here))
                    def _():
                        remote(
                            spot, spot, self.send_sem.at[0, 0], self.recv_sem.at[layer, i, g], sibling
                        ).wait_recv()

                spot = self.inbox_tiles.at[i, g]

                @pl.when(here)
                def _():
                    pltpu.make_async_copy(spot, spot, self.tile_local).wait()

                @pl.when(jnp.logical_not(here))
                def _():
                    remote(spot, spot, self.tile_send.at[0], self.tile_recv.at[i, g], sibling).wait_recv()

    def wait_sent(self):
        for s, here, owner in self.slices():

            @pl.when(jnp.logical_not(here))
            def _():
                for layer in range(2):
                    src = self.columns(layer, s * self.part, self.part)
                    remote(
                        src, src, self.send_sem.at[layer, s], self.recv_sem.at[0, 0, 0], owner
                    ).wait_send()
                src = self.tiles.at[s]
                remote(src, src, self.tile_send.at[s], self.tile_recv.at[0, 0], owner).wait_send()


class DenseSum:
    def __init__(
        self,
        geo,
        mine,
        got_pair,
        got_plane,
        piece,
        got_z,
        wide_z,
        wide_sum,
        wide_plane,
        whole,
        small,
        s_pair,
        s_plane,
        s_z,
        sems,
        wide_chunk,
    ):
        self.geo, self.mine, self.got_pair, self.got_plane = geo, mine, got_pair, got_plane
        self.piece, self.got_z, self.whole = piece, got_z, whole
        self.wide_z, self.wide_sum, self.wide_plane = wide_z, wide_sum, wide_plane
        self.wide_chunk = wide_chunk
        self.small, self.s_pair, self.s_plane, self.s_z = small, s_pair, s_plane, s_z
        self.sems = sems
        self.half = mine.shape[0] // 2
        self.rows = self.half // geo.places
        self.columns = self.chunk_columns(geo)
        self.part = self.columns // geo.planes

    @staticmethod
    def chunk_columns(geo):
        return 128 * geo.planes

    @staticmethod
    def semaphores(geo, chunks):
        dma = pltpu.SemaphoreType.DMA
        shapes = dict(
            pair=chunks, plane=chunks, z=chunks, zg=chunks, pg=chunks, cg=chunks, sp=1, sn=1, sz=1
        )
        return list(shapes), [dma((s,)) for s in shapes.values() for _ in range(2)]

    def sem(self, name):
        names, _ = self.semaphores(self.geo, 1)
        i = names.index(name) * 2
        return self.sems[i], self.sems[i + 1]

    def where(self):
        z, k, n = self.geo.here()
        return z, k, n, (z * 2 + 1 - k, n)

    def others(self, here, count):
        return [lax.rem(here + i, count) for i in range(1, count)]

    def bytes_of(self, name, c, spot):
        send, recv = self.sem(name)
        return remote(spot, spot, send.at[c], recv.at[c], self.where()[3])

    def all_plane(self, c):
        return self.bytes_of("plane", c, self.got_plane.at[c, pl.ds(0, self.geo.places - 1)])

    def all_z(self, c):
        return self.bytes_of("z", c, self.got_z.at[c, pl.ds(0, self.geo.planes - 1)])

    def all_zg(self, c):
        spot = self.whole.at[pl.ds(0, self.rows), pl.ds(0, (self.geo.planes - 1) * self.part)]
        return self.bytes_of("zg", c, spot)

    def all_pg(self, c):
        spot = self.whole.at[pl.ds(0, (self.geo.places - 1) * self.rows), pl.ds(0, self.columns)]
        return self.bytes_of("pg", c, spot)

    def all_sn(self):
        return self.bytes_of("sn", 0, self.s_plane.at[pl.ds(0, self.geo.places - 1)])

    def all_sz(self):
        return self.bytes_of("sz", 0, self.s_z.at[pl.ds(0, self.geo.planes - 1)])

    def all_wide_plane(self, c):
        return self.bytes_of("plane", c, self.wide_plane.at[pl.ds(0, self.geo.places - 1)])

    def all_wide_z(self, c):
        return self.bytes_of("z", c, self.wide_z.at[pl.ds(0, self.geo.planes - 1)])

    def all_wide_pg(self, c):
        spot = self.whole.at[pl.ds(0, (self.geo.places - 1) * self.rows), pl.ds(0, self.part)]
        return self.bytes_of("pg", c, spot)

    def all_wide_zg(self, c):
        spot = self.whole.at[pl.ds(0, self.half), pl.ds(0, (self.geo.planes - 1) * self.part)]
        return self.bytes_of("zg", c, spot)

    def cols(self, c):
        return pl.ds(c * self.columns, self.columns)

    def place_rows(self, k, q):
        return pl.ds(pl.multiple_of(k * self.half + q * self.rows, 16), self.rows)

    def pair(self, c):
        z, k, n, sibling = self.where()
        send, recv = self.sem("pair")
        away = pl.ds(pl.multiple_of((1 - k) * self.half, 16), self.half)
        return remote(
            self.mine.at[away, self.cols(c)], self.got_pair.at[c], send.at[c], recv.at[c], sibling
        )

    def plane_copy(self, c, q):
        z, k, n, _ = self.where()
        send, recv = self.sem("plane")
        src = self.mine.at[self.place_rows(k, q), self.cols(c)]
        return remote(src, self.got_plane.at[c, n], send.at[c], recv.at[c], (z * 2 + k, q))

    def plane_start(self, c):
        z, k, n, _ = self.where()
        self.pair(c).wait()
        keep = pl.ds(pl.multiple_of(k * self.half, 16), self.half)
        total = self.mine[keep, self.cols(c)].astype(F32) + self.got_pair[c].astype(F32)
        self.mine[keep, self.cols(c)] = total.astype(BF)
        for q in self.others(n, self.geo.places):
            self.plane_copy(c, q).start()
        self.got_plane[c, n] = self.mine[self.place_rows(k, n), self.cols(c)]

    def z_copy(self, c, q):
        z, k, n, _ = self.where()
        send, recv = self.sem("z")
        return remote(
            self.piece.at[c, q], self.got_z.at[c, z], send.at[c], recv.at[c], (q * 2 + k, n)
        )

    def z_start(self, c):
        z, k, n, sibling = self.where()
        self.all_plane(c).wait_recv()
        total = self.got_plane[c, 0].astype(F32)
        for i in range(1, self.geo.places):
            total = total + self.got_plane[c, i].astype(F32)
        for p in range(self.geo.planes):
            self.piece[c, p] = total[:, p * self.part : (p + 1) * self.part].astype(BF)
        for q in self.others(z, self.geo.planes):
            self.z_copy(c, q).start()
        self.got_z[c, z] = self.piece[c, z]

    def spot(self, c, p):
        k, n = self.geo.here()[1:]
        first = pl.multiple_of(c * self.columns + p * self.part, 128)
        return self.whole.at[self.place_rows(k, n), pl.ds(first, self.part)]

    def zg_copy(self, c, q):
        z, k, n, _ = self.where()
        send, recv = self.sem("zg")
        spot = self.spot(c, z)
        return remote(spot, spot, send.at[c], recv.at[c], (q * 2 + k, n))

    def gather_z(self, c):
        z, k, n, sibling = self.where()
        self.all_z(c).wait_recv()
        total = self.got_z[c, 0].astype(F32)
        for i in range(1, self.geo.planes):
            total = total + self.got_z[c, i].astype(F32)
        first = pl.multiple_of(c * self.columns + z * self.part, 128)
        self.whole[self.place_rows(k, n), pl.ds(first, self.part)] = total.astype(BF)
        for q in self.others(z, self.geo.planes):
            self.zg_copy(c, q).start()

    def row_spot(self, c, k, q):
        return self.whole.at[self.place_rows(k, q), self.cols(c)]

    def pg_copy(self, c, q):
        z, k, n, _ = self.where()
        send, recv = self.sem("pg")
        spot = self.row_spot(c, k, n)
        return remote(spot, spot, send.at[c], recv.at[c], (z * 2 + k, q))

    def cg_copy(self, c, k):
        send, recv = self.sem("cg")
        half = pl.ds(pl.multiple_of(k * self.half, 16), self.half)
        spot = self.whole.at[half, self.cols(c)]
        return remote(spot, spot, send.at[c], recv.at[c], self.where()[3])

    def gather_plane(self, c):
        z, k, n, sibling = self.where()
        self.all_zg(c).wait_recv()
        for q in self.others(n, self.geo.places):
            self.pg_copy(c, q).start()

    def gather_pair(self, c):
        self.all_pg(c).wait_recv()
        self.cg_copy(c, self.geo.here()[1]).start()

    def gather_end(self, c):
        self.cg_copy(c, 1 - self.geo.here()[1]).wait_recv()


    def half_part(self, p, c):
        k = self.geo.here()[1]
        first = pl.multiple_of(c * self.columns + p * self.part, 128)
        return pl.ds(pl.multiple_of(k * self.half, 16), self.half), pl.ds(first, self.part)

    def wide_z_copy(self, c, q):
        z, k, n, _ = self.where()
        send, recv = self.sem("z")
        src = self.mine.at[self.half_part(q, c)]
        return remote(src, self.wide_z.at[z], send.at[c], recv.at[c], (q * 2 + k, n))

    def wide_z_start(self, c):
        z, k, n, _ = self.where()
        self.pair(c).wait()
        keep = pl.ds(pl.multiple_of(k * self.half, 16), self.half)
        total = self.mine[keep, self.cols(c)].astype(F32) + self.got_pair[c].astype(F32)
        self.mine[keep, self.cols(c)] = total.astype(BF)
        for q in self.others(z, self.geo.planes):
            self.wide_z_copy(c, q).start()

    def wide_plane_copy(self, c, q):
        z, k, n, _ = self.where()
        send, recv = self.sem("plane")
        src = self.wide_sum.at[pl.ds(pl.multiple_of(q * self.rows, 16), self.rows)]
        return remote(src, self.wide_plane.at[n], send.at[c], recv.at[c], (z * 2 + k, q))

    def wide_plane_start(self, c):
        z, k, n, sibling = self.where()
        total = self.mine[self.half_part(z, c)].astype(F32)
        self.all_wide_z(c).wait_recv()
        for q in self.others(z, self.geo.planes):
            total = total + self.wide_z[q].astype(F32)
        self.wide_sum[...] = total.astype(BF)
        for q in self.others(n, self.geo.places):
            self.wide_plane_copy(c, q).start()

    def wide_gather_plane(self, c):
        z, k, n, sibling = self.where()
        here = pl.ds(pl.multiple_of(n * self.rows, 16), self.rows)
        total = self.wide_sum[here].astype(F32)
        self.all_wide_plane(c).wait_recv()
        for q in self.others(n, self.geo.places):
            total = total + self.wide_plane[q].astype(F32)
        first = pl.multiple_of(c * self.columns + z * self.part, 128)
        self.whole[self.place_rows(k, n), pl.ds(first, self.part)] = total.astype(BF)
        for q in self.others(n, self.geo.places):
            self.wide_pg_copy(c, q).start()

    def wide_spot(self, c, q):
        z, k, n, _ = self.where()
        first = pl.multiple_of(c * self.columns + z * self.part, 128)
        return self.whole.at[self.place_rows(k, q), pl.ds(first, self.part)]

    def wide_pg_copy(self, c, q):
        z, k, n, _ = self.where()
        send, recv = self.sem("pg")
        spot = self.wide_spot(c, n)
        return remote(spot, spot, send.at[c], recv.at[c], (z * 2 + k, q))

    def wide_zg_copy(self, c, q):
        z, k, n, _ = self.where()
        send, recv = self.sem("zg")
        spot = self.whole.at[self.half_part(z, c)]
        return remote(spot, spot, send.at[c], recv.at[c], (q * 2 + k, n))

    def wide_gather_z(self, c):
        z, k, n, sibling = self.where()
        self.all_wide_pg(c).wait_recv()
        for q in self.others(z, self.geo.planes):
            self.wide_zg_copy(c, q).start()

    def wide_gather_pair(self, c):
        self.all_wide_zg(c).wait_recv()
        self.cg_copy(c, self.geo.here()[1]).start()

    def stages(self, c):
        if c == self.wide_chunk:
            return (
                self.wide_z_start,
                self.wide_plane_start,
                self.wide_gather_plane,
                self.wide_gather_z,
                self.wide_gather_pair,
                self.gather_end,
            )
        return (
            self.plane_start,
            self.z_start,
            self.gather_z,
            self.gather_plane,
            self.gather_pair,
            self.gather_end,
        )

    def small_pair(self):
        send, recv = self.sem("sp")
        return remote(self.small, self.s_pair, send.at[0], recv.at[0], self.where()[3])

    def sn_copy(self, q):
        z, k, n, _ = self.where()
        send, recv = self.sem("sn")
        return remote(self.s_plane.at[n], self.s_plane.at[n], send.at[0], recv.at[0], (z * 2 + k, q))

    def sz_copy(self, q):
        z, k, n, _ = self.where()
        send, recv = self.sem("sz")
        return remote(self.s_z.at[z], self.s_z.at[z], send.at[0], recv.at[0], (q * 2 + k, n))

    def small_plane(self):
        z, k, n, _ = self.where()
        self.small_pair().wait()
        self.s_plane[n] = self.small[...] + self.s_pair[...]
        for i in range(1, self.geo.places):
            self.sn_copy(lax.rem(n + i, self.geo.places)).start()

    def small_z(self):
        z, k, n, sibling = self.where()
        geo = self.geo
        self.all_sn().wait_recv()
        total = self.s_plane[0]
        for i in range(1, geo.places):
            total = total + self.s_plane[i]
        self.s_z[z] = total
        for i in range(1, geo.planes):
            self.sz_copy(lax.rem(z + i, geo.planes)).start()

    def small_finish(self, out):
        z, k, n, sibling = self.where()
        geo = self.geo
        self.all_sz().wait_recv()
        total = self.s_z[0]
        for i in range(1, geo.planes):
            total = total + self.s_z[i]
        out[...] = total

    def wait_sent(self, chunks):
        self.all_sn().wait_send()
        self.all_sz().wait_send()
        for c in range(chunks):
            wide = c == self.wide_chunk
            (self.all_wide_plane if wide else self.all_plane)(c).wait_send()
            (self.all_wide_z if wide else self.all_z)(c).wait_send()
            (self.all_wide_pg if wide else self.all_pg)(c).wait_send()
            (self.all_wide_zg if wide else self.all_zg)(c).wait_send()
            self.cg_copy(c, 0).wait_send()


def greet_start(devices):
    barrier = pltpu.get_barrier_semaphore()
    for device in devices:
        pl.semaphore_signal(barrier, inc=1, device_id=device, device_id_type=MESH)


def all_devices(geo):
    z, k, n = geo.here()
    found = [(z * 2 + k, lax.rem(n + i, geo.places)) for i in range(1, geo.places)]
    found += [(z * 2 + 1 - k, lax.rem(n + i, geo.places)) for i in range(geo.places)]
    for i in range(1, geo.planes):
        other = lax.rem(z + i, geo.planes)
        found += [geo.partner(other * geo.plane_experts + j) for j in range(geo.plane_experts)]
    return found


def vector(ref, cols=slice(None)):
    return ref[...].astype(F32)[None, :][:, cols]


def lane_row(row, count):
    shape = (count, row.shape[1])
    diagonal = lax.broadcasted_iota(jnp.int32, shape, 0) == lax.broadcasted_iota(jnp.int32, shape, 1)
    return jnp.sum(jnp.where(diagonal, row, 0.0), axis=1, keepdims=True)


def row_of(column, lanes):
    shape = (column.shape[0], lanes)
    diagonal = lax.broadcasted_iota(jnp.int32, shape, 0) == lax.broadcasted_iota(jnp.int32, shape, 1)
    return jnp.sum(jnp.where(diagonal, column, 0.0), axis=0, keepdims=True)


def put_pair(rows, line, high, low):
    row = lax.broadcasted_iota(jnp.int32, rows.shape, 0)
    return jnp.where(row == line, high, jnp.where(row == line + 1, low, rows))


def block_kernel(geo, sizes, names, *refs):
    r = SimpleNamespace(**dict(zip(names, refs, strict=True)))
    rows, per_micro, seq, capacity, block, width, hidden = sizes
    experts = geo.partners
    slots = experts * block
    images = rows // seq
    z, k, n = geo.here()
    quad = geo.plane_experts
    chunk = quad * block
    part = r.w1.shape[2]
    tile = 256

    r.mine = r.hidden.at[0:width, 0 : 4 * width]
    r.grad_qkv = r.grad_pre.at[0:rows, 0 : 3 * width]
    r.grad_branch = r.grad_pre.at[rows : 2 * rows, 0:width]
    r.grad_att = r.grad_pre.at[rows : 2 * rows, width : 2 * width]
    r.logits_high = r.grad_pre.at[0:rows, 4 * width - 256 : 4 * width - 128]
    r.logits_low = r.grad_pre.at[0:rows, 4 * width - 128 : 4 * width]
    lanes = -(-rows // 128) * 128
    r.late_table = r.grad_pre.at[:, 0:lanes]
    r.late_table0 = r.grad_pre.at[:, lanes : 2 * lanes]
    head = -(-(capacity + 2) // 16) * 16
    rest = block - head
    heads = experts * head
    gate_group, gate_line = capacity // 16 * 16, capacity % 16
    r.slot_grad = r.grad_pre.at[:, 3 * width : 3 * width + 256]

    def span(i, count, align=16):
        return pl.ds(pl.multiple_of(i * count, align), count)

    def sems(name):
        return [ref for key, ref in zip(names, refs, strict=True) if key.startswith(name)]

    greet_start(all_devices(geo))
    own = [name for name in names if name.startswith("given_")]
    arrive = {
        name[6:]: pltpu.make_async_copy(getattr(r, name), getattr(r, name[6:]), r.in_sem.at[i])
        for i, name in enumerate(own)
    }
    for copy in arrive.values():
        copy.start()

    def need(*wanted):
        for name in wanted:
            arrive[name].wait()

    need("choices")
    weights = Weights(
        geo, (r.w1, r.w2), (r.first, r.second), r.tile, r.tiles, sems("weights_sem")
    )
    cot_swap = Swap(geo, block, r.send_a, r.cot_got, sems("cot_sem"))
    x_swap = Swap(geo, block, r.send_b, r.x_got, sems("x_sem"))
    grad_swap, late_grad_swap = (
        Swap(geo, block, r.send_a, r.grad_got, sems("head_grad_sem"), 0, head, 0, head),
        Swap(geo, block, r.send_a, r.grad_got, sems("rest_grad_sem"), head, rest, heads, rest),
    )
    ret_swap, late_ret_swap = (
        Swap(geo, block, r.send_b, r.ret_got, sems("head_ret_sem"), 0, head, 0, head),
        Swap(geo, block, r.send_b, r.ret_got, sems("rest_ret_sem"), head, rest, heads, rest),
    )

    r.ids[...] = jnp.zeros(r.ids.shape, F32)
    for m in range(rows // per_micro):
        r.ids[0:2, m * per_micro : (m + 1) * per_micro] = r.choices[m].astype(F32)
    lines = lax.broadcasted_iota(jnp.int32, (experts, rows), 0).astype(F32)
    named = [lines == r.ids[i : i + 1, 0:rows] for i in range(2)]
    either = jnp.logical_or(named[0], named[1])
    first_row = lax.broadcasted_iota(jnp.int32, (rows, rows), 0)
    second_row = lax.broadcasted_iota(jnp.int32, (rows, rows), 1)
    same = (first_row >= per_micro) == (second_row >= per_micro)
    earlier = jnp.logical_and(first_row < second_row, same)
    before = dot(either.astype(F32).astype(BF), earlier.astype(F32).astype(BF))
    late = lax.broadcasted_iota(jnp.int32, (experts, rows), 1) >= per_micro
    slot = before + jnp.where(late, float(capacity + 2), 0.0)
    r.held[...] = jnp.full(r.held.shape, -1.0, F32)
    r.held[0, :, 0:rows] = jnp.where(either, slot, -1.0)
    r.held[1, :, 0:rows] = jnp.where(named[0], slot, -1.0)
    spots = lax.broadcasted_iota(jnp.int32, (block, lanes), 0).astype(F32)

    def fill(e):
        either = jnp.where(spots == r.held[0, pl.ds(e, 1), :], 1.0, 0.0).astype(BF)
        r.table[span(e, block), :] = either[:, 0:rows]

    def late_fill(e):
        for i, table in enumerate((r.late_table, r.late_table0)):
            found = jnp.where(spots == r.held[i, pl.ds(e, 1), :], 1.0, 0.0).astype(BF)
            table[span(e, head), :] = found[0:head]
            table[pl.ds(pl.multiple_of(heads + e * rest, 16), rest), :] = found[head:]

    def send_cot(i):
        plane = lax.rem(z + 1 + i, geo.planes)
        for j in range(quad):
            fill(plane * quad + j)

        @pl.when(i == 0)
        def _():
            need("cot")
            pl.semaphore_wait(pltpu.get_barrier_semaphore(), len(all_devices(geo)))

        blocks = dot(r.table[span(plane, chunk), :], r.cot[...])
        r.send_a[span(plane, chunk), :] = blocks.astype(BF)
        for j in range(quad):
            cot_swap.send(plane * quad + j)

    each(geo.planes, send_cot)
    r.table[pl.ds(slots, 128), :] = jnp.zeros((128, rows), BF)
    need("b1", "b2")
    for i in range(geo.local_experts):
        r.tile[i] = jnp.zeros((8, width), F32)
        r.tile[i, 0:1, 0:part] = r.b1[i : i + 1, :].astype(F32)
        r.tile[i, 1:2, :] = r.b2[i : i + 1, :].astype(F32)
    weights.start()

    def norm_in(i):
        unit, _ = norm_parts(r.tokens[span(i, seq), :].astype(F32))
        normed = unit * vector(r.gain1) + vector(r.shift1)
        r.normed[span(i, seq), :] = normed.astype(BF)

    need("tokens", "gain1", "shift1")
    each(images, norm_in)
    need("w_qkv", "bias_q", "bias_v")
    for c in range(3 * width // tile):
        cols = slice(c * tile, (c + 1) * tile)
        out = dot(r.normed[...], r.w_qkv[:, cols])
        if c * tile < width:
            out = out + vector(r.bias_q, cols)
        elif c * tile >= 2 * width:
            out = out + vector(r.bias_v, slice(c * tile - 2 * width, (c + 1) * tile - 2 * width))
        r.qkv[:, cols] = out.astype(BF)

    def attend(i):
        here = span(i, seq)
        length = r.lengths[i // (per_micro // seq), i % (per_micro // seq)]
        r.attended[here, :] = attend_image(
            r.qkv[here, 0:width],
            r.qkv[here, width : 2 * width],
            r.qkv[here, 2 * width : 3 * width],
            length,
        )

    each(images, attend)

    def branch(i):
        here = span(i, seq)
        residual = (
            r.tokens[here, :].astype(F32)
            + dot(r.attended[here, :], r.w_out[...])
            + vector(r.bias_out)
        )
        r.residual[here, :] = residual
        unit, _ = norm_parts(residual)
        expert_in = (unit * vector(r.gain2) + vector(r.shift2)).astype(BF)
        r.expert_in[here, :] = expert_in
        logits = dot_nt(expert_in, r.w_router[...])
        raised = jnp.exp(logits - jnp.max(logits, axis=-1, keepdims=True))
        probs = raised / jnp.sum(raised, axis=-1, keepdims=True)
        r.probs[here, 0:experts] = probs

    r.probs[...] = jnp.zeros(r.probs.shape, F32)
    need("w_out", "bias_out", "gain2", "shift2", "w_router")
    each(images, branch)
    probs_t = jnp.transpose(r.probs[...])[0:experts, :]
    high, low = split_two(probs_t)
    r.probs_t[0:experts, :] = high
    r.probs_t[experts : 2 * experts, :] = low

    def send_x(i):
        plane = lax.rem(z + 1 + i, geo.planes)
        blocks = dot(r.table[span(plane, chunk), :], r.expert_in[...])
        for j in range(quad):
            e = plane * quad + j
            at = e * block
            values = blocks[j * block : (j + 1) * block]
            gates = dot_nt(r.probs_t[...], r.table[pl.ds(pl.multiple_of(at, 16), 128), :])
            line = lax.broadcasted_iota(jnp.int32, gates.shape, 0)
            high = jnp.sum(jnp.where(line == e, gates, 0.0), axis=0, keepdims=True)
            low = jnp.sum(jnp.where(line == experts + e, gates, 0.0), axis=0, keepdims=True)
            r.send_b[span(e, block), :] = values.astype(BF)
            group = put_pair(values[gate_group : gate_group + 16, 0:128], gate_line, high, low)
            r.send_b[pl.ds(pl.multiple_of(at + gate_group, 16), 16), 0:128] = group.astype(BF)
            x_swap.send(e)

    each(geo.planes, send_x)

    r.ids_t[...] = jnp.transpose(r.ids[...])
    each(experts, late_fill)
    r.table_t[...] = jnp.transpose(r.late_table[...])[0:rows, :]
    r.table0_t[...] = jnp.transpose(r.late_table0[...])[0:rows, :]
    weights.relay()
    weights.finish()
    for s in range(geo.places):
        r.bias1[:, s * part : (s + 1) * part] = jnp.broadcast_to(r.tiles[s, 0:1, 0:part], (8, part))
    cot_swap.wait_sent()
    x_swap.wait_sent()

    root = 0.7978845608028654
    r.sum_pre[...] = jnp.zeros(r.sum_pre.shape, F32)
    r.sum_ret[...] = jnp.zeros(r.sum_ret.shape, F32)

    def send_late(first, last):
        for i in range(first, last):
            for j in range(quad):
                late_grad_swap.send(lax.rem(z + i, geo.planes) * quad + j)

    def expert_chunk(i):
        plane = lax.rem(z + i, geo.planes)
        here = span(plane, chunk)
        cot_swap.wait_plane(plane)
        x_swap.wait_plane(plane)

        @pl.when(i == geo.planes - 1)
        def _():
            send_late(0, geo.planes // 2)

        for j in range(quad):
            at = (plane * quad + j) * block
            group = r.x_got[pl.ds(pl.multiple_of(at + gate_group, 16), 16), 0:128].astype(F32)
            gate = lane_row(group[gate_line : gate_line + 1] + group[gate_line + 1 : gate_line + 2], block)
            there = span(plane * quad + j, block)
            r.grad_ret[there, :] = (gate * r.cot_got[there, :].astype(F32)).astype(BF)
        total_ret = jnp.sum(r.grad_ret[here, :].astype(F32), axis=0, keepdims=True)
        r.sum_ret[0:1, :] = r.sum_ret[0:1, :] + total_ret
        for c in range(hidden // tile):
            cols = slice(c * tile, (c + 1) * tile)
            pre = dot(r.x_got[here, :], r.first[:, cols]) + r.bias1[0:1, cols]
            square = pre * pre
            bend = jnp.tanh(pre * (root + 0.044715 * root * square))
            half = 0.5 + 0.5 * bend
            hidden_rows = pre * half
            r.hidden[here, cols] = hidden_rows.astype(BF)
            slope = half + hidden_rows * (1.0 - bend) * (root + 3 * 0.044715 * root * square)
            back = dot_nt(r.grad_ret[here, :], r.second[cols, :])
            grad_pre = (back * slope).astype(BF)
            r.grad_pre[here, cols] = grad_pre
            total = jnp.sum(grad_pre.astype(F32), axis=0, keepdims=True)
            r.sum_pre[0:1, cols] = r.sum_pre[0:1, cols] + total
        returned = dot(r.hidden[here, :], r.second[...]) + r.tiles[0, 1:2, :]
        r.send_b[here, :] = returned.astype(BF)
        grad_in = dot_nt(r.grad_pre[here, :], r.first[...])
        for j in range(quad):
            e = plane * quad + j
            there = span(e, block)
            product = r.cot_got[there, :].astype(F32) * r.send_b[there, :].astype(F32)
            high, low = split_two(row_of(jnp.sum(product, axis=-1, keepdims=True), 128))
            values = grad_in[j * block : (j + 1) * block]
            r.send_a[there, :] = values.astype(BF)
            group = values[gate_group : gate_group + 16, 0:128]
            group = put_pair(group, gate_line, high.astype(F32), low.astype(F32))
            at = pl.ds(pl.multiple_of(e * block + gate_group, 16), 16)
            r.send_a[at, 0:128] = group.astype(BF)
            grad_swap.send(e)

    each(geo.planes, expert_chunk)
    send_late(geo.planes // 2, geo.planes)
    for swap in (ret_swap, late_ret_swap):
        swap.send_all()

    grads = ExpertGrads(
        geo,
        r.d_experts,
        r.d_got,
        r.d_tiles,
        r.d_got_tiles,
        r.inbox,
        r.inbox_tiles,
        sems("expert_sem"),
    )
    quarter = hidden // 4

    def weight_grads(side):
        for layer, left, right in ((0, r.x_got, r.grad_pre), (1, r.grad_ret, r.hidden)):
            for c in range(2):
                cols = pl.ds(pl.multiple_of(side * (hidden // 2) + c * quarter, 128), quarter)
                r.d_experts[layer, :, cols] = dot_tn(left[...], right[:, cols]).astype(BF)

    weight_grads(1 - k)
    grads.pair(0).start()
    grads.pair(1).start()
    r.d_tiles[...] = jnp.zeros(r.d_tiles.shape, F32)
    for s in range(geo.places):
        r.d_tiles[s, 0:1, 0:part] = r.sum_pre[0:1, s * part : (s + 1) * part]
        r.d_tiles[s, 1:2, :] = r.sum_ret[0:1, :]
    grads.pair_tiles().start()
    weight_grads(k)
    grads.forward()

    dense = DenseSum(
        geo,
        r.mine,
        r.got_pair,
        r.got_plane,
        r.piece,
        r.got_z,
        r.wide_z,
        r.wide_sum,
        r.wide_plane,
        r.whole,
        r.small,
        r.s_pair,
        r.s_plane,
        r.s_z,
        sems("dense_sem"),
        4 * width // (128 * geo.planes) - (2 if 128 * geo.planes == width else 1),
    )

    def slot_grads(e):
        at = pl.ds(pl.multiple_of(e * head + gate_group, 16), 16)
        group = r.grad_got[at, 0:128].astype(F32)
        column = lane_row(group[gate_line : gate_line + 1] + group[gate_line + 1 : gate_line + 2], block)
        lane = lax.broadcasted_iota(jnp.int32, (block, 128), 1)
        late = pl.ds(pl.multiple_of(heads + e * rest, 16), rest)
        for i, value in enumerate(split_two(jnp.where(lane == e, column, 0.0))):
            cols = slice(i * 128, (i + 1) * 128)
            r.slot_grad[span(e, head), cols] = value[0:head]
            r.slot_grad[late, cols] = value[head:]

    def combine(m):
        here = slice(m * per_micro, (m + 1) * per_micro)
        there = slice(0, heads if m == 0 else slots)
        for c in range(width // tile):
            cols = slice(c * tile, (c + 1) * tile)
            r.grad_two[here, cols] = dot(r.table_t[here, there], r.grad_got[there, cols])
        both = dot(r.table_t[here, there], r.slot_grad[there, :])
        r.grad_choice[here, :] = both[:, 0:128] + both[:, 128:256]

    r.small[...] = jnp.zeros(r.small.shape, F32)

    def add_small(row, value):
        r.small[row : row + 1, :] = r.small[row : row + 1, :] + jnp.sum(value, axis=0, keepdims=True)

    def norm_two_back(i):
        here = span(i, seq)
        probs = r.probs[here, :]
        choice = r.grad_choice[here, :]
        logits = probs * (choice - jnp.sum(probs * choice, axis=-1, keepdims=True))
        high, low = split_two(logits)
        r.logits_high[here, :] = high
        r.logits_low[here, :] = low
        weight = r.w_router[...]
        grad = r.grad_two[here, :]
        grad = grad + dot(high[:, 0:experts], weight) + dot(low[:, 0:experts], weight)
        unit, scale = norm_parts(r.residual[here, :])
        add_small(5, grad * unit)
        add_small(6, grad)
        grad = r.cot[here, :].astype(F32) + norm_back(grad, unit, scale, vector(r.gain2))
        r.grad_two[here, :] = grad
        low_grad = grad.astype(BF)
        r.grad_branch[here, :] = low_grad
        add_small(4, low_grad.astype(F32))

    columns = dense.columns
    chunks = 4 * width // columns
    stages = dense.stages(chunks - 1)

    def dense_grad(first):
        cols = pl.ds(first, tile)
        if first < 3 * width:
            out = dot_tn(r.normed[...], r.grad_qkv[:, cols])
        else:
            out = dot_tn(r.attended[...], r.grad_branch[:, pl.ds(first - 3 * width, tile)])
        r.mine[:, cols] = out.astype(BF)

    early = columns == width

    def attend_grad(m):
        here = slice(m * per_micro, (m + 1) * per_micro)
        for c in range(width // tile):
            cols = slice(c * tile, (c + 1) * tile)
            r.grad_att[here, cols] = dot_nt(r.grad_branch[here, :], r.w_out[cols, :]).astype(BF)

    def attend_back(i):
        here = span(i, seq)
        length = r.lengths[i // (per_micro // seq), i % (per_micro // seq)]
        parts = attend_image_back(
            r.qkv[here, 0:width],
            r.qkv[here, width : 2 * width],
            r.qkv[here, 2 * width : 3 * width],
            length,
            r.grad_att[here, :],
        )
        for c, value in enumerate(parts):
            r.grad_qkv[here, c * width : (c + 1) * width] = value
        add_small(2, parts[0].astype(F32))
        add_small(3, parts[2].astype(F32))

    def norm_one_back(i):
        here = span(i, seq)
        grad = dot_nt(r.grad_qkv[here, :], r.w_qkv[...])
        unit, scale = norm_parts(r.tokens[here, :].astype(F32))
        add_small(0, grad * unit)
        add_small(1, grad)
        r.grad_two[here, :] = r.grad_two[here, :] + norm_back(
            grad, unit, scale, vector(r.gain1)
        )

    def mix(there, i):
        here = span(i, seq)
        total = dot(r.table_t[here, there], r.ret_got[there, :])
        chosen = dot(r.table0_t[here, there], r.ret_got[there, :])
        probs = r.probs[here, :]
        lane = lax.broadcasted_iota(jnp.int32, probs.shape, 1).astype(F32)
        gates = [
            jnp.sum(jnp.where(lane == r.ids_t[here, j : j + 1], probs, 0.0), axis=-1, keepdims=True)
            for j in range(2)
        ]
        mixed = r.residual[here, :] + gates[0] * chosen + gates[1] * (total - chosen)
        r.expert_in[here, :] = mixed.astype(BF)

    def some(step, m):
        count = images * per_micro // rows
        each(count, lambda i: step(m * count + i))

    micros = rows // per_micro
    last = (micros - 1) * images // micros
    grad_swap.wait_all()
    each(experts, slot_grads)
    for m in range(micros):
        if m == 1:
            late_grad_swap.wait_all()
        combine(m)
        some(norm_two_back, m)
        if m == micros - 1 and early:
            for first in range(3 * width, 4 * width, tile):
                dense_grad(first)
            dense.pair(chunks - 1).start()
        attend_grad(m)
        if m == micros - 1 and early:
            attend_back(last)
            stages[0](chunks - 1)
            each(images - last - 1, lambda i: attend_back(last + 1 + i))
        else:
            some(attend_back, m)
        if m < micros - 1:
            some(norm_one_back, m)
    router = dot_tn(r.logits_high[...], r.expert_in[...]) + dot_tn(r.logits_low[...], r.expert_in[...])
    r.small[8 : 8 + experts, :] = router[0:experts, :]
    late = chunks - 1 if early else chunks
    done = 1 if early else 0
    tokens_copy = pltpu.make_async_copy(r.grad_two, r.grad_tokens, r.out_sem.at[1])
    mixed_copy = pltpu.make_async_copy(r.expert_in, r.mixed, r.out_sem.at[0])
    layers_copy = pltpu.make_async_copy(r.inbox, r.d_layers, r.out_sem.at[2])
    bias_copy = pltpu.make_async_copy(r.inbox_tiles, r.d_bias, r.out_sem.at[3])

    def tokens_done():
        tokens_copy.start()
        dense.small_pair().start()

    def owner_done():
        grads.wait_got()
        layers_copy.start()
        bias_copy.start()

    def early_mix():
        ret_swap.wait_all()
        each(last, functools.partial(mix, slice(0, heads)))

    def late_mix():
        late_ret_swap.wait_all()
        each(images - last, lambda i: mix(slice(0, slots), last + i))
        mixed_copy.start()

    beside = [[] for _ in stages]
    beside[0] = [lambda: some(norm_one_back, micros - 1), tokens_done]
    beside[1] = [dense.small_plane]
    beside[2] = [dense.small_z, early_mix]
    beside[3] = [owner_done]
    small_copy = pltpu.make_async_copy(r.small, r.small_out, r.out_sem.at[5])

    def small_done():
        dense.small_finish(r.small)
        small_copy.start()

    beside[4] = [small_done, late_mix]
    for c in range(late):
        for first in range(c * columns, (c + 1) * columns, tile):
            dense_grad(first)
        dense.pair(c).start()
    for stage in range(len(stages)):
        for c in range(late):
            dense.stages(c)[stage](c)
        if early and done + stage < len(stages):
            stages[done + stage](chunks - 1)
        for step in beside[stage]:
            step()
    big_copy = pltpu.make_async_copy(r.whole, r.big_out, r.out_sem.at[4])
    big_copy.start()
    for swap in (grad_swap, late_grad_swap, ret_swap, late_ret_swap):
        swap.wait_sent()
    weights.wait_sent()
    grads.wait_sent()
    dense.wait_sent(chunks)
    for copy in (mixed_copy, tokens_copy, layers_copy, bias_copy, small_copy, big_copy):
        copy.wait()


def finish_kernel(names, *refs):
    r = SimpleNamespace(**dict(zip(names, refs, strict=True)))
    width, part = r.w_out.shape[0], r.w1.shape[2]
    local, group = r.g_d_layers.shape[1:3]
    sems = iter(range(len(names)))

    def move(src, dst):
        copy = pltpu.make_async_copy(src, dst, r.sem.at[next(sems)])
        copy.start()
        return copy

    come_layers = [
        [move(r.g_d_layers.at[layer, i], r.v_layers.at[layer, i]) for layer in range(2)] for i in range(local)
    ]
    come_big = [
        move(r.g_big_out.at[:, c * width : (c + 1) * width], r.v_big.at[:, c * width : (c + 1) * width])
        for c in range(4)
    ]
    come_small, come_bias = move(r.g_small_out, r.v_small), move(r.g_d_bias, r.v_bias)
    come_tokens, come_mixed = move(r.g_grad_tokens, r.v_tokens), move(r.g_mixed, r.v_mixed)
    copies = []
    for i in range(local):
        for layer in range(2):
            come_layers[i][layer].wait()
            total = r.v_layers[layer, i, 0].astype(F32)
            for g in range(1, group):
                total = total + r.v_layers[layer, i, g].astype(F32)
            if layer == 0:
                r.o_first[i] = total
                copies.append(move(r.o_first.at[i], r.w1.at[i]))
            else:
                r.o_second[i] = jnp.transpose(total)
                copies.append(move(r.o_second.at[i], r.w2.at[i]))
    for c in range(4):
        come_big[c].wait()
        cols = slice(c * width, (c + 1) * width)
        r.o_big[:, cols] = r.v_big[:, cols].astype(F32)
        copies.append(move(r.o_big.at[:, cols], r.w_qkv.at[:, cols] if c < 3 else r.w_out))
    come_small.wait()
    lines = ("gain1", "shift1", "bias_q", "bias_v", "bias_out", "gain2", "shift2")
    for line, name in enumerate(lines):
        row = getattr(r, "v_" + name)
        row[...] = r.v_small[line]
        copies.append(move(row, getattr(r, name)))
    copies.append(move(r.v_small.at[8:], r.router))
    come_bias.wait()
    tiles = r.v_bias[:, 0]
    for g in range(1, group):
        tiles = tiles + r.v_bias[:, g]
    r.v_b1[...] = tiles[:, 0, 0:part]
    r.v_b2[...] = tiles[:, 1, :]
    copies += [move(r.v_b1, r.b1), move(r.v_b2, r.b2)]
    come_tokens.wait()
    copies.append(move(r.v_tokens, r.grad_tokens))
    come_mixed.wait()
    copies.append(move(r.v_mixed, r.mixed))
    for copy in copies:
        copy.wait()


def on_device(
    geo,
    tokens,
    image_lengths,
    expert_index,
    grad_out,
    ln1_gain,
    ln1_bias,
    w_qkv,
    bias_query,
    bias_value,
    w_out,
    bias_out,
    ln2_gain,
    ln2_bias,
    w_router,
    experts_in,
    experts_in_bias,
    experts_out,
    experts_out_bias,
):
    micros, per_micro, width = tokens.shape
    rows = micros * per_micro
    seq = per_micro // image_lengths.shape[1]
    experts = geo.partners
    capacity = (per_micro * 42 + 20 * experts - 1) // (20 * experts)
    block = -(-(micros * capacity + 2) // 16) * 16
    slots = experts * block
    part = experts_in.shape[2]
    hidden = part * geo.places
    places, planes, local, group = geo.places, geo.planes, geo.local_experts, geo.group
    inputs = dict(
        given_choices=jnp.swapaxes(expert_index, 1, 2),
        given_cot=grad_out.reshape(rows, width),
        given_tokens=tokens.reshape(rows, width),
        lengths=image_lengths,
        given_gain1=ln1_gain,
        given_shift1=ln1_bias,
        given_w_qkv=w_qkv,
        given_bias_q=bias_query,
        given_bias_v=bias_value,
        given_w_out=w_out,
        given_bias_out=bias_out,
        given_gain2=ln2_gain,
        given_shift2=ln2_bias,
        given_w_router=w_router.T,
        w1=experts_in,
        given_b1=experts_in_bias,
        w2=experts_out,
        given_b2=experts_out_bias,
    )
    vmem, smem = pl.BlockSpec(memory_space=pltpu.VMEM), pl.BlockSpec(memory_space=pltpu.SMEM)
    anywhere = pl.BlockSpec(memory_space=pl.ANY)
    in_specs = {name: vmem for name in inputs}
    in_specs.update(lengths=smem, w1=anywhere, w2=anywhere)
    in_specs.update({name: anywhere for name in inputs if name.startswith("given")})
    small_rows = 8 + experts
    outputs = dict(
        mixed=((rows, width), BF, anywhere),
        grad_tokens=((rows, width), F32, anywhere),
        big_out=((width, 4 * width), BF, anywhere),
        small_out=((small_rows, width), F32, anywhere),
        d_layers=((2, local, group, width, part), BF, anywhere),
        d_bias=((local, group, 8, width), F32, anywhere),
    )
    half = width // 2
    columns = DenseSum.chunk_columns(geo)
    chunks = 4 * width // columns
    scratch = {name[6:]: (a.shape, a.dtype) for name, a in inputs.items() if name.startswith("given")}
    scratch.update(
        tile=((local, 8, width), F32),
        tiles=((places, 8, width), F32),
        first=((width, hidden), BF),
        second=((hidden, width), BF),
        bias1=((8, hidden), F32),
        ids=((8, -(-rows // 128) * 128), F32),
        ids_t=((-(-rows // 128) * 128, 8), F32),
        held=((2, experts, -(-rows // 128) * 128), F32),
        table=((slots + 128, rows), BF),
        table_t=((rows, slots), BF),
        table0_t=((rows, slots), BF),
        send_a=((slots, width), BF),
        send_b=((slots, width), BF),
        cot_got=((slots, width), BF),
        x_got=((slots, width), BF),
        grad_got=((slots, width), BF),
        ret_got=((slots, width), BF),
        normed=((rows, width), BF),
        qkv=((rows, 3 * width), BF),
        attended=((rows, width), BF),
        residual=((rows, width), F32),
        expert_in=((rows, width), BF),
        probs=((rows, 128), F32),
        probs_t=((2 * experts, rows), BF),
        grad_ret=((slots, width), BF),
        hidden=((slots, hidden), BF),
        grad_pre=((slots, hidden), BF),
        sum_pre=((8, hidden), F32),
        sum_ret=((8, width), F32),
        d_experts=((2, width, hidden), BF),
        d_got=((2, width, hidden // 2), BF),
        d_tiles=((places, 8, width), F32),
        d_got_tiles=((places, 8, width), F32),
        inbox=((2, local, group, width, part), BF),
        inbox_tiles=((local, group, 8, width), F32),
        grad_two=((rows, width), F32),
        grad_choice=((rows, 128), F32),
        got_pair=((chunks, half, columns), BF),
        got_plane=((chunks, places, half // places, columns), BF),
        piece=((chunks, planes, half // places, 128), BF),
        got_z=((chunks, planes, half // places, 128), BF),
        wide_z=((planes, half, 128), BF),
        wide_sum=((half, 128), BF),
        wide_plane=((places, half // places, 128), BF),
        whole=((width, 4 * width), BF),
        small=((small_rows, width), F32),
        s_pair=((small_rows, width), F32),
        s_plane=((places, small_rows, width), F32),
        s_z=((planes, small_rows, width), F32),
    )
    sem_sets = dict(
        weights_sem=Weights.sems(geo),
        cot_sem=swap_sems(planes),
        x_sem=swap_sems(planes),
        head_grad_sem=swap_sems(1),
        rest_grad_sem=swap_sems(1),
        head_ret_sem=swap_sems(1),
        rest_ret_sem=swap_sems(1),
        expert_sem=ExpertGrads.sems(geo),
        dense_sem=DenseSum.semaphores(geo, chunks)[1],
    )
    sem_names = [name + str(i) for name, found in sem_sets.items() for i in range(len(found))]
    sem_shapes = [s for found in sem_sets.values() for s in found]
    names = [*inputs, *outputs, *scratch, *sem_names, "out_sem", "in_sem"]
    sizes = (rows, per_micro, seq, capacity, block, width, hidden)
    results = pl.pallas_call(
        functools.partial(block_kernel, geo, sizes, names),
        out_shape=[jax.ShapeDtypeStruct(shape, dtype) for shape, dtype, _ in outputs.values()],
        in_specs=list(in_specs.values()),
        out_specs=[spec for _, _, spec in outputs.values()],
        scratch_shapes=[pltpu.VMEM(shape, dtype) for shape, dtype in scratch.values()]
        + sem_shapes
        + [pltpu.SemaphoreType.DMA((6,)), pltpu.SemaphoreType.DMA((len(inputs),))],
        compiler_params=pltpu.CompilerParams(
            collective_id=0, has_side_effects=True, vmem_limit_bytes=VMEM_LIMIT
        ),
    )(*inputs.values())
    out = dict(zip(outputs, results, strict=True))
    shapes = dict(
        mixed=((rows, width), BF),
        grad_tokens=((rows, width), F32),
        gain1=((width,), F32),
        shift1=((width,), F32),
        w_qkv=((width, 3 * width), F32),
        bias_q=((width,), F32),
        bias_v=((width,), F32),
        w_out=((width, width), F32),
        bias_out=((width,), F32),
        gain2=((width,), F32),
        shift2=((width,), F32),
        router=((experts, width), F32),
        w1=((local, width, part), F32),
        b1=((local, part), F32),
        w2=((local, part, width), F32),
        b2=((local, width), F32),
    )
    room = dict(
        v_big=((width, 4 * width), BF),
        v_layers=((2, local, group, width, part), BF),
        v_tokens=((rows, width), F32),
        v_mixed=((rows, width), BF),
        v_small=((small_rows, width), F32),
        v_bias=((local, group, 8, width), F32),
        o_big=((width, 4 * width), F32),
        o_first=((local, width, part), F32),
        o_second=((local, part, width), F32),
    )
    room.update({"v_" + name: spec for name, spec in shapes.items() if len(spec[0]) == 1 or name in ("b1", "b2")})
    given = ["g_" + name for name in outputs]
    made = pl.pallas_call(
        functools.partial(finish_kernel, [*given, *shapes, *room, "sem"]),
        out_shape=[jax.ShapeDtypeStruct(shape, dtype) for shape, dtype in shapes.values()],
        in_specs=[anywhere] * len(outputs),
        out_specs=[anywhere] * len(shapes),
        scratch_shapes=[pltpu.VMEM(shape, dtype) for shape, dtype in room.values()]
        + [pltpu.SemaphoreType.DMA((24 + 4 * local,))],
        compiler_params=pltpu.CompilerParams(vmem_limit_bytes=VMEM_LIMIT),
    )(*results)
    made = dict(zip(shapes, made, strict=True))
    made.update(
        mixed=made["mixed"].reshape(tokens.shape),
        grad_tokens=made["grad_tokens"].reshape(tokens.shape),
        router=made["router"].T,
    )
    return tuple(made.values())


def solution(mesh):
    split = ("wide", "narrow")
    in_specs = (
        P(None, split, None),
        P(None, split),
        P(None, split, None),
        P(None, split, None),
        *([P()] * 10),
        P("wide", None, "narrow"),
        P("wide", "narrow"),
        P("wide", "narrow", None),
        P("wide", None),
    )
    out_specs = (
        P(None, split, None),
        P(None, split, None),
        *([P()] * 10),
        P("wide", None, "narrow"),
        P("wide", "narrow"),
        P("wide", "narrow", None),
        P("wide", None),
    )

    def step(*args):
        geo = Geometry(mesh.shape["wide"], mesh.shape["narrow"], args[14].shape[0])
        return on_device(geo, *args)

    return jax.shard_map(step, mesh=mesh, in_specs=in_specs, out_specs=out_specs, check_vma=False)
```

```python
import functools
from types import SimpleNamespace

import jax
import jax.numpy as jnp
from jax import lax
from jax.experimental import pallas as pl
from jax.experimental.pallas import tpu as pltpu
from jax.sharding import PartitionSpec as P

HEADS = 8
HEAD_DIM = 64
MESH = pl.DeviceIdType.MESH
BF = jnp.bfloat16
F32 = jnp.float32
VMEM_LIMIT = 62 * 2**20


def dot(a, b):
    return lax.dot_general(a, b, (((1,), (0,)), ((), ())), preferred_element_type=F32)


def dot_nt(a, b):
    return lax.dot_general(a, b, (((1,), (1,)), ((), ())), preferred_element_type=F32)


def dot_tn(a, b):
    return lax.dot_general(a, b, (((0,), (0,)), ((), ())), preferred_element_type=F32)


class Geometry:
    def __init__(self, n_wide, n_narrow, local_experts):
        self.planes = n_wide // 2
        self.places = n_narrow
        self.local_experts = local_experts
        self.plane_experts = 2 * local_experts
        self.group = n_narrow // self.plane_experts
        self.partners = self.planes * self.plane_experts

    def here(self):
        wide, place = lax.axis_index("wide"), lax.axis_index("narrow")
        return wide // 2, wide % 2, place

    def mine(self):
        z, _, n = self.here()
        return z * self.plane_experts + n // self.group

    def partner(self, p):
        _, k, n = self.here()
        place = (p % self.plane_experts) * self.group + n % self.group
        return ((p // self.plane_experts) * 2 + k, place)


def remote(src, dst, send_sem, recv_sem, device):
    return pltpu.make_async_remote_copy(
        src_ref=src,
        dst_ref=dst,
        send_sem=send_sem,
        recv_sem=recv_sem,
        device_id=device,
        device_id_type=MESH,
    )


def norm_parts(values):
    centred = values - jnp.mean(values, axis=-1, keepdims=True)
    scale = lax.rsqrt(jnp.mean(centred * centred, axis=-1, keepdims=True) + 1e-06)
    return centred * scale, scale


def norm_back(grad, unit, scale, gain):
    pulled = grad * gain
    inner = jnp.mean(pulled, axis=-1, keepdims=True)
    along = jnp.mean(pulled * unit, axis=-1, keepdims=True)
    return scale * (pulled - inner - unit * along)


def head_pair(rows, low):
    zero = jnp.zeros_like(rows)
    return jnp.concatenate([jnp.where(low, rows, zero), jnp.where(low, zero, rows)], axis=0)


def pair_probs(stacked, keys, length):
    scores = dot_nt(keys, stacked) * HEAD_DIM ** (-0.5)
    visible = lax.broadcasted_iota(jnp.int32, scores.shape, 0) < length
    scores = jnp.where(visible, scores, -1e30)
    raised = jnp.exp(scores - jnp.max(scores, axis=0, keepdims=True))
    return raised * (1.0 / jnp.sum(raised, axis=0, keepdims=True))


def attend_image(queries, keys, values, length):
    seq = queries.shape[0]
    low = lax.broadcasted_iota(jnp.int32, (seq, 128), 1) < HEAD_DIM
    parts = []
    for g in range(queries.shape[1] // 128):
        cols = slice(g * 128, (g + 1) * 128)
        probs = pair_probs(head_pair(queries[:, cols], low), keys[:, cols], length).astype(BF)
        out = dot_tn(probs, values[:, cols])
        parts.append(jnp.where(low, out[:seq], out[seq:]).astype(BF))
    return jnp.concatenate(parts, axis=1)


def attend_image_back(queries, keys, values, length, grad):
    seq = queries.shape[0]
    low = lax.broadcasted_iota(jnp.int32, (seq, 128), 1) < HEAD_DIM
    scale = HEAD_DIM ** (-0.5)
    parts = ([], [], [])
    for g in range(queries.shape[1] // 128):
        cols = slice(g * 128, (g + 1) * 128)
        stacked = head_pair(queries[:, cols], low)
        stacked_grad = head_pair(grad[:, cols], low)
        probs = pair_probs(stacked, keys[:, cols], length)
        grad_probs = dot_nt(values[:, cols], stacked_grad)
        parts[2].append(dot(probs.astype(BF), stacked_grad).astype(BF))
        centre = jnp.sum(probs * grad_probs, axis=0, keepdims=True)
        grad_scores = (probs * (grad_probs - centre)).astype(BF)
        grad_q = dot_tn(grad_scores, keys[:, cols])
        parts[0].append((jnp.where(low, grad_q[:seq], grad_q[seq:]) * scale).astype(BF))
        parts[1].append((dot(grad_scores, stacked) * scale).astype(BF))
    return [jnp.concatenate(part, axis=1) for part in parts]


def split_two(values):
    high = values.astype(BF)
    return high, (values - high.astype(F32)).astype(BF)


def each(count, step, unroll=False):
    if unroll:
        for i in range(count):
            step(i)
    else:

        def body(i, _):
            step(i)
            return 0

        lax.fori_loop(0, count, body, 0)


class Swap:
    def __init__(self, geo, block, src, dst, sems, first=0, count=None, base=0, stride=None):
        self.geo, self.block, self.src, self.dst = geo, block, src, dst
        self.first, self.count, self.base = first, count or block, base
        self.stride = stride or block
        self.send_sem, self.recv_sem, self.local_sem = sems
        self.apart = self.recv_sem.shape[0] > 1

    def given(self, p):
        return self.src.at[pl.ds(pl.multiple_of(p * self.block + self.first, 16), self.count)]

    def kept(self, p):
        return self.dst.at[pl.ds(pl.multiple_of(self.base + p * self.stride, 16), self.count)]

    def local(self):
        mine = self.geo.mine()
        return pltpu.make_async_copy(self.given(mine), self.kept(mine), self.local_sem)

    def send(self, p):
        mine = self.geo.mine()

        @pl.when(p == mine)
        def _():
            self.local().start()

        @pl.when(p != mine)
        def _():
            sem = self.recv_sem.at[self.geo.here()[0] if self.apart else 0]
            remote(self.given(p), self.kept(mine), self.send_sem.at[0], sem, self.geo.partner(p)).start()

    def send_all(self):
        mine, partners = self.geo.mine(), self.geo.partners
        each(partners, lambda i: self.send(lax.rem(mine + 1 + i, partners)))

    def blocks(self, count, sem):
        spot = self.dst.at[pl.ds(0, count * self.count)]
        return remote(spot, spot, self.send_sem.at[0], self.recv_sem.at[sem], self.geo.partner(0))

    def wait_plane(self, plane):
        z, quad = self.geo.here()[0], self.geo.plane_experts

        @pl.when(plane == z)
        def _():
            self.local().wait()
            self.blocks(quad - 1, plane).wait_recv()

        @pl.when(plane != z)
        def _():
            self.blocks(quad, plane).wait_recv()

    def wait_all(self):
        self.local().wait()
        self.blocks(self.geo.partners - 1, 0).wait_recv()

    def wait_sent(self):
        self.blocks(self.geo.partners - 1, 0).wait_send()


def swap_sems(groups):
    dma = pltpu.SemaphoreType.DMA
    return [dma((1,)), dma((groups,)), dma]


class Weights:
    def __init__(self, geo, own, full, tiles, all_tiles, sems):
        self.geo, self.own, self.full, self.tiles, self.all_tiles = geo, own, full, tiles, all_tiles
        (
            self.send_sem,
            self.recv_sem,
            self.tile_send,
            self.tile_recv,
            self.relay_send,
            self.relay_recv,
            self.local_sem,
            self.tile_local,
        ) = sems

    @staticmethod
    def sems(geo):
        dma = pltpu.SemaphoreType.DMA
        sends, places = (2, geo.local_experts, geo.group), (geo.places,)
        return [dma(sends), dma(places), dma(sends), dma(places), dma(places), dma(places), dma, dma]

    def slot(self, core, s):
        part = self.own[core].shape[2 - core]
        spot = pl.ds(pl.multiple_of(s * part, 128), part)
        return self.full[0].at[:, spot] if core == 0 else self.full[1].at[spot]

    def targets(self):
        geo = self.geo
        z, k, n = geo.here()
        for i in range(geo.local_experts):
            for g in range(geo.group):
                place = (geo.local_experts * k + i) * geo.group + g
                for core in range(2):
                    yield i, g, core, jnp.logical_and(k == core, place == n), (z * 2 + core, place)

    def start(self):
        n = self.geo.here()[2]
        for i, g, core, here, device in self.targets():

            @pl.when(here)
            def _():
                pltpu.make_async_copy(self.own[core].at[i], self.slot(core, n), self.local_sem).start()
                pltpu.make_async_copy(self.tiles.at[i], self.all_tiles.at[n], self.tile_local).start()

            @pl.when(jnp.logical_not(here))
            def _():
                remote(
                    self.own[core].at[i],
                    self.slot(core, n),
                    self.send_sem.at[core, i, g],
                    self.recv_sem.at[n],
                    device,
                ).start()
                remote(
                    self.tiles.at[i],
                    self.all_tiles.at[n],
                    self.tile_send.at[core, i, g],
                    self.tile_recv.at[n],
                    device,
                ).start()

    def relay_copy(self, core, s):
        z, k, n = self.geo.here()
        spot = self.slot(core, s)
        return remote(spot, spot, self.relay_send.at[s], self.relay_recv.at[s], (z * 2 + 1 - k, n))

    def relay(self):
        geo = self.geo
        z, k, n = geo.here()
        owner_core = (n // geo.group) // geo.local_experts
        sibling = (z * 2 + 1 - k, n)
        for s in range(geo.places):
            here = jnp.logical_and(k == owner_core, n == s)

            @pl.when(here)
            def _():
                pltpu.make_async_copy(self.tiles.at[0], self.all_tiles.at[s], self.tile_local).wait()

            @pl.when(jnp.logical_not(here))
            def _():
                spot = self.all_tiles.at[s]
                remote(spot, spot, self.tile_send.at[0, 0, 0], self.tile_recv.at[s], sibling).wait_recv()

            for core in range(2):
                spot = self.slot(core, s)

                @pl.when(jnp.logical_and(k == core, here))
                def _():
                    pltpu.make_async_copy(self.own[core].at[0], spot, self.local_sem).wait()

                @pl.when(jnp.logical_and(k == core, jnp.logical_not(here)))
                def _():
                    remote(spot, spot, self.send_sem.at[0, 0, 0], self.recv_sem.at[s], sibling).wait_recv()

                @pl.when(k == core)
                def _():
                    self.relay_copy(core, s).start()

    def finish(self):
        k = self.geo.here()[1]
        for s in range(self.geo.places):
            for core in range(2):

                @pl.when(k == core)
                def _():
                    self.relay_copy(1 - core, s).wait_recv()

    def wait_sent(self):
        k = self.geo.here()[1]
        for s in range(self.geo.places):
            for core in range(2):

                @pl.when(k == core)
                def _():
                    self.relay_copy(core, s).wait_send()

        for i, g, core, here, device in self.targets():

            @pl.when(jnp.logical_not(here))
            def _():
                remote(
                    self.own[core].at[i],
                    self.slot(core, 0),
                    self.send_sem.at[core, i, g],
                    self.recv_sem.at[0],
                    device,
                ).wait_send()
                remote(
                    self.tiles.at[i],
                    self.all_tiles.at[0],
                    self.tile_send.at[core, i, g],
                    self.tile_recv.at[0],
                    device,
                ).wait_send()


class ExpertGrads:
    def __init__(self, geo, grads, got, tiles, got_tiles, inbox, inbox_tiles, sems):
        self.geo, self.grads, self.got, self.tiles = geo, grads, got, tiles
        self.got_tiles, self.inbox, self.inbox_tiles = got_tiles, inbox, inbox_tiles
        (
            self.pair_send,
            self.pair_recv,
            self.send_sem,
            self.recv_sem,
            self.tile_send,
            self.tile_recv,
            self.local_sem,
            self.tile_local,
        ) = sems
        self.half = grads.shape[2] // 2
        self.part = grads.shape[2] // geo.places

    @staticmethod
    def sems(geo):
        dma = pltpu.SemaphoreType.DMA
        owners = (geo.local_experts, geo.group)
        return [
            dma((3,)),
            dma((3,)),
            dma((2, geo.places)),
            dma((2,) + owners),
            dma((geo.places,)),
            dma(owners),
            dma((2,)),
            dma,
        ]

    def columns(self, layer, first, count):
        return self.grads.at[layer, :, pl.ds(pl.multiple_of(first, 128), count)]

    def pair(self, layer):
        z, k, n = self.geo.here()
        away = self.columns(layer, (1 - k) * self.half, self.half)
        sibling = (z * 2 + 1 - k, n)
        return remote(away, self.got.at[layer], self.pair_send.at[layer], self.pair_recv.at[layer], sibling)

    def pair_tiles(self):
        z, k, n = self.geo.here()
        return remote(self.tiles, self.got_tiles, self.pair_send.at[2], self.pair_recv.at[2], (z * 2 + 1 - k, n))

    def towards(self):
        n = self.geo.here()[2]
        expert = n // self.geo.group
        return expert // self.geo.local_experts, expert % self.geo.local_experts, n % self.geo.group

    def slices(self):
        geo = self.geo
        z, k, n = geo.here()
        owner_core = self.towards()[0]
        for j in range(geo.places // 2):
            s = k * (geo.places // 2) + j
            yield s, jnp.logical_and(owner_core == k, n == s), (z * 2 + owner_core, s)

    def forward(self):
        k = self.geo.here()[1]
        _, i, g = self.towards()
        for layer in range(2):
            self.pair(layer).wait()
            for j in range(self.geo.places // 2):
                here = pl.ds(j * self.part, self.part)
                there = pl.ds(pl.multiple_of(k * self.half + j * self.part, 128), self.part)
                total = self.grads[layer, :, there].astype(F32) + self.got[layer, :, here].astype(F32)
                self.grads[layer, :, there] = total.astype(BF)
            for s, here, owner in self.slices():
                src = self.columns(layer, s * self.part, self.part)
                dst = self.inbox.at[layer, i, g]

                @pl.when(here)
                def _():
                    pltpu.make_async_copy(src, dst, self.local_sem.at[layer]).start()

                @pl.when(jnp.logical_not(here))
                def _():
                    remote(
                        src, dst, self.send_sem.at[layer, s], self.recv_sem.at[layer, i, g], owner
                    ).start()

        self.pair_tiles().wait()
        self.tiles[...] = self.tiles[...] + self.got_tiles[...]
        for s, here, owner in self.slices():
            src, dst = self.tiles.at[s], self.inbox_tiles.at[i, g]

            @pl.when(here)
            def _():
                pltpu.make_async_copy(src, dst, self.tile_local).start()

            @pl.when(jnp.logical_not(here))
            def _():
                remote(src, dst, self.tile_send.at[s], self.tile_recv.at[i, g], owner).start()

    def wait_got(self):
        geo = self.geo
        z, k, n = geo.here()
        sibling = (z * 2 + 1 - k, n)
        keeper = n // (geo.places // 2)
        for i in range(geo.local_experts):
            for g in range(geo.group):
                source = (k * geo.local_experts + i) * geo.group + g
                here = jnp.logical_and(source == n, keeper == k)
                for layer in range(2):
                    spot = self.inbox.at[layer, i, g]

                    @pl.when(here)
                    def _():
                        pltpu.make_async_copy(spot, spot, self.local_sem.at[layer]).wait()

                    @pl.when(jnp.logical_not(here))
                    def _():
                        remote(
                            spot, spot, self.send_sem.at[0, 0], self.recv_sem.at[layer, i, g], sibling
                        ).wait_recv()

                spot = self.inbox_tiles.at[i, g]

                @pl.when(here)
                def _():
                    pltpu.make_async_copy(spot, spot, self.tile_local).wait()

                @pl.when(jnp.logical_not(here))
                def _():
                    remote(spot, spot, self.tile_send.at[0], self.tile_recv.at[i, g], sibling).wait_recv()

    def wait_sent(self):
        for s, here, owner in self.slices():

            @pl.when(jnp.logical_not(here))
            def _():
                for layer in range(2):
                    src = self.columns(layer, s * self.part, self.part)
                    remote(
                        src, src, self.send_sem.at[layer, s], self.recv_sem.at[0, 0, 0], owner
                    ).wait_send()
                src = self.tiles.at[s]
                remote(src, src, self.tile_send.at[s], self.tile_recv.at[0, 0], owner).wait_send()


class DenseSum:
    def __init__(
        self,
        geo,
        mine,
        got_pair,
        got_plane,
        piece,
        got_z,
        wide_z,
        wide_sum,
        wide_plane,
        whole,
        small,
        s_pair,
        s_plane,
        s_z,
        sems,
        wide_chunk,
    ):
        self.geo, self.mine, self.got_pair, self.got_plane = geo, mine, got_pair, got_plane
        self.piece, self.got_z, self.whole = piece, got_z, whole
        self.wide_z, self.wide_sum, self.wide_plane = wide_z, wide_sum, wide_plane
        self.wide_chunk = wide_chunk
        self.small, self.s_pair, self.s_plane, self.s_z = small, s_pair, s_plane, s_z
        self.sems = sems
        self.half = mine.shape[0] // 2
        self.rows = self.half // geo.places
        self.columns = self.chunk_columns(geo)
        self.part = self.columns // geo.planes

    @staticmethod
    def chunk_columns(geo):
        return 128 * geo.planes

    @staticmethod
    def semaphores(geo, chunks):
        dma = pltpu.SemaphoreType.DMA
        shapes = dict(
            pair=chunks, plane=chunks, z=chunks, zg=chunks, pg=chunks, cg=chunks, sp=1, sn=1, sz=1
        )
        return list(shapes), [dma((s,)) for s in shapes.values() for _ in range(2)]

    def sem(self, name):
        names, _ = self.semaphores(self.geo, 1)
        i = names.index(name) * 2
        return self.sems[i], self.sems[i + 1]

    def where(self):
        z, k, n = self.geo.here()
        return z, k, n, (z * 2 + 1 - k, n)

    def others(self, here, count):
        return [lax.rem(here + i, count) for i in range(1, count)]

    def bytes_of(self, name, c, spot):
        send, recv = self.sem(name)
        return remote(spot, spot, send.at[c], recv.at[c], self.where()[3])

    def all_plane(self, c):
        return self.bytes_of("plane", c, self.got_plane.at[c, pl.ds(0, self.geo.places - 1)])

    def all_z(self, c):
        return self.bytes_of("z", c, self.got_z.at[c, pl.ds(0, self.geo.planes - 1)])

    def all_zg(self, c):
        spot = self.whole.at[pl.ds(0, self.rows), pl.ds(0, (self.geo.planes - 1) * self.part)]
        return self.bytes_of("zg", c, spot)

    def all_pg(self, c):
        spot = self.whole.at[pl.ds(0, (self.geo.places - 1) * self.rows), pl.ds(0, self.columns)]
        return self.bytes_of("pg", c, spot)

    def all_sn(self):
        return self.bytes_of("sn", 0, self.s_plane.at[pl.ds(0, self.geo.places - 1)])

    def all_sz(self):
        return self.bytes_of("sz", 0, self.s_z.at[pl.ds(0, self.geo.planes - 1)])

    def all_wide_plane(self, c):
        return self.bytes_of("plane", c, self.wide_plane.at[pl.ds(0, self.geo.places - 1)])

    def all_wide_z(self, c):
        return self.bytes_of("z", c, self.wide_z.at[pl.ds(0, self.geo.planes - 1)])

    def all_wide_pg(self, c):
        spot = self.whole.at[pl.ds(0, (self.geo.places - 1) * self.rows), pl.ds(0, self.part)]
        return self.bytes_of("pg", c, spot)

    def all_wide_zg(self, c):
        spot = self.whole.at[pl.ds(0, self.half), pl.ds(0, (self.geo.planes - 1) * self.part)]
        return self.bytes_of("zg", c, spot)

    def cols(self, c):
        return pl.ds(c * self.columns, self.columns)

    def place_rows(self, k, q):
        return pl.ds(pl.multiple_of(k * self.half + q * self.rows, 16), self.rows)

    def pair(self, c):
        z, k, n, sibling = self.where()
        send, recv = self.sem("pair")
        away = pl.ds(pl.multiple_of((1 - k) * self.half, 16), self.half)
        return remote(
            self.mine.at[away, self.cols(c)], self.got_pair.at[c], send.at[c], recv.at[c], sibling
        )

    def plane_copy(self, c, q):
        z, k, n, _ = self.where()
        send, recv = self.sem("plane")
        src = self.mine.at[self.place_rows(k, q), self.cols(c)]
        return remote(src, self.got_plane.at[c, n], send.at[c], recv.at[c], (z * 2 + k, q))

    def plane_start(self, c):
        z, k, n, _ = self.where()
        self.pair(c).wait()
        keep = pl.ds(pl.multiple_of(k * self.half, 16), self.half)
        total = self.mine[keep, self.cols(c)].astype(F32) + self.got_pair[c].astype(F32)
        self.mine[keep, self.cols(c)] = total.astype(BF)
        for q in self.others(n, self.geo.places):
            self.plane_copy(c, q).start()
        self.got_plane[c, n] = self.mine[self.place_rows(k, n), self.cols(c)]

    def z_copy(self, c, q):
        z, k, n, _ = self.where()
        send, recv = self.sem("z")
        return remote(
            self.piece.at[c, q], self.got_z.at[c, z], send.at[c], recv.at[c], (q * 2 + k, n)
        )

    def z_start(self, c):
        z, k, n, sibling = self.where()
        self.all_plane(c).wait_recv()
        total = self.got_plane[c, 0].astype(F32)
        for i in range(1, self.geo.places):
            total = total + self.got_plane[c, i].astype(F32)
        for p in range(self.geo.planes):
            self.piece[c, p] = total[:, p * self.part : (p + 1) * self.part].astype(BF)
        for q in self.others(z, self.geo.planes):
            self.z_copy(c, q).start()
        self.got_z[c, z] = self.piece[c, z]

    def spot(self, c, p):
        k, n = self.geo.here()[1:]
        first = pl.multiple_of(c * self.columns + p * self.part, 128)
        return self.whole.at[self.place_rows(k, n), pl.ds(first, self.part)]

    def zg_copy(self, c, q):
        z, k, n, _ = self.where()
        send, recv = self.sem("zg")
        spot = self.spot(c, z)
        return remote(spot, spot, send.at[c], recv.at[c], (q * 2 + k, n))

    def gather_z(self, c):
        z, k, n, sibling = self.where()
        self.all_z(c).wait_recv()
        total = self.got_z[c, 0].astype(F32)
        for i in range(1, self.geo.planes):
            total = total + self.got_z[c, i].astype(F32)
        first = pl.multiple_of(c * self.columns + z * self.part, 128)
        self.whole[self.place_rows(k, n), pl.ds(first, self.part)] = total.astype(BF)
        for q in self.others(z, self.geo.planes):
            self.zg_copy(c, q).start()

    def row_spot(self, c, k, q):
        return self.whole.at[self.place_rows(k, q), self.cols(c)]

    def pg_copy(self, c, q):
        z, k, n, _ = self.where()
        send, recv = self.sem("pg")
        spot = self.row_spot(c, k, n)
        return remote(spot, spot, send.at[c], recv.at[c], (z * 2 + k, q))

    def cg_copy(self, c, k):
        send, recv = self.sem("cg")
        half = pl.ds(pl.multiple_of(k * self.half, 16), self.half)
        spot = self.whole.at[half, self.cols(c)]
        return remote(spot, spot, send.at[c], recv.at[c], self.where()[3])

    def gather_plane(self, c):
        z, k, n, sibling = self.where()
        self.all_zg(c).wait_recv()
        for q in self.others(n, self.geo.places):
            self.pg_copy(c, q).start()

    def gather_pair(self, c):
        self.all_pg(c).wait_recv()
        self.cg_copy(c, self.geo.here()[1]).start()

    def gather_end(self, c):
        self.cg_copy(c, 1 - self.geo.here()[1]).wait_recv()


    def half_part(self, p, c):
        k = self.geo.here()[1]
        first = pl.multiple_of(c * self.columns + p * self.part, 128)
        return pl.ds(pl.multiple_of(k * self.half, 16), self.half), pl.ds(first, self.part)

    def wide_z_copy(self, c, q):
        z, k, n, _ = self.where()
        send, recv = self.sem("z")
        src = self.mine.at[self.half_part(q, c)]
        return remote(src, self.wide_z.at[z], send.at[c], recv.at[c], (q * 2 + k, n))

    def wide_z_start(self, c):
        z, k, n, _ = self.where()
        self.pair(c).wait()
        keep = pl.ds(pl.multiple_of(k * self.half, 16), self.half)
        total = self.mine[keep, self.cols(c)].astype(F32) + self.got_pair[c].astype(F32)
        self.mine[keep, self.cols(c)] = total.astype(BF)
        for q in self.others(z, self.geo.planes):
            self.wide_z_copy(c, q).start()

    def wide_plane_copy(self, c, q):
        z, k, n, _ = self.where()
        send, recv = self.sem("plane")
        src = self.wide_sum.at[pl.ds(pl.multiple_of(q * self.rows, 16), self.rows)]
        return remote(src, self.wide_plane.at[n], send.at[c], recv.at[c], (z * 2 + k, q))

    def wide_plane_start(self, c):
        z, k, n, sibling = self.where()
        total = self.mine[self.half_part(z, c)].astype(F32)
        self.all_wide_z(c).wait_recv()
        for q in self.others(z, self.geo.planes):
            total = total + self.wide_z[q].astype(F32)
        self.wide_sum[...] = total.astype(BF)
        for q in self.others(n, self.geo.places):
            self.wide_plane_copy(c, q).start()

    def wide_gather_plane(self, c):
        z, k, n, sibling = self.where()
        here = pl.ds(pl.multiple_of(n * self.rows, 16), self.rows)
        total = self.wide_sum[here].astype(F32)
        self.all_wide_plane(c).wait_recv()
        for q in self.others(n, self.geo.places):
            total = total + self.wide_plane[q].astype(F32)
        first = pl.multiple_of(c * self.columns + z * self.part, 128)
        self.whole[self.place_rows(k, n), pl.ds(first, self.part)] = total.astype(BF)
        for q in self.others(n, self.geo.places):
            self.wide_pg_copy(c, q).start()

    def wide_spot(self, c, q):
        z, k, n, _ = self.where()
        first = pl.multiple_of(c * self.columns + z * self.part, 128)
        return self.whole.at[self.place_rows(k, q), pl.ds(first, self.part)]

    def wide_pg_copy(self, c, q):
        z, k, n, _ = self.where()
        send, recv = self.sem("pg")
        spot = self.wide_spot(c, n)
        return remote(spot, spot, send.at[c], recv.at[c], (z * 2 + k, q))

    def wide_zg_copy(self, c, q):
        z, k, n, _ = self.where()
        send, recv = self.sem("zg")
        spot = self.whole.at[self.half_part(z, c)]
        return remote(spot, spot, send.at[c], recv.at[c], (q * 2 + k, n))

    def wide_gather_z(self, c):
        z, k, n, sibling = self.where()
        self.all_wide_pg(c).wait_recv()
        for q in self.others(z, self.geo.planes):
            self.wide_zg_copy(c, q).start()

    def wide_gather_pair(self, c):
        self.all_wide_zg(c).wait_recv()
        self.cg_copy(c, self.geo.here()[1]).start()

    def stages(self, c):
        if c == self.wide_chunk:
            return (
                self.wide_z_start,
                self.wide_plane_start,
                self.wide_gather_plane,
                self.wide_gather_z,
                self.wide_gather_pair,
                self.gather_end,
            )
        return (
            self.plane_start,
            self.z_start,
            self.gather_z,
            self.gather_plane,
            self.gather_pair,
            self.gather_end,
        )

    def small_pair(self):
        send, recv = self.sem("sp")
        return remote(self.small, self.s_pair, send.at[0], recv.at[0], self.where()[3])

    def sn_copy(self, q):
        z, k, n, _ = self.where()
        send, recv = self.sem("sn")
        return remote(self.s_plane.at[n], self.s_plane.at[n], send.at[0], recv.at[0], (z * 2 + k, q))

    def sz_copy(self, q):
        z, k, n, _ = self.where()
        send, recv = self.sem("sz")
        return remote(self.s_z.at[z], self.s_z.at[z], send.at[0], recv.at[0], (q * 2 + k, n))

    def small_plane(self):
        z, k, n, _ = self.where()
        self.small_pair().wait()
        self.s_plane[n] = self.small[...] + self.s_pair[...]
        for i in range(1, self.geo.places):
            self.sn_copy(lax.rem(n + i, self.geo.places)).start()

    def small_z(self):
        z, k, n, sibling = self.where()
        geo = self.geo
        self.all_sn().wait_recv()
        total = self.s_plane[0]
        for i in range(1, geo.places):
            total = total + self.s_plane[i]
        self.s_z[z] = total
        for i in range(1, geo.planes):
            self.sz_copy(lax.rem(z + i, geo.planes)).start()

    def small_finish(self, out):
        z, k, n, sibling = self.where()
        geo = self.geo
        self.all_sz().wait_recv()
        total = self.s_z[0]
        for i in range(1, geo.planes):
            total = total + self.s_z[i]
        out[...] = total

    def wait_sent(self, chunks):
        self.all_sn().wait_send()
        self.all_sz().wait_send()
        for c in range(chunks):
            wide = c == self.wide_chunk
            (self.all_wide_plane if wide else self.all_plane)(c).wait_send()
            (self.all_wide_z if wide else self.all_z)(c).wait_send()
            (self.all_wide_pg if wide else self.all_pg)(c).wait_send()
            (self.all_wide_zg if wide else self.all_zg)(c).wait_send()
            self.cg_copy(c, 0).wait_send()


def greet_start(devices):
    barrier = pltpu.get_barrier_semaphore()
    for device in devices:
        pl.semaphore_signal(barrier, inc=1, device_id=device, device_id_type=MESH)


def all_devices(geo):
    z, k, n = geo.here()
    found = [(z * 2 + k, lax.rem(n + i, geo.places)) for i in range(1, geo.places)]
    found += [(z * 2 + 1 - k, lax.rem(n + i, geo.places)) for i in range(geo.places)]
    for i in range(1, geo.planes):
        other = lax.rem(z + i, geo.planes)
        found += [geo.partner(other * geo.plane_experts + j) for j in range(geo.plane_experts)]
    return found


def vector(ref, cols=slice(None)):
    return ref[...].astype(F32)[None, :][:, cols]


def lane_row(row, count):
    shape = (count, row.shape[1])
    diagonal = lax.broadcasted_iota(jnp.int32, shape, 0) == lax.broadcasted_iota(jnp.int32, shape, 1)
    return jnp.sum(jnp.where(diagonal, row, 0.0), axis=1, keepdims=True)


def row_of(column, lanes):
    shape = (column.shape[0], lanes)
    diagonal = lax.broadcasted_iota(jnp.int32, shape, 0) == lax.broadcasted_iota(jnp.int32, shape, 1)
    return jnp.sum(jnp.where(diagonal, column, 0.0), axis=0, keepdims=True)


def put_pair(rows, line, high, low):
    row = lax.broadcasted_iota(jnp.int32, rows.shape, 0)
    return jnp.where(row == line, high, jnp.where(row == line + 1, low, rows))


def block_kernel(geo, sizes, names, *refs):
    r = SimpleNamespace(**dict(zip(names, refs, strict=True)))
    rows, per_micro, seq, capacity, block, width, hidden = sizes
    experts = geo.partners
    slots = experts * block
    images = rows // seq
    z, k, n = geo.here()
    quad = geo.plane_experts
    chunk = quad * block
    part = r.w1.shape[2]
    tile = 256

    r.mine = r.hidden.at[0:width, 0 : 4 * width]
    r.grad_qkv = r.grad_pre.at[0:rows, 0 : 3 * width]
    r.grad_branch = r.grad_pre.at[rows : 2 * rows, 0:width]
    r.grad_att = r.grad_pre.at[rows : 2 * rows, width : 2 * width]
    r.logits_high = r.grad_pre.at[0:rows, 4 * width - 256 : 4 * width - 128]
    r.logits_low = r.grad_pre.at[0:rows, 4 * width - 128 : 4 * width]
    lanes = -(-rows // 128) * 128
    r.late_table = r.grad_pre.at[:, 0:lanes]
    r.late_table0 = r.grad_pre.at[:, lanes : 2 * lanes]
    head = -(-(capacity + 2) // 16) * 16
    rest = block - head
    heads = experts * head
    gate_group, gate_line = capacity // 16 * 16, capacity % 16
    r.slot_grad = r.grad_pre.at[:, 3 * width : 3 * width + 256]

    def span(i, count, align=16):
        return pl.ds(pl.multiple_of(i * count, align), count)

    def sems(name):
        return [ref for key, ref in zip(names, refs, strict=True) if key.startswith(name)]

    greet_start(all_devices(geo))
    own = [name for name in names if name.startswith("given_")]
    arrive = {
        name[6:]: pltpu.make_async_copy(getattr(r, name), getattr(r, name[6:]), r.in_sem.at[i])
        for i, name in enumerate(own)
    }
    for copy in arrive.values():
        copy.start()

    def need(*wanted):
        for name in wanted:
            arrive[name].wait()

    need("choices")
    weights = Weights(
        geo, (r.w1, r.w2), (r.first, r.second), r.tile, r.tiles, sems("weights_sem")
    )
    cot_swap = Swap(geo, block, r.send_a, r.cot_got, sems("cot_sem"))
    x_swap = Swap(geo, block, r.send_b, r.x_got, sems("x_sem"))
    grad_swap, late_grad_swap = (
        Swap(geo, block, r.send_a, r.grad_got, sems("head_grad_sem"), 0, head, 0, head),
        Swap(geo, block, r.send_a, r.grad_got, sems("rest_grad_sem"), head, rest, heads, rest),
    )
    ret_swap, late_ret_swap = (
        Swap(geo, block, r.send_b, r.ret_got, sems("head_ret_sem"), 0, head, 0, head),
        Swap(geo, block, r.send_b, r.ret_got, sems("rest_ret_sem"), head, rest, heads, rest),
    )

    r.ids[...] = jnp.zeros(r.ids.shape, F32)
    for m in range(rows // per_micro):
        r.ids[0:2, m * per_micro : (m + 1) * per_micro] = r.choices[m].astype(F32)
    lines = lax.broadcasted_iota(jnp.int32, (experts, rows), 0).astype(F32)
    named = [lines == r.ids[i : i + 1, 0:rows] for i in range(2)]
    either = jnp.logical_or(named[0], named[1])
    first_row = lax.broadcasted_iota(jnp.int32, (rows, rows), 0)
    second_row = lax.broadcasted_iota(jnp.int32, (rows, rows), 1)
    same = (first_row >= per_micro) == (second_row >= per_micro)
    earlier = jnp.logical_and(first_row < second_row, same)
    before = dot(either.astype(F32).astype(BF), earlier.astype(F32).astype(BF))
    late = lax.broadcasted_iota(jnp.int32, (experts, rows), 1) >= per_micro
    slot = before + jnp.where(late, float(capacity + 2), 0.0)
    r.held[...] = jnp.full(r.held.shape, -1.0, F32)
    r.held[0, :, 0:rows] = jnp.where(either, slot, -1.0)
    r.held[1, :, 0:rows] = jnp.where(named[0], slot, -1.0)
    spots = lax.broadcasted_iota(jnp.int32, (block, lanes), 0).astype(F32)

    def fill(e):
        either = jnp.where(spots == r.held[0, pl.ds(e, 1), :], 1.0, 0.0).astype(BF)
        r.table[span(e, block), :] = either[:, 0:rows]

    def late_fill(e):
        for i, table in enumerate((r.late_table, r.late_table0)):
            found = jnp.where(spots == r.held[i, pl.ds(e, 1), :], 1.0, 0.0).astype(BF)
            table[span(e, head), :] = found[0:head]
            table[pl.ds(pl.multiple_of(heads + e * rest, 16), rest), :] = found[head:]

    def send_cot(i):
        plane = lax.rem(z + 1 + i, geo.planes)
        for j in range(quad):
            fill(plane * quad + j)

        @pl.when(i == 0)
        def _():
            need("cot")
            pl.semaphore_wait(pltpu.get_barrier_semaphore(), len(all_devices(geo)))

        blocks = dot(r.table[span(plane, chunk), :], r.cot[...])
        r.send_a[span(plane, chunk), :] = blocks.astype(BF)
        for j in range(quad):
            cot_swap.send(plane * quad + j)

    each(geo.planes, send_cot)
    r.table[pl.ds(slots, 128), :] = jnp.zeros((128, rows), BF)
    need("b1", "b2")
    for i in range(geo.local_experts):
        r.tile[i] = jnp.zeros((8, width), F32)
        r.tile[i, 0:1, 0:part] = r.b1[i : i + 1, :].astype(F32)
        r.tile[i, 1:2, :] = r.b2[i : i + 1, :].astype(F32)
    weights.start()

    def norm_in(i):
        unit, _ = norm_parts(r.tokens[span(i, seq), :].astype(F32))
        normed = unit * vector(r.gain1) + vector(r.shift1)
        r.normed[span(i, seq), :] = normed.astype(BF)

    need("tokens", "gain1", "shift1")
    each(images, norm_in)
    need("w_qkv", "bias_q", "bias_v")
    for c in range(3 * width // tile):
        cols = slice(c * tile, (c + 1) * tile)
        out = dot(r.normed[...], r.w_qkv[:, cols])
        if c * tile < width:
            out = out + vector(r.bias_q, cols)
        elif c * tile >= 2 * width:
            out = out + vector(r.bias_v, slice(c * tile - 2 * width, (c + 1) * tile - 2 * width))
        r.qkv[:, cols] = out.astype(BF)

    def attend(i):
        here = span(i, seq)
        length = r.lengths[i // (per_micro // seq), i % (per_micro // seq)]
        r.attended[here, :] = attend_image(
            r.qkv[here, 0:width],
            r.qkv[here, width : 2 * width],
            r.qkv[here, 2 * width : 3 * width],
            length,
        )

    each(images, attend)

    def branch(i):
        here = span(i, seq)
        residual = (
            r.tokens[here, :].astype(F32)
            + dot(r.attended[here, :], r.w_out[...])
            + vector(r.bias_out)
        )
        r.residual[here, :] = residual
        unit, _ = norm_parts(residual)
        expert_in = (unit * vector(r.gain2) + vector(r.shift2)).astype(BF)
        r.expert_in[here, :] = expert_in
        logits = dot_nt(expert_in, r.w_router[...])
        raised = jnp.exp(logits - jnp.max(logits, axis=-1, keepdims=True))
        probs = raised / jnp.sum(raised, axis=-1, keepdims=True)
        r.probs[here, 0:experts] = probs

    r.probs[...] = jnp.zeros(r.probs.shape, F32)
    need("w_out", "bias_out", "gain2", "shift2", "w_router")
    each(images, branch)
    probs_t = jnp.transpose(r.probs[...])[0:experts, :]
    high, low = split_two(probs_t)
    r.probs_t[0:experts, :] = high
    r.probs_t[experts : 2 * experts, :] = low

    def send_x(i):
        plane = lax.rem(z + 1 + i, geo.planes)
        blocks = dot(r.table[span(plane, chunk), :], r.expert_in[...])
        for j in range(quad):
            e = plane * quad + j
            at = e * block
            values = blocks[j * block : (j + 1) * block]
            gates = dot_nt(r.probs_t[...], r.table[pl.ds(pl.multiple_of(at, 16), 128), :])
            line = lax.broadcasted_iota(jnp.int32, gates.shape, 0)
            high = jnp.sum(jnp.where(line == e, gates, 0.0), axis=0, keepdims=True)
            low = jnp.sum(jnp.where(line == experts + e, gates, 0.0), axis=0, keepdims=True)
            r.send_b[span(e, block), :] = values.astype(BF)
            group = put_pair(values[gate_group : gate_group + 16, 0:128], gate_line, high, low)
            r.send_b[pl.ds(pl.multiple_of(at + gate_group, 16), 16), 0:128] = group.astype(BF)
            x_swap.send(e)

    each(geo.planes, send_x)

    r.ids_t[...] = jnp.transpose(r.ids[...])
    each(experts, late_fill)
    r.table_t[...] = jnp.transpose(r.late_table[...])[0:rows, :]
    r.table0_t[...] = jnp.transpose(r.late_table0[...])[0:rows, :]
    weights.relay()
    weights.finish()
    for s in range(geo.places):
        r.bias1[:, s * part : (s + 1) * part] = jnp.broadcast_to(r.tiles[s, 0:1, 0:part], (8, part))
    cot_swap.wait_sent()
    x_swap.wait_sent()

    root = 0.7978845608028654

    def send_late(first, last):
        for i in range(first, last):
            for j in range(quad):
                late_grad_swap.send(lax.rem(z + i, geo.planes) * quad + j)

    def expert_chunk(i):
        plane = lax.rem(z + i, geo.planes)
        here = span(plane, chunk)
        cot_swap.wait_plane(plane)
        x_swap.wait_plane(plane)

        @pl.when(i == geo.planes - 1)
        def _():
            send_late(0, geo.planes // 2)

        for j in range(quad):
            at = (plane * quad + j) * block
            group = r.x_got[pl.ds(pl.multiple_of(at + gate_group, 16), 16), 0:128].astype(F32)
            gate = lane_row(group[gate_line : gate_line + 1] + group[gate_line + 1 : gate_line + 2], block)
            there = span(plane * quad + j, block)
            r.grad_ret[there, :] = (gate * r.cot_got[there, :].astype(F32)).astype(BF)
        for c in range(hidden // tile):
            cols = slice(c * tile, (c + 1) * tile)
            pre = dot(r.x_got[here, :], r.first[:, cols]) + r.bias1[0:1, cols]
            square = pre * pre
            bend = jnp.tanh(pre * (root + 0.044715 * root * square))
            half = 0.5 + 0.5 * bend
            hidden_rows = pre * half
            r.hidden[here, cols] = hidden_rows.astype(BF)
            slope = half + hidden_rows * (1.0 - bend) * (root + 3 * 0.044715 * root * square)
            back = dot_nt(r.grad_ret[here, :], r.second[cols, :])
            r.grad_pre[here, cols] = (back * slope).astype(BF)
        returned = dot(r.hidden[here, :], r.second[...]) + r.tiles[0, 1:2, :]
        r.send_b[here, :] = returned.astype(BF)
        grad_in = dot_nt(r.grad_pre[here, :], r.first[...])
        for j in range(quad):
            e = plane * quad + j
            there = span(e, block)
            product = r.cot_got[there, :].astype(F32) * r.send_b[there, :].astype(F32)
            high, low = split_two(row_of(jnp.sum(product, axis=-1, keepdims=True), 128))
            values = grad_in[j * block : (j + 1) * block]
            r.send_a[there, :] = values.astype(BF)
            group = values[gate_group : gate_group + 16, 0:128]
            group = put_pair(group, gate_line, high.astype(F32), low.astype(F32))
            at = pl.ds(pl.multiple_of(e * block + gate_group, 16), 16)
            r.send_a[at, 0:128] = group.astype(BF)
            grad_swap.send(e)

    each(geo.planes, expert_chunk)
    send_late(geo.planes // 2, geo.planes)
    for swap in (ret_swap, late_ret_swap):
        swap.send_all()

    grads = ExpertGrads(
        geo,
        r.d_experts,
        r.d_got,
        r.d_tiles,
        r.d_got_tiles,
        r.inbox,
        r.inbox_tiles,
        sems("expert_sem"),
    )
    quarter = hidden // 4

    def weight_grads(side):
        for layer, left, right in ((0, r.x_got, r.grad_pre), (1, r.grad_ret, r.hidden)):
            for c in range(2):
                cols = pl.ds(pl.multiple_of(side * (hidden // 2) + c * quarter, 128), quarter)
                r.d_experts[layer, :, cols] = dot_tn(left[...], right[:, cols]).astype(BF)

    weight_grads(1 - k)
    grads.pair(0).start()
    grads.pair(1).start()
    ones = jnp.ones((16, slots), BF)
    r.sum_pre[...] = dot(ones, r.grad_pre[...])[0:8]
    r.sum_ret[...] = dot(ones, r.grad_ret[...])[0:8]
    r.d_tiles[...] = jnp.zeros(r.d_tiles.shape, F32)
    for s in range(geo.places):
        r.d_tiles[s, 0:1, 0:part] = r.sum_pre[0:1, s * part : (s + 1) * part]
        r.d_tiles[s, 1:2, :] = r.sum_ret[0:1, :]
    grads.pair_tiles().start()
    weight_grads(k)
    grads.forward()

    dense = DenseSum(
        geo,
        r.mine,
        r.got_pair,
        r.got_plane,
        r.piece,
        r.got_z,
        r.wide_z,
        r.wide_sum,
        r.wide_plane,
        r.whole,
        r.small,
        r.s_pair,
        r.s_plane,
        r.s_z,
        sems("dense_sem"),
        4 * width // (128 * geo.planes) - (2 if 128 * geo.planes == width else 1),
    )

    def slot_grads(e):
        at = pl.ds(pl.multiple_of(e * head + gate_group, 16), 16)
        group = r.grad_got[at, 0:128].astype(F32)
        column = lane_row(group[gate_line : gate_line + 1] + group[gate_line + 1 : gate_line + 2], block)
        lane = lax.broadcasted_iota(jnp.int32, (block, 128), 1)
        late = pl.ds(pl.multiple_of(heads + e * rest, 16), rest)
        for i, value in enumerate(split_two(jnp.where(lane == e, column, 0.0))):
            cols = slice(i * 128, (i + 1) * 128)
            r.slot_grad[span(e, head), cols] = value[0:head]
            r.slot_grad[late, cols] = value[head:]

    def combine(m):
        here = slice(m * per_micro, (m + 1) * per_micro)
        there = slice(0, heads if m == 0 else slots)
        for c in range(width // tile):
            cols = slice(c * tile, (c + 1) * tile)
            r.grad_two[here, cols] = dot(r.table_t[here, there], r.grad_got[there, cols])
        both = dot(r.table_t[here, there], r.slot_grad[there, :])
        r.grad_choice[here, :] = both[:, 0:128] + both[:, 128:256]

    r.small[...] = jnp.zeros(r.small.shape, F32)

    def add_small(row, value):
        r.small[row : row + 1, :] = r.small[row : row + 1, :] + jnp.sum(value, axis=0, keepdims=True)

    def norm_two_back(i):
        here = span(i, seq)
        probs = r.probs[here, :]
        choice = r.grad_choice[here, :]
        logits = probs * (choice - jnp.sum(probs * choice, axis=-1, keepdims=True))
        high, low = split_two(logits)
        r.logits_high[here, :] = high
        r.logits_low[here, :] = low
        weight = r.w_router[...]
        grad = r.grad_two[here, :]
        grad = grad + dot(high[:, 0:experts], weight) + dot(low[:, 0:experts], weight)
        unit, scale = norm_parts(r.residual[here, :])
        add_small(5, grad * unit)
        add_small(6, grad)
        grad = r.cot[here, :].astype(F32) + norm_back(grad, unit, scale, vector(r.gain2))
        r.grad_two[here, :] = grad
        low_grad = grad.astype(BF)
        r.grad_branch[here, :] = low_grad
        add_small(4, low_grad.astype(F32))

    columns = dense.columns
    chunks = 4 * width // columns
    stages = dense.stages(chunks - 1)

    def dense_grad(first):
        cols = pl.ds(first, tile)
        if first < 3 * width:
            out = dot_tn(r.normed[...], r.grad_qkv[:, cols])
        else:
            out = dot_tn(r.attended[...], r.grad_branch[:, pl.ds(first - 3 * width, tile)])
        r.mine[:, cols] = out.astype(BF)

    early = columns == width

    def attend_grad(m):
        here = slice(m * per_micro, (m + 1) * per_micro)
        for c in range(width // tile):
            cols = slice(c * tile, (c + 1) * tile)
            r.grad_att[here, cols] = dot_nt(r.grad_branch[here, :], r.w_out[cols, :]).astype(BF)

    def attend_back(i):
        here = span(i, seq)
        length = r.lengths[i // (per_micro // seq), i % (per_micro // seq)]
        parts = attend_image_back(
            r.qkv[here, 0:width],
            r.qkv[here, width : 2 * width],
            r.qkv[here, 2 * width : 3 * width],
            length,
            r.grad_att[here, :],
        )
        for c, value in enumerate(parts):
            r.grad_qkv[here, c * width : (c + 1) * width] = value
        add_small(2, parts[0].astype(F32))
        add_small(3, parts[2].astype(F32))

    def norm_one_back(i):
        here = span(i, seq)
        grad = dot_nt(r.grad_qkv[here, :], r.w_qkv[...])
        unit, scale = norm_parts(r.tokens[here, :].astype(F32))
        add_small(0, grad * unit)
        add_small(1, grad)
        r.grad_two[here, :] = r.grad_two[here, :] + norm_back(
            grad, unit, scale, vector(r.gain1)
        )

    def mix(there, i):
        here = span(i, seq)
        total = dot(r.table_t[here, there], r.ret_got[there, :])
        chosen = dot(r.table0_t[here, there], r.ret_got[there, :])
        probs = r.probs[here, :]
        lane = lax.broadcasted_iota(jnp.int32, probs.shape, 1).astype(F32)
        gates = [
            jnp.sum(jnp.where(lane == r.ids_t[here, j : j + 1], probs, 0.0), axis=-1, keepdims=True)
            for j in range(2)
        ]
        mixed = r.residual[here, :] + gates[0] * chosen + gates[1] * (total - chosen)
        r.expert_in[here, :] = mixed.astype(BF)

    def some(step, m):
        count = images * per_micro // rows
        each(count, lambda i: step(m * count + i))

    micros = rows // per_micro
    last = (micros - 1) * images // micros
    grad_swap.wait_all()
    each(experts, slot_grads)
    for m in range(micros):
        if m == 1:
            late_grad_swap.wait_all()
        combine(m)
        some(norm_two_back, m)
        if m == micros - 1 and early:
            for first in range(3 * width, 4 * width, tile):
                dense_grad(first)
            dense.pair(chunks - 1).start()
        attend_grad(m)
        if m == micros - 1 and early:
            attend_back(last)
            stages[0](chunks - 1)
            each(images - last - 1, lambda i: attend_back(last + 1 + i))
        else:
            some(attend_back, m)
        if m < micros - 1:
            some(norm_one_back, m)
    router = dot_tn(r.logits_high[...], r.expert_in[...]) + dot_tn(r.logits_low[...], r.expert_in[...])
    r.small[8 : 8 + experts, :] = router[0:experts, :]
    late = chunks - 1 if early else chunks
    done = 1 if early else 0
    tokens_copy = pltpu.make_async_copy(r.grad_two, r.grad_tokens, r.out_sem.at[1])
    mixed_copy = pltpu.make_async_copy(r.expert_in, r.mixed, r.out_sem.at[0])
    layers_copy = pltpu.make_async_copy(r.inbox, r.d_layers, r.out_sem.at[2])
    bias_copy = pltpu.make_async_copy(r.inbox_tiles, r.d_bias, r.out_sem.at[3])

    def tokens_done():
        tokens_copy.start()
        dense.small_pair().start()

    def owner_done():
        grads.wait_got()
        layers_copy.start()
        bias_copy.start()

    def early_mix():
        ret_swap.wait_all()
        each(last, functools.partial(mix, slice(0, heads)))

    def late_mix():
        late_ret_swap.wait_all()
        each(images - last, lambda i: mix(slice(0, slots), last + i))
        mixed_copy.start()

    beside = [[] for _ in stages]
    beside[0] = [lambda: some(norm_one_back, micros - 1), tokens_done]
    beside[1] = [dense.small_plane]
    beside[2] = [dense.small_z, early_mix]
    beside[3] = [owner_done]
    small_copy = pltpu.make_async_copy(r.small, r.small_out, r.out_sem.at[5])

    def small_done():
        dense.small_finish(r.small)
        small_copy.start()

    beside[4] = [small_done, late_mix]
    for c in range(late):
        for first in range(c * columns, (c + 1) * columns, tile):
            dense_grad(first)
        dense.pair(c).start()
    for stage in range(len(stages)):
        for c in range(late):
            dense.stages(c)[stage](c)
        if early and done + stage < len(stages):
            stages[done + stage](chunks - 1)
        for step in beside[stage]:
            step()
    big_copy = pltpu.make_async_copy(r.whole, r.big_out, r.out_sem.at[4])
    big_copy.start()
    for swap in (grad_swap, late_grad_swap, ret_swap, late_ret_swap):
        swap.wait_sent()
    weights.wait_sent()
    grads.wait_sent()
    dense.wait_sent(chunks)
    for copy in (mixed_copy, tokens_copy, layers_copy, bias_copy, small_copy, big_copy):
        copy.wait()


def finish_kernel(names, *refs):
    r = SimpleNamespace(**dict(zip(names, refs, strict=True)))
    width, part = r.w_out.shape[0], r.w1.shape[2]
    local, group = r.g_d_layers.shape[1:3]
    sems = iter(range(len(names)))

    def move(src, dst):
        copy = pltpu.make_async_copy(src, dst, r.sem.at[next(sems)])
        copy.start()
        return copy

    come_layers = [
        [move(r.g_d_layers.at[layer, i], r.v_layers.at[layer, i]) for layer in range(2)] for i in range(local)
    ]
    come_big = [
        move(r.g_big_out.at[:, c * width : (c + 1) * width], r.v_big.at[:, c * width : (c + 1) * width])
        for c in range(4)
    ]
    come_small, come_bias = move(r.g_small_out, r.v_small), move(r.g_d_bias, r.v_bias)
    come_tokens, come_mixed = move(r.g_grad_tokens, r.v_tokens), move(r.g_mixed, r.v_mixed)
    copies = []
    for i in range(local):
        for layer in range(2):
            come_layers[i][layer].wait()
            total = r.v_layers[layer, i, 0].astype(F32)
            for g in range(1, group):
                total = total + r.v_layers[layer, i, g].astype(F32)
            if layer == 0:
                r.o_first[i] = total
                copies.append(move(r.o_first.at[i], r.w1.at[i]))
            else:
                r.o_second[i] = jnp.transpose(total)
                copies.append(move(r.o_second.at[i], r.w2.at[i]))
    for c in range(4):
        come_big[c].wait()
        cols = slice(c * width, (c + 1) * width)
        r.o_big[:, cols] = r.v_big[:, cols].astype(F32)
        copies.append(move(r.o_big.at[:, cols], r.w_qkv.at[:, cols] if c < 3 else r.w_out))
    come_small.wait()
    lines = ("gain1", "shift1", "bias_q", "bias_v", "bias_out", "gain2", "shift2")
    for line, name in enumerate(lines):
        row = getattr(r, "v_" + name)
        row[...] = r.v_small[line]
        copies.append(move(row, getattr(r, name)))
    copies.append(move(r.v_small.at[8:], r.router))
    come_bias.wait()
    tiles = r.v_bias[:, 0]
    for g in range(1, group):
        tiles = tiles + r.v_bias[:, g]
    r.v_b1[...] = tiles[:, 0, 0:part]
    r.v_b2[...] = tiles[:, 1, :]
    copies += [move(r.v_b1, r.b1), move(r.v_b2, r.b2)]
    come_tokens.wait()
    copies.append(move(r.v_tokens, r.grad_tokens))
    come_mixed.wait()
    copies.append(move(r.v_mixed, r.mixed))
    for copy in copies:
        copy.wait()


def on_device(
    geo,
    tokens,
    image_lengths,
    expert_index,
    grad_out,
    ln1_gain,
    ln1_bias,
    w_qkv,
    bias_query,
    bias_value,
    w_out,
    bias_out,
    ln2_gain,
    ln2_bias,
    w_router,
    experts_in,
    experts_in_bias,
    experts_out,
    experts_out_bias,
):
    micros, per_micro, width = tokens.shape
    rows = micros * per_micro
    seq = per_micro // image_lengths.shape[1]
    experts = geo.partners
    capacity = (per_micro * 42 + 20 * experts - 1) // (20 * experts)
    block = -(-(micros * capacity + 2) // 16) * 16
    slots = experts * block
    part = experts_in.shape[2]
    hidden = part * geo.places
    places, planes, local, group = geo.places, geo.planes, geo.local_experts, geo.group
    inputs = dict(
        given_choices=jnp.swapaxes(expert_index, 1, 2),
        given_cot=grad_out.reshape(rows, width),
        given_tokens=tokens.reshape(rows, width),
        lengths=image_lengths,
        given_gain1=ln1_gain,
        given_shift1=ln1_bias,
        given_w_qkv=w_qkv,
        given_bias_q=bias_query,
        given_bias_v=bias_value,
        given_w_out=w_out,
        given_bias_out=bias_out,
        given_gain2=ln2_gain,
        given_shift2=ln2_bias,
        given_w_router=w_router.T,
        w1=experts_in,
        given_b1=experts_in_bias,
        w2=experts_out,
        given_b2=experts_out_bias,
    )
    vmem, smem = pl.BlockSpec(memory_space=pltpu.VMEM), pl.BlockSpec(memory_space=pltpu.SMEM)
    anywhere = pl.BlockSpec(memory_space=pl.ANY)
    in_specs = {name: vmem for name in inputs}
    in_specs.update(lengths=smem, w1=anywhere, w2=anywhere)
    in_specs.update({name: anywhere for name in inputs if name.startswith("given")})
    small_rows = 8 + experts
    outputs = dict(
        mixed=((rows, width), BF, anywhere),
        grad_tokens=((rows, width), F32, anywhere),
        big_out=((width, 4 * width), BF, anywhere),
        small_out=((small_rows, width), F32, anywhere),
        d_layers=((2, local, group, width, part), BF, anywhere),
        d_bias=((local, group, 8, width), F32, anywhere),
    )
    half = width // 2
    columns = DenseSum.chunk_columns(geo)
    chunks = 4 * width // columns
    scratch = {name[6:]: (a.shape, a.dtype) for name, a in inputs.items() if name.startswith("given")}
    scratch.update(
        tile=((local, 8, width), F32),
        tiles=((places, 8, width), F32),
        first=((width, hidden), BF),
        second=((hidden, width), BF),
        bias1=((8, hidden), F32),
        ids=((8, -(-rows // 128) * 128), F32),
        ids_t=((-(-rows // 128) * 128, 8), F32),
        held=((2, experts, -(-rows // 128) * 128), F32),
        table=((slots + 128, rows), BF),
        table_t=((rows, slots), BF),
        table0_t=((rows, slots), BF),
        send_a=((slots, width), BF),
        send_b=((slots, width), BF),
        cot_got=((slots, width), BF),
        x_got=((slots, width), BF),
        grad_got=((slots, width), BF),
        ret_got=((slots, width), BF),
        normed=((rows, width), BF),
        qkv=((rows, 3 * width), BF),
        attended=((rows, width), BF),
        residual=((rows, width), F32),
        expert_in=((rows, width), BF),
        probs=((rows, 128), F32),
        probs_t=((2 * experts, rows), BF),
        grad_ret=((slots, width), BF),
        hidden=((slots, hidden), BF),
        grad_pre=((slots, hidden), BF),
        sum_pre=((8, hidden), F32),
        sum_ret=((8, width), F32),
        d_experts=((2, width, hidden), BF),
        d_got=((2, width, hidden // 2), BF),
        d_tiles=((places, 8, width), F32),
        d_got_tiles=((places, 8, width), F32),
        inbox=((2, local, group, width, part), BF),
        inbox_tiles=((local, group, 8, width), F32),
        grad_two=((rows, width), F32),
        grad_choice=((rows, 128), F32),
        got_pair=((chunks, half, columns), BF),
        got_plane=((chunks, places, half // places, columns), BF),
        piece=((chunks, planes, half // places, 128), BF),
        got_z=((chunks, planes, half // places, 128), BF),
        wide_z=((planes, half, 128), BF),
        wide_sum=((half, 128), BF),
        wide_plane=((places, half // places, 128), BF),
        whole=((width, 4 * width), BF),
        small=((small_rows, width), F32),
        s_pair=((small_rows, width), F32),
        s_plane=((places, small_rows, width), F32),
        s_z=((planes, small_rows, width), F32),
    )
    sem_sets = dict(
        weights_sem=Weights.sems(geo),
        cot_sem=swap_sems(planes),
        x_sem=swap_sems(planes),
        head_grad_sem=swap_sems(1),
        rest_grad_sem=swap_sems(1),
        head_ret_sem=swap_sems(1),
        rest_ret_sem=swap_sems(1),
        expert_sem=ExpertGrads.sems(geo),
        dense_sem=DenseSum.semaphores(geo, chunks)[1],
    )
    sem_names = [name + str(i) for name, found in sem_sets.items() for i in range(len(found))]
    sem_shapes = [s for found in sem_sets.values() for s in found]
    names = [*inputs, *outputs, *scratch, *sem_names, "out_sem", "in_sem"]
    sizes = (rows, per_micro, seq, capacity, block, width, hidden)
    results = pl.pallas_call(
        functools.partial(block_kernel, geo, sizes, names),
        out_shape=[jax.ShapeDtypeStruct(shape, dtype) for shape, dtype, _ in outputs.values()],
        in_specs=list(in_specs.values()),
        out_specs=[spec for _, _, spec in outputs.values()],
        scratch_shapes=[pltpu.VMEM(shape, dtype) for shape, dtype in scratch.values()]
        + sem_shapes
        + [pltpu.SemaphoreType.DMA((6,)), pltpu.SemaphoreType.DMA((len(inputs),))],
        compiler_params=pltpu.CompilerParams(
            collective_id=0, has_side_effects=True, vmem_limit_bytes=VMEM_LIMIT
        ),
    )(*inputs.values())
    out = dict(zip(outputs, results, strict=True))
    shapes = dict(
        mixed=((rows, width), BF),
        grad_tokens=((rows, width), F32),
        gain1=((width,), F32),
        shift1=((width,), F32),
        w_qkv=((width, 3 * width), F32),
        bias_q=((width,), F32),
        bias_v=((width,), F32),
        w_out=((width, width), F32),
        bias_out=((width,), F32),
        gain2=((width,), F32),
        shift2=((width,), F32),
        router=((experts, width), F32),
        w1=((local, width, part), F32),
        b1=((local, part), F32),
        w2=((local, part, width), F32),
        b2=((local, width), F32),
    )
    room = dict(
        v_big=((width, 4 * width), BF),
        v_layers=((2, local, group, width, part), BF),
        v_tokens=((rows, width), F32),
        v_mixed=((rows, width), BF),
        v_small=((small_rows, width), F32),
        v_bias=((local, group, 8, width), F32),
        o_big=((width, 4 * width), F32),
        o_first=((local, width, part), F32),
        o_second=((local, part, width), F32),
    )
    room.update({"v_" + name: spec for name, spec in shapes.items() if len(spec[0]) == 1 or name in ("b1", "b2")})
    given = ["g_" + name for name in outputs]
    made = pl.pallas_call(
        functools.partial(finish_kernel, [*given, *shapes, *room, "sem"]),
        out_shape=[jax.ShapeDtypeStruct(shape, dtype) for shape, dtype in shapes.values()],
        in_specs=[anywhere] * len(outputs),
        out_specs=[anywhere] * len(shapes),
        scratch_shapes=[pltpu.VMEM(shape, dtype) for shape, dtype in room.values()]
        + [pltpu.SemaphoreType.DMA((24 + 4 * local,))],
        compiler_params=pltpu.CompilerParams(vmem_limit_bytes=VMEM_LIMIT),
    )(*results)
    made = dict(zip(shapes, made, strict=True))
    made.update(
        mixed=made["mixed"].reshape(tokens.shape),
        grad_tokens=made["grad_tokens"].reshape(tokens.shape),
        router=made["router"].T,
    )
    return tuple(made.values())


def solution(mesh):
    split = ("wide", "narrow")
    in_specs = (
        P(None, split, None),
        P(None, split),
        P(None, split, None),
        P(None, split, None),
        *([P()] * 10),
        P("wide", None, "narrow"),
        P("wide", "narrow"),
        P("wide", "narrow", None),
        P("wide", None),
    )
    out_specs = (
        P(None, split, None),
        P(None, split, None),
        *([P()] * 10),
        P("wide", None, "narrow"),
        P("wide", "narrow"),
        P("wide", "narrow", None),
        P("wide", None),
    )

    def step(*args):
        geo = Geometry(mesh.shape["wide"], mesh.shape["narrow"], args[14].shape[0])
        return on_device(geo, *args)

    return jax.shard_map(step, mesh=mesh, in_specs=in_specs, out_specs=out_specs, check_vma=False)
```
